256 devices in a mesh: lon: 32 (over z, y), lat: 8 (over x, core).
Axes of the slice: x: 4, y: 4, z: 8, core: 2. Of those that a mesh axis runs over, the one named last changes fastest.
Arguments:
- cotangent: float32 [8, 512, 4096], P(None, 'lat', 'lon'), may hold values from -6 to 6
- diff_east: float32 [512, 4096], P('lat', 'lon'), may hold values from 0.02 to 0.2
- diff_north: float32 [512, 4096], P('lat', 'lon'), may hold values from 0.02 to 0.2
- flow_east: float32 [512, 4096], P('lat', 'lon'), may hold values from -0.2 to 0.2
- flow_north: float32 [512, 4096], P('lat', 'lon'), may hold values from -0.2 to 0.2
- sea_mask: int32 [512, 4096], P('lat', 'lon'), may hold values 0 or 1
- cutoff: int32 [512], P('lat'), may hold values from 16 to 2048, as said below
Outputs:
- adjoint_field: float32 [8, 512, 4096], P(None, 'lat', 'lon')
The draws below stay inside these ranges and needn't reach their ends.
Inputs may be any that keep to these rules, and one draw needn't show every extreme that they name: cutoff equals 2048 on every row except the first 64 and the last 64 rows.
All inputs are finite; a program needn't handle non-finite values. No bound on the sum of `sea_mask` on one device may be relied on, other than what follows from the above.
Results may differ from the reference program's by a relative error of at most 0.00012.
Values sent between devices are 32-bit elements; how exact they have to be, the bound alone decides.
A program may use at most 64 MiB of HBM per device.

```python
import math
import jax
import jax.numpy as jnp

NLON = 4096
LEV = 8
LAT_DEV = 64
STEPS = 4
NLAT = 512


def draw_cutoff(key, part):
    key = jax.random.fold_in(key, 7)
    latitude = jnp.arange(NLAT, dtype=jnp.int32)
    polar_band = (latitude < LAT_DEV) | (latitude >= NLAT - LAT_DEV)
    random_cuts = jax.random.randint(key, (NLAT,), 16, NLON // 2 + 1)
    return jnp.where(polar_band, random_cuts, NLON // 2).astype(jnp.int32)


def touch_ends(values, stream_key, low, top_value):
    longest = values.shape.index(max(values.shape))
    spots = []
    for shift in (0, 1):
        where = [jax.random.randint(jax.random.fold_in(stream_key, axis), (), 0, length) for axis, length in enumerate(values.shape)]
        where[longest] = (where[longest] + shift) % values.shape[longest]
        spots.append(tuple(where))
    return values.at[spots[0]].set(low).at[spots[1]].set(top_value)


def level_of(stream_key, extent, pieces, least, top_value):
    level = 1.0
    for position, blocks in pieces:
        heights = jax.random.uniform(jax.random.fold_in(jax.random.fold_in(stream_key, 6), position), (blocks,), jnp.float32, least / len(pieces), top_value / len(pieces))
        level = level * jnp.repeat(jnp.exp(heights), extent[position] // blocks).reshape((-1,) + (1,) * (len(extent) - 1 - position))
    return level


def centred(stream_key, dims, scale, limit, shards=(), kind=jnp.bfloat16):
    result = jax.random.normal(stream_key, dims, jnp.float32) * scale
    if len(shards) > 0:
        result = level_of(stream_key, dims, shards, -0.22, 0.18) * result
    return jnp.clip(result, min=-limit, max=limit).astype(kind)


def setup_inputs(seed: int = 0) -> dict:
    key_list = jax.random.split(jax.random.key(seed), 8)
    cotangent = centred(key_list[0], (LEV, NLAT, NLON), 1.0, 6.0, ((1, 8), (2, 32)), jnp.float32)
    diff_east = jnp.clip(jnp.exp(math.log(0.2) - 2.3025851 * jax.random.uniform(key_list[1], (NLAT, NLON), jnp.float32) ** level_of(key_list[1], (NLAT, NLON), ((0, 8), (1, 32)), -0.2, 0.2)), 0.02, 0.2)
    diff_north = jnp.clip(jnp.exp(math.log(0.2) - 2.3025851 * jax.random.uniform(key_list[2], (NLAT, NLON), jnp.float32) ** level_of(key_list[2], (NLAT, NLON), ((0, 8), (1, 32)), -0.2, 0.2)), 0.02, 0.2)
    flow_east = jnp.clip(jax.random.uniform(key_list[3], (NLAT, NLON), jnp.float32, -0.2, 0.2) * level_of(key_list[3], (NLAT, NLON), ((0, 8), (1, 32)), -0.4, 0.0), -0.2, 0.2)
    flow_north = jnp.clip(jax.random.uniform(key_list[4], (NLAT, NLON), jnp.float32, -0.2, 0.2) * level_of(key_list[4], (NLAT, NLON), ((0, 8), (1, 32)), -0.4, 0.0), -0.2, 0.2)
    sea_mask = touch_ends((jax.random.randint(key_list[5], (NLAT, NLON), 0, 5) < 4).astype(jnp.int32), jax.random.fold_in(key_list[5], 1), 0, 1)
    cutoff = draw_cutoff(jax.random.fold_in(key_list[7], 71), 0)
    return dict(cotangent=cotangent, diff_east=diff_east, diff_north=diff_north, flow_east=flow_east, flow_north=flow_north, sea_mask=sea_mask, cutoff=cutoff)


def transport(tracer, diff_east, diff_north, flow_east, flow_north, sea):
    east_open = sea * jnp.roll(sea, -1, axis=1)
    east_minus = east_open * (-diff_east - 0.5 * flow_east)
    east_plus = east_open * (diff_east - 0.5 * flow_east)
    east_flux = east_minus * tracer + east_plus * jnp.roll(tracer, -1, axis=2)
    north_open = sea[:-1] * sea[1:]
    north_minus = north_open * (-diff_north[:-1] - 0.5 * flow_north[:-1])
    north_plus = north_open * (diff_north[:-1] - 0.5 * flow_north[:-1])
    north_flux = north_minus * tracer[:, :-1] + north_plus * tracer[:, 1:]
    north_flux = jnp.pad(north_flux, ((0, 0), (1, 1), (0, 0)))
    divergence = east_flux - jnp.roll(east_flux, 1, axis=2) + north_flux[:, 1:] - north_flux[:, :-1]
    return tracer + sea * divergence

def zonal_filter(tracer, cutoff):
    spectrum = jnp.fft.rfft(tracer, axis=2)
    wavenumber = jnp.arange(NLON // 2 + 1, dtype=jnp.int32)
    kept_mask = wavenumber[None, :] <= cutoff[:, None]
    return jnp.fft.irfft(spectrum * kept_mask[None], n=NLON, axis=2)

def reference(cotangent, diff_east, diff_north, flow_east, flow_north, sea_mask, cutoff):
    sea = sea_mask.astype(jnp.float32)

    def forward(tracer):
        for section in range(STEPS):
            tracer = zonal_filter(transport(tracer, diff_east, diff_north, flow_east, flow_north, sea), cutoff)
        return tracer
    start = jnp.zeros(cotangent.shape, jnp.float32)
    result_value, pullback = jax.vjp(forward, start)
    return pullback(cotangent)[0]
```

```python
import functools
import math

import jax
import jax.numpy as jnp
import numpy as np
from jax import lax
from jax.experimental import pallas as pl
from jax.experimental.pallas import tpu as pltpu
from jax.sharding import PartitionSpec as P

STEPS = 4
LEVELS = 8
ROWS = 64
LANES = 128
TILES = 32
NLON = TILES * LANES
BLOCKS = 8
PAIRS = 4
HALO = 8
EXT = ROWS + 2 * HALO
PLANES = LEVELS + 5
MASK = LEVELS + 4
EDGE = 4
LATS = 8

F32 = jnp.float32


def tables():
    n = np.arange(LANES)
    angle = 2 * np.pi * (np.outer(n, n) % LANES) / LANES
    cos, sin = np.cos(angle), np.sin(angle)
    wide = np.block([[cos, -sin], [sin, cos]])
    high = wide.astype(jnp.bfloat16)
    low = (wide - high.astype(np.float64)).astype(jnp.bfloat16)
    q = np.arange(8)[:, None, None]
    c = np.arange(4)[None, :, None]
    first = 2 * np.pi * ((q * (n[None, None, :] + LANES * c)) % NLON) / NLON
    r = np.arange(4)[:, None]
    second = 2 * np.pi * ((r * n[None, :]) % 512) / 512

    def spread(values):
        values = values.reshape(-1, 1, LANES)
        return np.broadcast_to(values, (values.shape[0], 8, LANES)).astype(np.float32)

    turn = np.concatenate(
        [spread(np.cos(first)), spread(np.sin(first)), spread(np.cos(second)), spread(np.sin(second))]
    )
    return high, low, turn


def cadd(x, y):
    return x[0] + y[0], x[1] + y[1]


def csub(x, y):
    return x[0] - y[0], x[1] - y[1]


def quarter(x, sign):
    if sign < 0:
        return x[1], -x[0]
    return -x[1], x[0]


def dft4(x, sign):
    even, odd = cadd(x[0], x[2]), csub(x[0], x[2])
    even2, odd2 = cadd(x[1], x[3]), quarter(csub(x[1], x[3]), sign)
    return [cadd(even, even2), cadd(odd, odd2), csub(even, even2), csub(odd, odd2)]


def dft8(x, sign):
    even = dft4([x[0], x[2], x[4], x[6]], sign)
    odd = dft4([x[1], x[3], x[5], x[7]], sign)
    half = math.sqrt(0.5)

    def eighth(v):
        rot = quarter(v, sign)
        return (v[0] + rot[0]) * half, (v[1] + rot[1]) * half

    odd[1] = eighth(odd[1])
    odd[2] = quarter(odd[2], sign)
    odd[3] = quarter(eighth(odd[3]), sign)
    return [cadd(e, o) for e, o in zip(even, odd)] + [csub(e, o) for e, o in zip(even, odd)]


def cmul(x, cos, sin, sign):
    if sign < 0:
        return x[0] * cos + x[1] * sin, x[1] * cos - x[0] * sin
    return x[0] * cos - x[1] * sin, x[1] * cos + x[0] * sin


def split_dot(left, high_ref, low_ref):
    high = left.astype(jnp.bfloat16)
    low = (left - high.astype(F32)).astype(jnp.bfloat16)
    dot = functools.partial(jnp.dot, preferred_element_type=F32)
    return dot(high, high_ref[...]) + (dot(low, high_ref[...]) + dot(high, low_ref[...]))


def filter_circles(real, imag, cuts, high_ref, low_ref, turn_ref):
    shape = (8, 4, 8, LANES)
    cos1 = turn_ref[0:32].reshape(shape)
    sin1 = turn_ref[32:64].reshape(shape)
    real, imag = real.reshape(shape), imag.reshape(shape)
    parts = dft8([(real[a], imag[a]) for a in range(8)], -1)
    parts = [cmul(parts[q], cos1[q], sin1[q], -1) for q in range(8)]
    real = jnp.stack([p[0] for p in parts])
    imag = jnp.stack([p[1] for p in parts])
    parts = dft4([(real[:, c], imag[:, c]) for c in range(4)], -1)
    parts = [parts[0]] + [
        cmul(parts[r], turn_ref[64 + r], turn_ref[68 + r], -1) for r in range(1, 4)
    ]
    real = jnp.concatenate([p[0] for p in parts]).reshape(256, LANES)
    imag = jnp.concatenate([p[1] for p in parts]).reshape(256, LANES)
    spec = split_dot(jnp.concatenate([real, imag], axis=1), high_ref, low_ref)
    wave = lax.broadcasted_iota(jnp.int32, (TILES, 8, LANES), 0) + TILES * lax.broadcasted_iota(
        jnp.int32, (TILES, 8, LANES), 2
    )
    wave = jnp.minimum(wave, NLON - wave)
    kept = jnp.where(wave <= cuts[None], 1.0 / NLON, 0.0).astype(F32).reshape(256, LANES)
    real = spec[:, :LANES] * kept
    imag = spec[:, LANES:] * kept
    back = split_dot(jnp.concatenate([imag, real], axis=1), high_ref, low_ref)
    real = back[:, LANES:].reshape(4, 8, 8, LANES)
    imag = back[:, :LANES].reshape(4, 8, 8, LANES)
    parts = [(real[0], imag[0])] + [
        cmul((real[r], imag[r]), turn_ref[64 + r], turn_ref[68 + r], 1) for r in range(1, 4)
    ]
    parts = dft4(parts, 1)
    real = jnp.stack([p[0] for p in parts], axis=1)
    imag = jnp.stack([p[1] for p in parts], axis=1)
    parts = [cmul((real[q], imag[q]), cos1[q], sin1[q], 1) for q in range(8)]
    parts = dft8(parts, 1)
    real = jnp.concatenate([p[0] for p in parts])
    imag = jnp.concatenate([p[1] for p in parts])
    return real, imag


def iota(shape, dim):
    return lax.broadcasted_iota(jnp.int32, shape, dim)


def circle_step(x, coef, north, south):
    shape = (TILES * 2, 8, LANES)
    lane = iota(shape, 2)
    row = iota(shape, 1)
    east = pltpu.roll(x, LANES - 1, 2)
    east = jnp.where(lane == LANES - 1, jnp.concatenate([east[2:], east[:2]]), east)
    west = pltpu.roll(x, 1, 2)
    west = jnp.where(lane == 0, jnp.concatenate([west[-2:], west[:-2]]), west)
    up = jnp.where(row == 7, north, pltpu.roll(x, 7, 1))
    down = jnp.where(row == 0, south, pltpu.roll(x, 1, 1))
    full = (TILES, 2, 8, LANES)
    x4 = x.reshape(full)
    total = x4
    for k, near in enumerate((east, west, up, down)):
        total = total + coef[:, k : k + 1] * (x4 - near.reshape(full))
    return total.reshape(shape)


def kernel(
    cot, diff_east, diff_north, flow_east, flow_north, sea, cutoff, high_ref, low_ref, turn_ref,
    out,
    ext, lam, fil, coef, coef_src, lam_x, coef_x, coef_x_src, row_x, rim_e, rim_w, rim_src,
    packed, packed_l, packed_r, wide_coef, edge_out, edge_in,
    row_send, row_recv, col_send, col_recv, in_send, in_recv, cf_send, cf_recv,
    lx_send, lx_recv, cx_send, cx_recv, step_send, step_recv, out_send, out_recv, ox_send, ox_recv,
):
    lon = lax.axis_index("lon")
    lat = lax.axis_index("lat")
    block = lon // PAIRS
    pair = lax.rem(lon, PAIRS)
    polar = jnp.logical_or(lat == 0, lat == LATS - 1)
    beside = jnp.logical_or(lat == 1, lat == LATS - 2)
    edge_block = jnp.where(lat < LATS // 2, BLOCKS - 1, 0)
    has_extra = jnp.logical_and(polar, block == edge_block)
    polar_lat = jnp.where(lat < LATS // 2, 0, LATS - 1)
    beside_lat = jnp.where(lat < LATS // 2, 1, LATS - 2)

    barrier = pltpu.get_barrier_semaphore()

    def at(to_lat, to_lon):
        return {"lon": to_lon, "lat": to_lat}

    def hail(to_lat, to_lon):
        pl.semaphore_signal(
            barrier, inc=1, device_id=at(to_lat, to_lon), device_id_type=pl.DeviceIdType.MESH
        )

    def remote(src, dst, send, recv, to_lat, to_lon):
        return pltpu.make_async_remote_copy(
            src_ref=src, dst_ref=dst, send_sem=send, recv_sem=recv,
            device_id=at(to_lat, to_lon), device_id_type=pl.DeviceIdType.MESH,
        )

    def wait_bytes(ref, sem):
        pltpu.make_async_copy(ref, ref, sem).wait()

    right = lax.rem(lon + 1, TILES)
    left = lax.rem(lon + TILES - 1, TILES)

    @pl.when(lat > 0)
    def _():
        hail(lat - 1, lon)

    @pl.when(lat < LATS - 1)
    def _():
        hail(lat + 1, lon)

    @pl.when(polar)
    def _():
        def greet(s, carry):
            hail(lat, lax.rem(lon + s, TILES))
            return carry

        lax.fori_loop(1, TILES, greet, 0)

    @pl.when(jnp.logical_not(polar))
    def _():
        hail(lat, left)
        hail(lat, right)

    @pl.when(beside)
    def _():
        for p in range(PAIRS):
            hail(polar_lat, edge_block * PAIRS + p)

    @pl.when(has_extra)
    def _():
        def greet(d, carry):
            hail(beside_lat, d)
            return carry

        lax.fori_loop(0, TILES, greet, 0)

    main = pl.ds(HALO, ROWS)
    ext[0:LEVELS, HALO : HALO + ROWS] = cot[...]
    ext[LEVELS, HALO : HALO + ROWS] = diff_east[...]
    ext[LEVELS + 1, HALO : HALO + ROWS] = flow_east[...]
    ext[LEVELS + 2, HALO : HALO + ROWS] = diff_north[...]
    ext[LEVELS + 3, HALO : HALO + ROWS] = flow_north[...]
    mask = sea[...].astype(F32)
    ext[MASK, HALO : HALO + ROWS] = mask

    @pl.when(lat == 0)
    def _():
        ext[:, 0:HALO] = jnp.zeros((PLANES, HALO, LANES), F32)

    @pl.when(lat == LATS - 1)
    def _():
        ext[:, HALO + ROWS : EXT] = jnp.zeros((PLANES, HALO, LANES), F32)

    @pl.when(polar)
    def _():
        rim_src[...] = mask * (diff_east[...] - 0.5 * flow_east[...])
        edge_in[...] = jnp.zeros(edge_in.shape, F32)
        lam[lon] = cot[pl.ds(2 * pair, 2), pl.ds(pl.multiple_of(8 * block, 8), 8), :]

    peers = jnp.where(polar, TILES, 4)
    peers = peers + jnp.where(has_extra, TILES, 0) + jnp.where(beside, PAIRS, 0)
    pl.semaphore_wait(barrier, peers)

    low_rows = ext.at[:, pl.ds(HALO, HALO)]
    high_rows = ext.at[:, pl.ds(ROWS, HALO)]
    south_rows = ext.at[:, pl.ds(0, HALO)]
    north_rows = ext.at[:, pl.ds(HALO + ROWS, HALO)]
    to_south = remote(low_rows, north_rows, row_send.at[0], row_recv.at[0], lat - 1, lon)
    to_north = remote(high_rows, south_rows, row_send.at[1], row_recv.at[1], lat + 1, lon)

    @pl.when(lat > 0)
    def _():
        to_south.start()

    @pl.when(lat < LATS - 1)
    def _():
        to_north.start()

    def wait_rows():
        @pl.when(lat < LATS - 1)
        def _():
            to_south.wait_recv()

        @pl.when(lat > 0)
        def _():
            to_north.wait_recv()

    @pl.when(polar)
    def _():
        to_left = remote(ext.at[MASK, main], rim_e, col_send.at[0], col_recv.at[0], lat, left)
        to_right = remote(rim_src, rim_w, col_send.at[1], col_recv.at[1], lat, right)
        to_left.start()
        to_right.start()

        def send_in(s, carry):
            owner = lax.rem(lon + s, TILES)
            rows = pl.ds(pl.multiple_of(8 * (owner // PAIRS), 8), 8)
            remote(
                cot.at[pl.ds(2 * lax.rem(owner, PAIRS), 2), rows], lam.at[lon],
                in_send.at[0], in_recv.at[0], lat, owner,
            ).start()
            return carry

        lax.fori_loop(1, TILES, send_in, 0)

        wait_rows()
        to_left.wait_recv()
        to_right.wait_recv()
        lane = iota((ROWS, LANES), 1)
        mine = ext[MASK, HALO : HALO + ROWS]
        mask_east = jnp.where(
            lane == LANES - 1, pltpu.roll(rim_e[...], LANES - 1, 1), pltpu.roll(mine, LANES - 1, 1)
        )
        plus_west = jnp.where(
            lane == 0, pltpu.roll(rim_w[...], 1, 1), pltpu.roll(rim_src[...], 1, 1)
        )
        mask_north = ext[MASK, HALO + 1 : HALO + ROWS + 1]
        tail = slice(HALO - 1, HALO + ROWS - 1)
        plus_south = ext[MASK, tail] * (ext[LEVELS + 2, tail] - 0.5 * ext[LEVELS + 3, tail])
        shape = (BLOCKS, 8, LANES)
        coef_src[:, 0] = (
            mine * mask_east * (-diff_east[...] - 0.5 * flow_east[...])
        ).reshape(shape)
        coef_src[:, 1] = (-mine * plus_west).reshape(shape)
        coef_src[:, 2] = (
            mine * mask_north * (-diff_north[...] - 0.5 * flow_north[...])
        ).reshape(shape)
        coef_src[:, 3] = (-mine * plus_south).reshape(shape)

        def send_coef(s, carry):
            owner = lax.rem(lon + s, TILES)
            remote(
                coef_src.at[owner // PAIRS], coef.at[lon], cf_send.at[0], cf_recv.at[0], lat, owner
            ).start()
            return carry

        lax.fori_loop(1, TILES, send_coef, 0)
        coef[lon] = coef_src[block]

        row = iota((8, LANES), 0)
        cuts = jnp.zeros((8, LANES), jnp.int32)
        for j in range(8):
            cuts = jnp.where(row == j, cutoff[8 * block + j], cuts)

        wait_bytes(lam.at[pl.ds(0, TILES - 1)], in_recv.at[0])

        def step(s, carry):
            real, imag = filter_circles(
                lam[:, 0], lam[:, 1], cuts, high_ref, low_ref, turn_ref
            )
            fil[:, 0] = real
            fil[:, 1] = imag
            x = fil[...].reshape(2 * TILES, 8, LANES)
            edge_out[s, 0] = x[:, 0:1]
            edge_out[s, 1] = x[:, 7:8]
            go_south = remote(
                edge_out.at[s, 0], edge_in.at[s, 0], step_send.at[s, 0], step_recv.at[s, 0],
                lat, lon - PAIRS,
            )
            go_north = remote(
                edge_out.at[s, 1], edge_in.at[s, 1], step_send.at[s, 1], step_recv.at[s, 1],
                lat, lon + PAIRS,
            )

            @pl.when(block > 0)
            def _():
                go_south.start()

            @pl.when(block < BLOCKS - 1)
            def _():
                go_north.start()

            @pl.when(s == 0)
            def _():
                wait_bytes(coef.at[pl.ds(0, TILES - 1)], cf_recv.at[0])

            @pl.when(jnp.logical_and(has_extra, s == 0))
            def _():
                wait_bytes(lam_x, lx_recv.at[0])
                wait_bytes(coef_x, cx_recv.at[0])

            @pl.when(has_extra)
            def _():
                beyond = lam_x[...].reshape(2 * TILES, 8, LANES)

                @pl.when(lat == 0)
                def _():
                    edge_in[s, 0] = beyond[:, 0:1]

                @pl.when(lat > 0)
                def _():
                    edge_in[s, 1] = beyond[:, 7:8]

                lam_x[...] = circle_step(
                    beyond, coef_x[...], edge_out[s, 0], edge_out[s, 1]
                ).reshape(lam_x.shape)

            @pl.when(block < BLOCKS - 1)
            def _():
                go_south.wait_recv()

            @pl.when(block > 0)
            def _():
                go_north.wait_recv()

            lam[...] = circle_step(x, coef[...], edge_in[s, 0], edge_in[s, 1]).reshape(lam.shape)
            return carry

        lax.fori_loop(0, STEPS, step, 0)

        mine_out = (pl.ds(2 * pair, 2), pl.ds(pl.multiple_of(8 * block, 8), 8))

        def send_out(s, carry):
            tile = lax.rem(lon + s, TILES)
            remote(
                lam.at[tile], out.at[mine_out], out_send.at[0], out_recv.at[0], lat, tile
            ).start()
            return carry

        lax.fori_loop(1, TILES, send_out, 0)

        @pl.when(has_extra)
        def _():
            def send_x(s, carry):
                tile = lax.rem(lon + s, TILES)
                remote(
                    lam_x.at[tile], row_x.at[pl.ds(2 * pair, 2)], ox_send.at[0], ox_recv.at[0],
                    beside_lat, tile,
                ).start()
                return carry

            lax.fori_loop(0, TILES, send_x, 0)

        out[pl.ds(2 * pair, 2), pl.ds(pl.multiple_of(8 * block, 8), 8), :] = lam[lon]

        to_left.wait_send()
        to_right.wait_send()
        wait_bytes(lam.at[pl.ds(0, TILES - 1)], in_send.at[0])
        wait_bytes(coef.at[pl.ds(0, TILES - 1)], cf_send.at[0])

        def drain(s, carry):
            @pl.when(block > 0)
            def _():
                wait_bytes(edge_out.at[s, 0], step_send.at[s, 0])

            @pl.when(block < BLOCKS - 1)
            def _():
                wait_bytes(edge_out.at[s, 1], step_send.at[s, 1])

            return carry

        lax.fori_loop(0, STEPS, drain, 0)

        @pl.when(has_extra)
        def _():
            wait_bytes(lam_x, ox_send.at[0])

        wait_bytes(lam.at[pl.ds(0, TILES - 1)], out_send.at[0])
        wait_bytes(lam.at[pl.ds(0, TILES - 1)], out_recv.at[0])

    @pl.when(jnp.logical_not(polar))
    def _():
        beside_rows = pl.ds(pl.multiple_of(jnp.where(lat == 1, 0, ROWS - 8), 8), 8)

        @pl.when(beside)
        def _():
            for p in range(PAIRS):
                remote(
                    cot.at[pl.ds(2 * p, 2), beside_rows], lam_x.at[lon],
                    lx_send.at[0], lx_recv.at[0], polar_lat, edge_block * PAIRS + p,
                ).start()

        wait_rows()
        lane = iota((EXT, LANES), 1)
        total = jnp.zeros((EXT, LANES), F32)
        for p in range(PLANES):
            v = ext[p]
            u = jnp.where(lane < EDGE, v, pltpu.roll(v, 2 * EDGE, 1))
            if p:
                u = pltpu.roll(u, 8 * p, 1)
            total = jnp.where((lane // 8) == p, u, total)
        packed[...] = total
        to_left = remote(packed, packed_r, col_send.at[0], col_recv.at[0], lat, left)
        to_right = remote(packed, packed_l, col_send.at[1], col_recv.at[1], lat, right)
        to_left.start()
        to_right.start()
        to_left.wait_recv()
        to_right.wait_recv()

        def beyond(p):
            from_right = packed_r[...]
            if p:
                from_right = pltpu.roll(from_right, LANES - 8 * p, 1)
            from_left = pltpu.roll(packed_l[...], (LANES - 8 - 8 * p) % LANES, 1)
            return jnp.where(lane < LANES // 2, from_right, from_left)

        def east_of(x):
            here, there = (pltpu.roll(v, LANES - 1, 1) for v in x)
            last = lane == LANES - 1
            return jnp.where(last, there, here), jnp.where(last, here, there)

        def west_of(x):
            here, there = (pltpu.roll(v, 1, 1) for v in x)
            last = lane == 0
            return jnp.where(last, there, here), jnp.where(last, here, there)

        def north_of(x):
            return [pltpu.roll(v, EXT - 1, 0) for v in x]

        def south_of(x):
            return [pltpu.roll(v, 1, 0) for v in x]

        def both(p):
            return ext[p], beyond(p)

        kappa_e, speed_e, kappa_n, speed_n, open_m = (both(LEVELS + k) for k in range(5))

        def minus(kappa, speed):
            return [m * (-k - 0.5 * f) for m, k, f in zip(open_m, kappa, speed)]

        def plus(kappa, speed):
            return [m * (k - 0.5 * f) for m, k, f in zip(open_m, kappa, speed)]

        faces = (
            [a * b for a, b in zip(minus(kappa_e, speed_e), east_of(open_m))],
            [-a * b for a, b in zip(open_m, west_of(plus(kappa_e, speed_e)))],
            [a * b for a, b in zip(minus(kappa_n, speed_n), north_of(open_m))],
            [-a * b for a, b in zip(open_m, south_of(plus(kappa_n, speed_n)))],
        )
        for k in range(4):
            for side in range(2):
                wide_coef[k, side] = faces[k][side]

        @pl.when(beside)
        def _():
            rows = pl.ds(pl.multiple_of(jnp.where(lat == 1, HALO, ROWS), 8), 8)
            coef_x_src[...] = wide_coef[:, 0, rows]
            for p in range(PAIRS):
                remote(
                    coef_x_src, coef_x.at[lon], cx_send.at[0], cx_recv.at[0],
                    polar_lat, edge_block * PAIRS + p,
                ).start()

        def level(p, carry):
            from_right = pltpu.roll(packed_r[...], LANES - 8 * p, 1)
            from_left = pltpu.roll(packed_l[...], LANES - 8 - 8 * p, 1)
            x = (ext[p], jnp.where(lane < LANES // 2, from_right, from_left))
            for _ in range(STEPS):
                new = list(x)
                for k, near in enumerate((east_of(x), west_of(x), north_of(x), south_of(x))):
                    for side in range(2):
                        new[side] = new[side] + wide_coef[k, side] * (x[side] - near[side])
                x = tuple(new)
            out[p] = x[0][HALO : HALO + ROWS]
            return carry

        lax.fori_loop(0, LEVELS, level, 0)

        to_left.wait_send()
        to_right.wait_send()

        @pl.when(beside)
        def _():
            wait_bytes(cot.at[:, pl.ds(0, 8)], lx_send.at[0])
            wait_bytes(coef_x.at[pl.ds(0, PAIRS)], cx_send.at[0])
            wait_bytes(row_x, ox_recv.at[0])

        row = iota((LEVELS, 8, LANES), 1)

        @pl.when(lat == 1)
        def _():
            out[:, 0:8] = jnp.where(row < EDGE, row_x[...], out[:, 0:8])

        @pl.when(lat == LATS - 2)
        def _():
            out[:, ROWS - 8 : ROWS] = jnp.where(row < EDGE, out[:, ROWS - 8 : ROWS], row_x[...])

    @pl.when(lat > 0)
    def _():
        to_south.wait_send()

    @pl.when(lat < LATS - 1)
    def _():
        to_north.wait_send()


def shards(cotangent, diff_east, diff_north, flow_east, flow_north, sea_mask, cutoff):
    high, low, turn = tables()
    vmem = pl.BlockSpec(memory_space=pltpu.VMEM)
    smem = pl.BlockSpec(memory_space=pltpu.SMEM)
    dma = pltpu.SemaphoreType.DMA
    circles = pltpu.VMEM((TILES, 2, 8, LANES), F32)
    faces = pltpu.VMEM((TILES, 4, 8, LANES), F32)
    plane = pltpu.VMEM((ROWS, LANES), F32)
    tall = pltpu.VMEM((EXT, LANES), F32)
    edges = pltpu.VMEM((STEPS, 2, 2 * TILES, 1, LANES), F32)
    return pl.pallas_call(
        kernel,
        out_shape=jax.ShapeDtypeStruct((LEVELS, ROWS, LANES), F32),
        in_specs=[vmem] * 6 + [smem] + [vmem] * 3,
        out_specs=vmem,
        scratch_shapes=[
            pltpu.VMEM((PLANES, EXT, LANES), F32),
            circles,
            circles,
            faces,
            pltpu.VMEM((BLOCKS, 4, 8, LANES), F32),
            circles,
            faces,
            pltpu.VMEM((4, 8, LANES), F32),
            pltpu.VMEM((LEVELS, 8, LANES), F32),
            plane,
            plane,
            plane,
            tall,
            tall,
            tall,
            pltpu.VMEM((4, 2, EXT, LANES), F32),
            edges,
            edges,
            dma((2,)), dma((2,)), dma((2,)), dma((2,)),
            dma((1,)), dma((1,)), dma((1,)), dma((1,)),
            dma((1,)), dma((1,)), dma((1,)), dma((1,)),
            dma((STEPS, 2)), dma((STEPS, 2)),
            dma((1,)), dma((1,)), dma((1,)), dma((1,)),
        ],
        compiler_params=pltpu.CompilerParams(
            collective_id=0, has_side_effects=True, vmem_limit_bytes=40 * 1024 * 1024
        ),
    )(
        cotangent, diff_east, diff_north, flow_east, flow_north, sea_mask, cutoff,
        jnp.asarray(high), jnp.asarray(low), jnp.asarray(turn),
    )


def solution(mesh):
    return jax.shard_map(
        shards,
        mesh=mesh,
        in_specs=(
            P(None, "lat", "lon"),
            P("lat", "lon"),
            P("lat", "lon"),
            P("lat", "lon"),
            P("lat", "lon"),
            P("lat", "lon"),
            P("lat"),
        ),
        out_specs=P(None, "lat", "lon"),
        check_vma=False,
    )
```

```python
import functools
import math

import jax
import jax.numpy as jnp
import numpy as np
from jax import lax
from jax.experimental import pallas as pl
from jax.experimental.pallas import tpu as pltpu
from jax.sharding import PartitionSpec as P

STEPS = 4
LEVELS = 8
ROWS = 64
LANES = 128
TILES = 32
NLON = TILES * LANES
BLOCKS = 8
PAIRS = 4
HALO = 16
EXT = ROWS + 2 * HALO
WIDE = ROWS + HALO
PLANES = LEVELS + 5
MASK = LEVELS + 4
EDGE = 4
LATS = 8

F32 = jnp.float32


def tables():
    n = np.arange(LANES)
    angle = 2 * np.pi * (np.outer(n, n) % LANES) / LANES
    cos, sin = np.cos(angle), np.sin(angle)
    wide = np.block([[cos, -sin], [sin, cos]])
    q = np.arange(8)[:, None, None]
    c = np.arange(4)[None, :, None]
    first = 2 * np.pi * ((q * (n[None, None, :] + LANES * c)) % NLON) / NLON
    r = np.arange(4)[:, None]
    second = 2 * np.pi * ((r * n[None, :]) % 512) / 512

    def spread(values):
        values = values.reshape(-1, 1, LANES)
        return np.broadcast_to(values, (values.shape[0], 8, LANES)).astype(np.float32)

    turn = np.concatenate(
        [spread(np.cos(first)), spread(np.sin(first)), spread(np.cos(second)), spread(np.sin(second))]
    )
    return wide.astype(np.float32), turn


def cadd(x, y):
    return x[0] + y[0], x[1] + y[1]


def csub(x, y):
    return x[0] - y[0], x[1] - y[1]


def quarter(x, sign):
    if sign < 0:
        return x[1], -x[0]
    return -x[1], x[0]


def dft4(x, sign):
    even, odd = cadd(x[0], x[2]), csub(x[0], x[2])
    even2, odd2 = cadd(x[1], x[3]), quarter(csub(x[1], x[3]), sign)
    return [cadd(even, even2), cadd(odd, odd2), csub(even, even2), csub(odd, odd2)]


def dft8(x, sign):
    even = dft4([x[0], x[2], x[4], x[6]], sign)
    odd = dft4([x[1], x[3], x[5], x[7]], sign)
    half = math.sqrt(0.5)

    def eighth(v):
        rot = quarter(v, sign)
        return (v[0] + rot[0]) * half, (v[1] + rot[1]) * half

    odd[1] = eighth(odd[1])
    odd[2] = quarter(odd[2], sign)
    odd[3] = quarter(eighth(odd[3]), sign)
    return [cadd(e, o) for e, o in zip(even, odd)] + [csub(e, o) for e, o in zip(even, odd)]


def cmul(x, cos, sin, sign):
    if sign < 0:
        return x[0] * cos + x[1] * sin, x[1] * cos - x[0] * sin
    return x[0] * cos - x[1] * sin, x[1] * cos + x[0] * sin


def split_dot(left, high_ref, low_ref):
    high = left.astype(jnp.bfloat16)
    low = (left - high.astype(F32)).astype(jnp.bfloat16)
    dot = functools.partial(jnp.dot, preferred_element_type=F32)
    return dot(high, high_ref[...]) + (dot(low, high_ref[...]) + dot(high, low_ref[...]))


def filter_circles(real, imag, cuts, high_ref, low_ref, turn_ref):
    shape = (8, 4, 8, LANES)
    cos1 = turn_ref[0:32].reshape(shape)
    sin1 = turn_ref[32:64].reshape(shape)
    real, imag = real.reshape(shape), imag.reshape(shape)
    parts = dft8([(real[a], imag[a]) for a in range(8)], -1)
    parts = [cmul(parts[q], cos1[q], sin1[q], -1) for q in range(8)]
    real = jnp.stack([p[0] for p in parts])
    imag = jnp.stack([p[1] for p in parts])
    parts = dft4([(real[:, c], imag[:, c]) for c in range(4)], -1)
    parts = [parts[0]] + [
        cmul(parts[r], turn_ref[64 + r], turn_ref[68 + r], -1) for r in range(1, 4)
    ]
    real = jnp.concatenate([p[0] for p in parts]).reshape(256, LANES)
    imag = jnp.concatenate([p[1] for p in parts]).reshape(256, LANES)
    spec = split_dot(jnp.concatenate([real, imag], axis=1), high_ref, low_ref)
    wave = lax.broadcasted_iota(jnp.int32, (TILES, 8, LANES), 0) + TILES * lax.broadcasted_iota(
        jnp.int32, (TILES, 8, LANES), 2
    )
    wave = jnp.minimum(wave, NLON - wave)
    kept = jnp.where(wave <= cuts[None], 1.0 / NLON, 0.0).astype(F32).reshape(256, LANES)
    real = spec[:, :LANES] * kept
    imag = spec[:, LANES:] * kept
    back = split_dot(jnp.concatenate([imag, real], axis=1), high_ref, low_ref)
    real = back[:, LANES:].reshape(4, 8, 8, LANES)
    imag = back[:, :LANES].reshape(4, 8, 8, LANES)
    parts = [(real[0], imag[0])] + [
        cmul((real[r], imag[r]), turn_ref[64 + r], turn_ref[68 + r], 1) for r in range(1, 4)
    ]
    parts = dft4(parts, 1)
    real = jnp.stack([p[0] for p in parts], axis=1)
    imag = jnp.stack([p[1] for p in parts], axis=1)
    parts = [cmul((real[q], imag[q]), cos1[q], sin1[q], 1) for q in range(8)]
    parts = dft8(parts, 1)
    real = jnp.concatenate([p[0] for p in parts])
    imag = jnp.concatenate([p[1] for p in parts])
    return real, imag


def iota(shape, dim):
    return lax.broadcasted_iota(jnp.int32, shape, dim)


def circle_step(x, coef):
    shape = (TILES * 4, 8, LANES)
    full = (TILES, 2, 2, 8, LANES)
    lane = iota(shape, 2)
    row = iota(full, 3)
    flat = x.reshape(shape)
    east = pltpu.roll(flat, LANES - 1, 2)
    east = jnp.where(lane == LANES - 1, jnp.concatenate([east[4:], east[:4]]), east)
    west = pltpu.roll(flat, 1, 2)
    west = jnp.where(lane == 0, jnp.concatenate([west[-4:], west[:-4]]), west)

    def across(turned, edge):
        turned = turned.reshape(full)
        other = jnp.stack([turned[:, :, 1], turned[:, :, 0]], axis=2)
        return jnp.where(row == edge, other, turned)

    up = across(pltpu.roll(flat, 7, 1), 7)
    down = across(pltpu.roll(flat, 1, 1), 0)
    total = x
    for k, near in enumerate((east.reshape(full), west.reshape(full), up, down)):
        total = total + coef[:, k : k + 1] * (x - near)
    return total


def kernel(
    cot, diff_east_in, diff_north_in, flow_east_in, flow_north_in, sea_in, cutoff_in, wide_in,
    turn_in,
    out,
    sea, cutoff, wide_ref, high_ref, low_ref, turn_ref,
    ext, lam_src, coef_src, cut_src, rim_e, rim_w, rim_src,
    lam, fil, coef, cuts_ref, row_x, packed, packed_l, packed_r, wide_coef, mid_out,
    load_sem, row_send, row_recv, col_send, col_recv, cut_send, cut_recv, in_send, in_recv,
    cf_send, cf_recv, out_send, out_recv, ox_recv, store_sem,
):
    lon = lax.axis_index("lon")
    lat = lax.axis_index("lat")
    y = lax.rem(lon, 4)
    z = lon // 4
    first_band = lat < LATS // 2
    polar = jnp.logical_or(lat == 0, lat == LATS - 1)
    beside = jnp.logical_or(lat == 1, lat == LATS - 2)
    polar_lat = jnp.where(first_band, 0, LATS - 1)
    beside_lat = jnp.where(first_band, 1, LATS - 2)
    plane = jnp.where(first_band, lat - 1, LATS - 2 - lat)
    skew = lax.rem(y + 8 - z, 4)
    odd = lax.rem(skew, 2) == 1
    is_owner = jnp.logical_and(
        jnp.logical_and(plane >= 0, plane < 2), jnp.logical_or(jnp.logical_not(odd), z == 0)
    )
    block = jnp.where(odd, BLOCKS, z)
    pair = 2 * jnp.clip(plane, 0, 1) + skew // 2
    last_block = block == BLOCKS

    def owner_of(b, p):
        spot = lax.rem(b, 8) * 4 + lax.rem(b + b // 8 + 2 * (p % 2), 4)
        return jnp.where(first_band, 1 + p // 2, LATS - 2 - p // 2), spot

    main = pl.ds(HALO, ROWS)
    plane_loads = [
        pltpu.make_async_copy(src, dst, load_sem.at[k])
        for k, (src, dst) in enumerate(
            (
                (sea_in, sea),
                (diff_east_in, ext.at[LEVELS, main]),
                (flow_east_in, ext.at[LEVELS + 1, main]),
                (diff_north_in, ext.at[LEVELS + 2, main]),
                (flow_north_in, ext.at[LEVELS + 3, main]),
                (cot, ext.at[pl.ds(0, LEVELS), main]),
            )
        )
    ]
    cut_load = pltpu.make_async_copy(cutoff_in, cutoff, load_sem.at[6])
    table_loads = [
        pltpu.make_async_copy(turn_in, turn_ref, load_sem.at[7]),
        pltpu.make_async_copy(wide_in, wide_ref, load_sem.at[8]),
    ]
    for load in plane_loads:
        load.start()

    @pl.when(polar)
    def _():
        cut_load.start()

    @pl.when(is_owner)
    def _():
        for load in table_loads:
            load.start()

    barrier = pltpu.get_barrier_semaphore()

    def at(to_lat, to_lon):
        return {"lon": to_lon, "lat": to_lat}

    def hail(to_lat, to_lon):
        pl.semaphore_signal(
            barrier, inc=1, device_id=at(to_lat, to_lon), device_id_type=pl.DeviceIdType.MESH
        )

    def remote(src, dst, send, recv, to_lat, to_lon):
        return pltpu.make_async_remote_copy(
            src_ref=src, dst_ref=dst, send_sem=send, recv_sem=recv,
            device_id=at(to_lat, to_lon), device_id_type=pl.DeviceIdType.MESH,
        )

    def wait_bytes(ref, sem):
        pltpu.make_async_copy(ref, ref, sem).wait()

    def over(count, body):
        def go(k, carry):
            body(k)
            return carry

        lax.fori_loop(0, count, go, 0)

    right = lax.rem(lon + 1, TILES)
    left = lax.rem(lon + TILES - 1, TILES)

    @pl.when(polar)
    def _():
        def greet(t):
            b = lax.rem(z + 4 + t, BLOCKS)
            for p in range(PAIRS):
                hail(*owner_of(b, p))

        over(BLOCKS, greet)

    @pl.when(is_owner)
    def _():
        over(TILES, lambda t: hail(polar_lat, lax.rem(lon + TILES // 2 + t, TILES)))

    @pl.when(beside)
    def _():
        for p in range(PAIRS):
            to_lat, to_lon = owner_of(BLOCKS, p)

            @pl.when(jnp.logical_not(jnp.logical_and(to_lat == lat, to_lon == lon)))
            def _():
                hail(to_lat, to_lon)

    hail(lat, left)
    hail(lat, right)

    @pl.when(lat > 0)
    def _():
        hail(lat - 1, lon)

    @pl.when(lat < LATS - 1)
    def _():
        hail(lat + 1, lon)

    for load in plane_loads:
        load.wait()
    ext[MASK, HALO : HALO + ROWS] = sea[...].astype(F32)
    sub = iota((LEVELS, 8, LANES), 1)

    def fill(b, tile):
        rows = 8 * tile
        lam_src[b, :, 0] = ext[0:LEVELS, rows : rows + 8]
        lam_src[b, :, 1] = jnp.where(
            sub < EDGE, ext[0:LEVELS, rows + 8 : rows + 16], ext[0:LEVELS, rows - 8 : rows]
        )

    def plus_face(kappa, rows):
        return ext[MASK, rows] * (ext[LEVELS + kappa, rows] - 0.5 * ext[LEVELS + kappa + 1, rows])

    def minus_face(kappa, rows):
        return -ext[MASK, rows] * (ext[LEVELS + kappa, rows] + 0.5 * ext[LEVELS + kappa + 1, rows])

    @pl.when(polar)
    def _():
        zeros = jnp.zeros((PLANES, 8, LANES), F32)
        ext[:, 0:8] = zeros
        ext[:, EXT - 8 : EXT] = zeros

        @pl.when(lat == 0)
        def _():
            ext[:, 8:16] = zeros
            rim_e[8:16] = zeros[0]
            rim_w[8:16] = zeros[0]
            for b in range(BLOCKS - 1):
                fill(b, b + 2)

        @pl.when(lat > 0)
        def _():
            ext[:, EXT - 16 : EXT - 8] = zeros
            rim_e[EXT - 16 : EXT - 8] = zeros[0]
            rim_w[EXT - 16 : EXT - 8] = zeros[0]
            for b in range(1, BLOCKS):
                fill(b, b + 2)

        rim_src[...] = jnp.zeros((EXT, LANES), F32)
        rim_src[HALO : HALO + ROWS] = plus_face(0, slice(HALO, HALO + ROWS))

        cut_load.wait()
        row = iota((8, LANES), 0)
        open_cut = jnp.full((8, LANES), float(NLON // 2), F32)
        cuts = [open_cut, open_cut]
        for b in range(BLOCKS):
            tile = open_cut
            for j in range(8):
                tile = jnp.where(row == j, cutoff[8 * b + j].astype(F32), tile)
            cuts.append(tile)
        cuts += [open_cut, open_cut]
        for b in range(BLOCKS):
            cut_src[b, 0] = cuts[b + 2]
            cut_src[b, 1] = jnp.where(row < EDGE, cuts[b + 3], cuts[b + 1])
        cut_src[BLOCKS, 0] = open_cut
        low_half = jnp.where(first_band, open_cut, cuts[2])
        high_half = jnp.where(first_band, cuts[BLOCKS + 1], open_cut)
        cut_src[BLOCKS, 1] = jnp.where(row < EDGE, low_half, high_half)

    peers = jnp.where(polar, 3 + 9 * PAIRS, 4)
    own_beside = jnp.logical_and(last_block, plane == 0)
    from_tiles = jnp.where(own_beside, TILES - 1, TILES)
    peers = peers + jnp.where(is_owner, from_tiles, 0)
    pl.semaphore_wait(barrier, peers)

    low_rows = ext.at[:, pl.ds(HALO, 8)]
    high_rows = ext.at[:, pl.ds(HALO + ROWS - 8, 8)]
    south_rows = ext.at[:, pl.ds(HALO - 8, 8)]
    north_rows = ext.at[:, pl.ds(HALO + ROWS, 8)]
    to_south = remote(low_rows, north_rows, row_send.at[0], row_recv.at[0], lat - 1, lon)
    to_north = remote(high_rows, south_rows, row_send.at[1], row_recv.at[1], lat + 1, lon)

    @pl.when(lat > 0)
    def _():
        to_south.start()

    @pl.when(lat < LATS - 1)
    def _():
        to_north.start()

    def wait_rows():
        @pl.when(lat < LATS - 1)
        def _():
            to_south.wait_recv()

        @pl.when(lat > 0)
        def _():
            to_north.wait_recv()

    @pl.when(polar)
    def _():
        extra = pl.ds(pl.multiple_of(jnp.where(lat == 0, HALO + ROWS, HALO - 8), 8), 8)
        rims = [
            remote(ext.at[MASK, main], rim_e.at[main], col_send.at[0], col_recv.at[0], lat, left),
            remote(rim_src.at[main], rim_w.at[main], col_send.at[1], col_recv.at[1], lat, right),
            remote(ext.at[MASK, extra], rim_e.at[extra], col_send.at[2], col_recv.at[2], lat, left),
            remote(rim_src.at[extra], rim_w.at[extra], col_send.at[3], col_recv.at[3], lat, right),
        ]
        rims[0].start()
        rims[1].start()
        wait_rows()

        @pl.when(lat == 0)
        def _():
            rim_src[HALO + ROWS : HALO + ROWS + 8] = plus_face(
                0, slice(HALO + ROWS, HALO + ROWS + 8)
            )

        @pl.when(lat > 0)
        def _():
            rim_src[HALO - 8 : HALO] = plus_face(0, slice(HALO - 8, HALO))

        rims[2].start()
        rims[3].start()

        @pl.when(lat == 0)
        def _():
            fill(BLOCKS - 1, BLOCKS + 1)
            fill(BLOCKS, BLOCKS + 2)

        @pl.when(lat > 0)
        def _():
            fill(0, 2)
            fill(BLOCKS, 1)

        cut_sends = []
        for h in range(2):
            to_lat = jnp.where(first_band, 1 + h, LATS - 2 - h)
            cut_sends.append(
                remote(
                    cut_src.at[block], cuts_ref, cut_send.at[h], cut_recv.at[0], to_lat, lon
                )
            )
        owner_spot = jnp.logical_or(jnp.logical_not(odd), z == 0)

        @pl.when(owner_spot)
        def _():
            for send in cut_sends:
                send.start()

        def send_in(t):
            b = lax.rem(z + 4 + t, BLOCKS + 1)
            for p in range(PAIRS):
                remote(
                    lam_src.at[b, pl.ds(2 * p, 2)], lam.at[lon], in_send.at[0], in_recv.at[0],
                    *owner_of(b, p),
                ).start()

        over(BLOCKS + 1, send_in)

        for rim in rims:
            rim.wait_recv()
        here = slice(8, 8 + WIDE)
        lane = iota((WIDE, LANES), 1)
        mine = ext[MASK, here]
        mask_east = jnp.where(
            lane == LANES - 1, pltpu.roll(rim_e[here], LANES - 1, 1), pltpu.roll(mine, LANES - 1, 1)
        )
        plus_west = jnp.where(
            lane == 0, pltpu.roll(rim_w[here], 1, 1), pltpu.roll(rim_src[here], 1, 1)
        )
        faces = (
            minus_face(0, here) * mask_east,
            -mine * plus_west,
            minus_face(2, here) * ext[MASK, 9 : 9 + WIDE],
            -mine * plus_face(2, slice(7, 7 + WIDE)),
        )
        low = iota((8, LANES), 0) < EDGE
        for k in range(4):
            face = faces[k].reshape(WIDE // 8, 8, LANES)
            coef_src[0:BLOCKS, k, 0] = face[1:9]
            coef_src[0:BLOCKS, k, 1] = jnp.where(low[None], face[2:10], face[0:8])

            @pl.when(lat == 0)
            def _():
                coef_src[BLOCKS, k, 0] = face[9]
                coef_src[BLOCKS, k, 1] = jnp.where(low, 0.0, face[8])

            @pl.when(lat > 0)
            def _():
                coef_src[BLOCKS, k, 0] = face[0]
                coef_src[BLOCKS, k, 1] = jnp.where(low, face[1], 0.0)

        def send_coef(t):
            b = lax.rem(z + 4 + t, BLOCKS + 1)
            for p in range(PAIRS):
                remote(
                    coef_src.at[b], coef.at[lon], cf_send.at[p], cf_recv.at[0], *owner_of(b, p)
                ).start()

        over(BLOCKS + 1, send_coef)

        for rim in rims:
            rim.wait_send()

        @pl.when(owner_spot)
        def _():
            for send in cut_sends:
                send.wait_send()

        wait_bytes(lam_src, in_send.at[0])
        for p in range(PAIRS):
            wait_bytes(coef_src, cf_send.at[p])
        wait_bytes(out, out_recv.at[0])

    @pl.when(jnp.logical_not(polar))
    def _():
        wait_rows()
        here = slice(8, 8 + WIDE)
        lane = iota((WIDE, LANES), 1)
        total = jnp.zeros((WIDE, LANES), F32)
        for p in range(PLANES):
            v = ext[p, here]
            u = jnp.where(lane < EDGE, v, pltpu.roll(v, 2 * EDGE, 1))
            if p:
                u = pltpu.roll(u, 8 * p, 1)
            total = jnp.where((lane // 8) == p, u, total)
        packed[...] = total
        to_left = remote(packed, packed_r, col_send.at[0], col_recv.at[0], lat, left)
        to_right = remote(packed, packed_l, col_send.at[1], col_recv.at[1], lat, right)
        to_left.start()
        to_right.start()
        to_left.wait_recv()
        to_right.wait_recv()

        def beyond(p):
            from_right = packed_r[...]
            if p:
                from_right = pltpu.roll(from_right, LANES - 8 * p, 1)
            from_left = pltpu.roll(packed_l[...], (LANES - 8 - 8 * p) % LANES, 1)
            return jnp.where(lane < LANES // 2, from_right, from_left)

        def east_of(x):
            near, far = (pltpu.roll(v, LANES - 1, 1) for v in x)
            last = lane == LANES - 1
            return jnp.where(last, far, near), jnp.where(last, near, far)

        def west_of(x):
            near, far = (pltpu.roll(v, 1, 1) for v in x)
            last = lane == 0
            return jnp.where(last, far, near), jnp.where(last, near, far)

        def north_of(x):
            return [pltpu.roll(v, WIDE - 1, 0) for v in x]

        def south_of(x):
            return [pltpu.roll(v, 1, 0) for v in x]

        kappa_e, speed_e, kappa_n, speed_n, open_m = (
            (ext[LEVELS + k, here], beyond(LEVELS + k)) for k in range(5)
        )

        def minus(kappa, speed):
            return [m * (-k - 0.5 * f) for m, k, f in zip(open_m, kappa, speed)]

        def plus(kappa, speed):
            return [m * (k - 0.5 * f) for m, k, f in zip(open_m, kappa, speed)]

        faces = (
            [a * b for a, b in zip(minus(kappa_e, speed_e), east_of(open_m))],
            [-a * b for a, b in zip(open_m, west_of(plus(kappa_e, speed_e)))],
            [a * b for a, b in zip(minus(kappa_n, speed_n), north_of(open_m))],
            [-a * b for a, b in zip(open_m, south_of(plus(kappa_n, speed_n)))],
        )
        for k in range(4):
            for side in range(2):
                wide_coef[k, side] = faces[k][side]

        def level(p):
            from_right = pltpu.roll(packed_r[...], LANES - 8 * p, 1)
            from_left = pltpu.roll(packed_l[...], LANES - 8 - 8 * p, 1)
            x = (ext[p, here], jnp.where(lane < LANES // 2, from_right, from_left))
            for _ in range(STEPS):
                new = list(x)
                for k, near in enumerate((east_of(x), west_of(x), north_of(x), south_of(x))):
                    for side in range(2):
                        new[side] = new[side] + wide_coef[k, side] * (x[side] - near[side])
                x = tuple(new)
            mid_out[p] = x[0][8 : 8 + ROWS]

        over(LEVELS, level)

        kept = pl.ds(pl.multiple_of(jnp.where(first_band, 8, 0), 8), ROWS - 8)
        shared = pl.ds(pl.multiple_of(jnp.where(first_band, 0, ROWS - 8), 8), 8)
        store_kept = pltpu.make_async_copy(mid_out.at[:, kept], out.at[:, kept], store_sem.at[0])
        store_shared = pltpu.make_async_copy(
            mid_out.at[:, shared], out.at[:, shared], store_sem.at[1]
        )
        store_kept.start()

        @pl.when(jnp.logical_not(beside))
        def _():
            store_shared.start()

        @pl.when(is_owner)
        def _():
            for load in table_loads:
                load.wait()
            high = wide_ref[...].astype(jnp.bfloat16)
            high_ref[...] = high
            low_ref[...] = (wide_ref[...] - high.astype(F32)).astype(jnp.bfloat16)
            wait_bytes(cuts_ref, cut_recv.at[0])
            cuts = cuts_ref[...].astype(jnp.int32)
            wait_bytes(lam, in_recv.at[0])

            def step(s):
                for half in range(2):
                    real, imag = filter_circles(
                        lam[:, 0, half], lam[:, 1, half], cuts[half], high_ref, low_ref, turn_ref
                    )
                    fil[:, 0, half] = real
                    fil[:, 1, half] = imag

                @pl.when(s == 0)
                def _():
                    wait_bytes(coef, cf_recv.at[0])

                lam[...] = circle_step(fil[...], coef[...])

            over(STEPS, step)

            my_levels = pl.ds(2 * pair, 2)

            @pl.when(jnp.logical_not(last_block))
            def _():
                rows = pl.ds(pl.multiple_of(8 * jnp.minimum(block, BLOCKS - 1), 8), 8)

                def send_out(t):
                    tile = lax.rem(lon + TILES // 2 + t, TILES)
                    remote(
                        lam.at[tile, :, 0], out.at[my_levels, rows], out_send.at[0],
                        out_recv.at[0], polar_lat, tile,
                    ).start()

                over(TILES, send_out)
                wait_bytes(lam.at[:, :, 0], out_send.at[0])

            @pl.when(last_block)
            def _():
                def send_x(t):
                    tile = lax.rem(lon + 1 + t, TILES)
                    remote(
                        lam.at[tile, :, 0], row_x.at[my_levels], out_send.at[0], ox_recv.at[0],
                        beside_lat, tile,
                    ).start()

                over(TILES - 1, send_x)

                @pl.when(plane > 0)
                def _():
                    send_x(TILES - 1)
                    wait_bytes(lam.at[0, :, 0], out_send.at[0])

                @pl.when(plane == 0)
                def _():
                    pltpu.make_async_copy(
                        lam.at[lon, :, 0], row_x.at[my_levels], ox_recv.at[0]
                    ).start()

                wait_bytes(lam.at[pl.ds(0, TILES - 1), :, 0], out_send.at[0])

        to_left.wait_send()
        to_right.wait_send()

        @pl.when(beside)
        def _():
            wait_bytes(row_x, ox_recv.at[0])

            @pl.when(lat == 1)
            def _():
                mid_out[:, 0:8] = jnp.where(sub < EDGE, row_x[...], mid_out[:, 0:8])

            @pl.when(lat > 1)
            def _():
                mid_out[:, ROWS - 8 : ROWS] = jnp.where(
                    sub < EDGE, mid_out[:, ROWS - 8 : ROWS], row_x[...]
                )

            store_shared.start()

        store_kept.wait()
        store_shared.wait()

    @pl.when(lat > 0)
    def _():
        to_south.wait_send()

    @pl.when(lat < LATS - 1)
    def _():
        to_north.wait_send()


def shards(cotangent, diff_east, diff_north, flow_east, flow_north, sea_mask, cutoff):
    wide, turn = tables()
    hbm = pl.BlockSpec(memory_space=pltpu.HBM)
    dma = pltpu.SemaphoreType.DMA

    def room(*shape):
        return pltpu.VMEM(shape, F32)

    table = pltpu.VMEM((2 * LANES, 2 * LANES), jnp.bfloat16)
    return pl.pallas_call(
        kernel,
        out_shape=jax.ShapeDtypeStruct((LEVELS, ROWS, LANES), F32),
        in_specs=[hbm] * 9,
        out_specs=hbm,
        scratch_shapes=[
            pltpu.VMEM((ROWS, LANES), jnp.int32),
            pltpu.SMEM((ROWS,), jnp.int32),
            room(2 * LANES, 2 * LANES),
            table,
            table,
            room(72, 8, LANES),
            room(PLANES, EXT, LANES),
            room(BLOCKS + 1, LEVELS, 2, 8, LANES),
            room(BLOCKS + 1, 4, 2, 8, LANES),
            room(BLOCKS + 1, 2, 8, LANES),
            room(EXT, LANES),
            room(EXT, LANES),
            room(EXT, LANES),
            room(TILES, 2, 2, 8, LANES),
            room(TILES, 2, 2, 8, LANES),
            room(TILES, 4, 2, 8, LANES),
            room(2, 8, LANES),
            room(LEVELS, 8, LANES),
            room(WIDE, LANES),
            room(WIDE, LANES),
            room(WIDE, LANES),
            room(4, 2, WIDE, LANES),
            room(LEVELS, ROWS, LANES),
            dma((9,)),
            dma((2,)), dma((2,)), dma((4,)), dma((4,)), dma((2,)), dma((1,)), dma((1,)), dma((1,)),
            dma((4,)), dma((1,)), dma((1,)), dma((1,)), dma((1,)), dma((2,)),
        ],
        compiler_params=pltpu.CompilerParams(
            collective_id=0, has_side_effects=True, vmem_limit_bytes=63 * 1024 * 1024
        ),
    )(
        cotangent, diff_east, diff_north, flow_east, flow_north, sea_mask, cutoff,
        jnp.asarray(wide), jnp.asarray(turn),
    )


def solution(mesh):
    return jax.shard_map(
        shards,
        mesh=mesh,
        in_specs=(
            P(None, "lat", "lon"),
            P("lat", "lon"),
            P("lat", "lon"),
            P("lat", "lon"),
            P("lat", "lon"),
            P("lat", "lon"),
            P("lat"),
        ),
        out_specs=P(None, "lat", "lon"),
        check_vma=False,
    )
```

```python
import functools
import math

import jax
import jax.numpy as jnp
import numpy as np
from jax import lax
from jax.experimental import pallas as pl
from jax.experimental.pallas import tpu as pltpu
from jax.sharding import PartitionSpec as P

STEPS = 4
LEVELS = 8
ROWS = 64
LANES = 128
TILES = 32
NLON = TILES * LANES
BLOCKS = 8
PAIRS = 4
HALO = 16
EXT = ROWS + 2 * HALO
WIDE = ROWS + HALO
PLANES = LEVELS + 5
MASK = LEVELS + 4
EDGE = 4
LATS = 8
COLS = 4
RINGS = 8
LAST_RING = 4

F32 = jnp.float32


def tables():
    n = np.arange(LANES)
    angle = 2 * np.pi * (np.outer(n, n) % LANES) / LANES
    cos, sin = np.cos(angle), np.sin(angle)
    wide = np.block([[cos, -sin], [sin, cos]])
    q = np.arange(8)[:, None, None]
    c = np.arange(4)[None, :, None]
    first = 2 * np.pi * ((q * (n[None, None, :] + LANES * c)) % NLON) / NLON
    r = np.arange(4)[:, None]
    second = 2 * np.pi * ((r * n[None, :]) % 512) / 512

    def spread(values):
        values = values.reshape(-1, 1, LANES)
        return np.broadcast_to(values, (values.shape[0], 8, LANES)).astype(np.float32)

    turn = np.concatenate(
        [spread(np.cos(first)), spread(np.sin(first)), spread(np.cos(second)), spread(np.sin(second))]
    )
    return wide.astype(np.float32), turn


def cadd(x, y):
    return x[0] + y[0], x[1] + y[1]


def csub(x, y):
    return x[0] - y[0], x[1] - y[1]


def quarter(x, sign):
    if sign < 0:
        return x[1], -x[0]
    return -x[1], x[0]


def dft4(x, sign):
    even, odd = cadd(x[0], x[2]), csub(x[0], x[2])
    even2, odd2 = cadd(x[1], x[3]), quarter(csub(x[1], x[3]), sign)
    return [cadd(even, even2), cadd(odd, odd2), csub(even, even2), csub(odd, odd2)]


def dft8(x, sign):
    even = dft4([x[0], x[2], x[4], x[6]], sign)
    odd = dft4([x[1], x[3], x[5], x[7]], sign)
    half = math.sqrt(0.5)

    def eighth(v):
        rot = quarter(v, sign)
        return (v[0] + rot[0]) * half, (v[1] + rot[1]) * half

    odd[1] = eighth(odd[1])
    odd[2] = quarter(odd[2], sign)
    odd[3] = quarter(eighth(odd[3]), sign)
    return [cadd(e, o) for e, o in zip(even, odd)] + [csub(e, o) for e, o in zip(even, odd)]


def cmul(x, cos, sin, sign):
    if sign < 0:
        return x[0] * cos + x[1] * sin, x[1] * cos - x[0] * sin
    return x[0] * cos - x[1] * sin, x[1] * cos + x[0] * sin


def split_dot(left, high_ref, low_ref):
    high = left.astype(jnp.bfloat16)
    low = (left - high.astype(F32)).astype(jnp.bfloat16)
    dot = functools.partial(jnp.dot, preferred_element_type=F32)
    return dot(high, high_ref[...]) + (dot(low, high_ref[...]) + dot(high, low_ref[...]))


def filter_circles(real, imag, cuts, high_ref, low_ref, turn_ref):
    shape = (8, 4, 8, LANES)
    cos1 = turn_ref[0:32].reshape(shape)
    sin1 = turn_ref[32:64].reshape(shape)
    real, imag = real.reshape(shape), imag.reshape(shape)
    parts = dft8([(real[a], imag[a]) for a in range(8)], -1)
    parts = [cmul(parts[q], cos1[q], sin1[q], -1) for q in range(8)]
    real = jnp.stack([p[0] for p in parts])
    imag = jnp.stack([p[1] for p in parts])
    parts = dft4([(real[:, c], imag[:, c]) for c in range(4)], -1)
    parts = [parts[0]] + [
        cmul(parts[r], turn_ref[64 + r], turn_ref[68 + r], -1) for r in range(1, 4)
    ]
    real = jnp.concatenate([p[0] for p in parts]).reshape(256, LANES)
    imag = jnp.concatenate([p[1] for p in parts]).reshape(256, LANES)
    spec = split_dot(jnp.concatenate([real, imag], axis=1), high_ref, low_ref)
    wave = lax.broadcasted_iota(jnp.int32, (TILES, 8, LANES), 0) + TILES * lax.broadcasted_iota(
        jnp.int32, (TILES, 8, LANES), 2
    )
    wave = jnp.minimum(wave, NLON - wave)
    kept = jnp.where(wave <= cuts[None], 1.0 / NLON, 0.0).astype(F32).reshape(256, LANES)
    real = spec[:, :LANES] * kept
    imag = spec[:, LANES:] * kept
    back = split_dot(jnp.concatenate([imag, real], axis=1), high_ref, low_ref)
    real = back[:, LANES:].reshape(4, 8, 8, LANES)
    imag = back[:, :LANES].reshape(4, 8, 8, LANES)
    parts = [(real[0], imag[0])] + [
        cmul((real[r], imag[r]), turn_ref[64 + r], turn_ref[68 + r], 1) for r in range(1, 4)
    ]
    parts = dft4(parts, 1)
    real = jnp.stack([p[0] for p in parts], axis=1)
    imag = jnp.stack([p[1] for p in parts], axis=1)
    parts = [cmul((real[q], imag[q]), cos1[q], sin1[q], 1) for q in range(8)]
    parts = dft8(parts, 1)
    real = jnp.concatenate([p[0] for p in parts])
    imag = jnp.concatenate([p[1] for p in parts])
    return real, imag


def iota(shape, dim):
    return lax.broadcasted_iota(jnp.int32, shape, dim)


def circle_step(x, coef):
    shape = (TILES * 4, 8, LANES)
    full = (TILES, 2, 2, 8, LANES)
    lane = iota(shape, 2)
    row = iota(full, 3)
    flat = x.reshape(shape)
    east = pltpu.roll(flat, LANES - 1, 2)
    east = jnp.where(lane == LANES - 1, jnp.concatenate([east[4:], east[:4]]), east)
    west = pltpu.roll(flat, 1, 2)
    west = jnp.where(lane == 0, jnp.concatenate([west[-4:], west[:-4]]), west)

    def across(turned, edge):
        turned = turned.reshape(full)
        other = jnp.stack([turned[:, :, 1], turned[:, :, 0]], axis=2)
        return jnp.where(row == edge, other, turned)

    up = across(pltpu.roll(flat, 7, 1), 7)
    down = across(pltpu.roll(flat, 1, 1), 0)
    total = x
    for k, near in enumerate((east.reshape(full), west.reshape(full), up, down)):
        face = jnp.stack([coef[c, :, k] for c in range(COLS)], axis=1).reshape(TILES, 1, 2, 8, LANES)
        total = total + face * (x - near)
    return total


def kernel(
    cot, diff_east_in, diff_north_in, flow_east_in, flow_north_in, sea_in, cutoff_in, wide_in,
    turn_in,
    out,
    sea, cutoff, wide_ref, high_ref, low_ref, turn_ref,
    ext, lam_src, coef_src, cut_src, rim_e, rim_w, rim_src,
    lam, fil, coef, cuts_ref, row_x, packed, packed_l, packed_r, wide_coef, mid_out,
    load_sem, row_send, row_recv, col_send, col_recv, cut_send, cut_recv, in_send, in_recv,
    cf_send, cf_recv, pass_send, pass_recv, out_send, out_recv, ox_recv, store_sem,
):
    lon = lax.axis_index("lon")
    lat = lax.axis_index("lat")
    y = lax.rem(lon, 4)
    z = lon // 4
    first_band = lat < LATS // 2
    polar = jnp.logical_or(lat == 0, lat == LATS - 1)
    beside = jnp.logical_or(lat == 1, lat == LATS - 2)
    polar_lat = jnp.where(first_band, 0, LATS - 1)
    beside_lat = jnp.where(first_band, 1, LATS - 2)
    last_lat = jnp.where(first_band, 2, LATS - 3)
    last_block = jnp.logical_and(lat == last_lat, z == LAST_RING)
    is_owner = jnp.logical_or(beside, last_block)
    block = jnp.where(beside, z, BLOCKS)
    pair = y

    def owner_of(b, p):
        to_lat = jnp.where(b == BLOCKS, last_lat, beside_lat)
        return to_lat, COLS * jnp.where(b == BLOCKS, LAST_RING, b) + p

    main = pl.ds(HALO, ROWS)
    plane_loads = [
        pltpu.make_async_copy(src, dst, load_sem.at[k])
        for k, (src, dst) in enumerate(
            (
                (sea_in, sea),
                (diff_east_in, ext.at[LEVELS, main]),
                (flow_east_in, ext.at[LEVELS + 1, main]),
                (diff_north_in, ext.at[LEVELS + 2, main]),
                (flow_north_in, ext.at[LEVELS + 3, main]),
                (cot, ext.at[pl.ds(0, LEVELS), main]),
            )
        )
    ]
    cut_load = pltpu.make_async_copy(cutoff_in, cutoff, load_sem.at[6])
    table_loads = [
        pltpu.make_async_copy(turn_in, turn_ref, load_sem.at[7]),
        pltpu.make_async_copy(wide_in, wide_ref, load_sem.at[8]),
    ]
    for load in plane_loads:
        load.start()

    @pl.when(polar)
    def _():
        cut_load.start()

    @pl.when(is_owner)
    def _():
        for load in table_loads:
            load.start()

    barrier = pltpu.get_barrier_semaphore()

    def at(to_lat, to_lon):
        return {"lon": to_lon, "lat": to_lat}

    def hail(to_lat, to_lon):
        pl.semaphore_signal(
            barrier, inc=1, device_id=at(to_lat, to_lon), device_id_type=pl.DeviceIdType.MESH
        )

    def remote(src, dst, send, recv, to_lat, to_lon):
        return pltpu.make_async_remote_copy(
            src_ref=src, dst_ref=dst, send_sem=send, recv_sem=recv,
            device_id=at(to_lat, to_lon), device_id_type=pl.DeviceIdType.MESH,
        )

    def wait_bytes(ref, sem):
        pltpu.make_async_copy(ref, ref, sem).wait()

    def over(count, body):
        def go(k, carry):
            body(k)
            return carry

        lax.fori_loop(0, count, go, 0)

    right = lax.rem(lon + 1, TILES)
    left = lax.rem(lon + TILES - 1, TILES)

    @pl.when(polar)
    def _():
        def greet(t):
            b = lax.rem(z + 4 + t, BLOCKS)
            for p in range(PAIRS):
                hail(*owner_of(b, p))

        over(BLOCKS, greet)

    @pl.when(is_owner)
    def _():
        over(TILES, lambda t: hail(polar_lat, lax.rem(lon + TILES // 2 + t, TILES)))
        for c in range(1, COLS):
            hail(lat, COLS * z + lax.rem(y + c, COLS))

    @pl.when(beside)
    def _():
        for p in range(PAIRS):
            hail(*owner_of(BLOCKS, p))

    hail(lat, left)
    hail(lat, right)

    @pl.when(lat > 0)
    def _():
        hail(lat - 1, lon)

    @pl.when(lat < LATS - 1)
    def _():
        hail(lat + 1, lon)

    for load in plane_loads:
        load.wait()
    ext[MASK, HALO : HALO + ROWS] = sea[...].astype(F32)
    sub = iota((LEVELS, 8, LANES), 1)

    def fill(b, tile):
        rows = 8 * tile
        lam_src[b, :, 0] = ext[0:LEVELS, rows : rows + 8]
        lam_src[b, :, 1] = jnp.where(
            sub < EDGE, ext[0:LEVELS, rows + 8 : rows + 16], ext[0:LEVELS, rows - 8 : rows]
        )

    def plus_face(kappa, rows):
        return ext[MASK, rows] * (ext[LEVELS + kappa, rows] - 0.5 * ext[LEVELS + kappa + 1, rows])

    def minus_face(kappa, rows):
        return -ext[MASK, rows] * (ext[LEVELS + kappa, rows] + 0.5 * ext[LEVELS + kappa + 1, rows])

    @pl.when(polar)
    def _():
        zeros = jnp.zeros((PLANES, 8, LANES), F32)
        ext[:, 0:8] = zeros
        ext[:, EXT - 8 : EXT] = zeros

        @pl.when(lat == 0)
        def _():
            ext[:, 8:16] = zeros
            rim_e[8:16] = zeros[0]
            rim_w[8:16] = zeros[0]
            for b in range(BLOCKS - 1):
                fill(b, b + 2)

        @pl.when(lat > 0)
        def _():
            ext[:, EXT - 16 : EXT - 8] = zeros
            rim_e[EXT - 16 : EXT - 8] = zeros[0]
            rim_w[EXT - 16 : EXT - 8] = zeros[0]
            for b in range(1, BLOCKS):
                fill(b, b + 2)

        rim_src[...] = jnp.zeros((EXT, LANES), F32)
        rim_src[HALO : HALO + ROWS] = plus_face(0, slice(HALO, HALO + ROWS))

        cut_load.wait()
        row = iota((8, LANES), 0)
        open_cut = jnp.full((8, LANES), float(NLON // 2), F32)
        cuts = [open_cut, open_cut]
        for b in range(BLOCKS):
            tile = open_cut
            for j in range(8):
                tile = jnp.where(row == j, cutoff[8 * b + j].astype(F32), tile)
            cuts.append(tile)
        cuts += [open_cut, open_cut]
        for b in range(BLOCKS):
            cut_src[b, 0] = cuts[b + 2]
            cut_src[b, 1] = jnp.where(row < EDGE, cuts[b + 3], cuts[b + 1])
        cut_src[BLOCKS, 0] = open_cut
        low_half = jnp.where(first_band, open_cut, cuts[2])
        high_half = jnp.where(first_band, cuts[BLOCKS + 1], open_cut)
        cut_src[BLOCKS, 1] = jnp.where(row < EDGE, low_half, high_half)

    peers = jnp.where(polar, 3 + 9 * PAIRS, 4)
    peers = peers + jnp.where(is_owner, TILES + COLS - 1, 0)
    pl.semaphore_wait(barrier, peers)

    low_rows = ext.at[:, pl.ds(HALO, 8)]
    high_rows = ext.at[:, pl.ds(HALO + ROWS - 8, 8)]
    south_rows = ext.at[:, pl.ds(HALO - 8, 8)]
    north_rows = ext.at[:, pl.ds(HALO + ROWS, 8)]
    to_south = remote(low_rows, north_rows, row_send.at[0], row_recv.at[0], lat - 1, lon)
    to_north = remote(high_rows, south_rows, row_send.at[1], row_recv.at[1], lat + 1, lon)

    @pl.when(lat > 0)
    def _():
        to_south.start()

    @pl.when(lat < LATS - 1)
    def _():
        to_north.start()

    def wait_rows():
        @pl.when(lat < LATS - 1)
        def _():
            to_south.wait_recv()

        @pl.when(lat > 0)
        def _():
            to_north.wait_recv()

    @pl.when(polar)
    def _():
        extra = pl.ds(pl.multiple_of(jnp.where(lat == 0, HALO + ROWS, HALO - 8), 8), 8)
        rims = [
            remote(ext.at[MASK, main], rim_e.at[main], col_send.at[0], col_recv.at[0], lat, left),
            remote(rim_src.at[main], rim_w.at[main], col_send.at[1], col_recv.at[1], lat, right),
            remote(ext.at[MASK, extra], rim_e.at[extra], col_send.at[2], col_recv.at[2], lat, left),
            remote(rim_src.at[extra], rim_w.at[extra], col_send.at[3], col_recv.at[3], lat, right),
        ]
        rims[0].start()
        rims[1].start()
        pltpu.make_async_remote_copy(
            src_ref=cut_src.at[z], dst_ref=cuts_ref, send_sem=cut_send.at[0],
            recv_sem=cut_recv.at[0], device_id=at(beside_lat, lon),
            device_id_type=pl.DeviceIdType.MESH,
        ).start()

        @pl.when(z == LAST_RING)
        def _():
            remote(
                cut_src.at[BLOCKS], cuts_ref, cut_send.at[1], cut_recv.at[0], last_lat, lon
            ).start()

        def send_block(b):
            for p in range(PAIRS):
                remote(
                    lam_src.at[b, pl.ds(2 * p, 2)], lam.at[lon], in_send.at[0], in_recv.at[0],
                    *owner_of(b, p),
                ).start()

        def send_free(t):
            send_block(lax.rem(z + 4 + t, BLOCKS - 1) + jnp.where(lat == 0, 0, 1))

        def send_some(first, count):
            over(count, lambda t: send_free(first + t))

        send_some(0, 2)
        wait_rows()

        @pl.when(lat == 0)
        def _():
            rim_src[HALO + ROWS : HALO + ROWS + 8] = plus_face(
                0, slice(HALO + ROWS, HALO + ROWS + 8)
            )

        @pl.when(lat > 0)
        def _():
            rim_src[HALO - 8 : HALO] = plus_face(0, slice(HALO - 8, HALO))

        rims[2].start()
        rims[3].start()
        send_some(2, 2)

        @pl.when(lat == 0)
        def _():
            fill(BLOCKS - 1, BLOCKS + 1)
            fill(BLOCKS, BLOCKS + 2)

        @pl.when(lat > 0)
        def _():
            fill(0, 2)
            fill(BLOCKS, 1)

        for rim in rims:
            rim.wait_recv()
        here = slice(8, 8 + WIDE)
        lane = iota((WIDE, LANES), 1)
        mine = ext[MASK, here]
        mask_east = jnp.where(
            lane == LANES - 1, pltpu.roll(rim_e[here], LANES - 1, 1), pltpu.roll(mine, LANES - 1, 1)
        )
        plus_west = jnp.where(
            lane == 0, pltpu.roll(rim_w[here], 1, 1), pltpu.roll(rim_src[here], 1, 1)
        )
        faces = (
            minus_face(0, here) * mask_east,
            -mine * plus_west,
            minus_face(2, here) * ext[MASK, 9 : 9 + WIDE],
            -mine * plus_face(2, slice(7, 7 + WIDE)),
        )
        low = iota((8, LANES), 0) < EDGE
        for k in range(4):
            face = faces[k].reshape(WIDE // 8, 8, LANES)
            coef_src[0:BLOCKS, k, 0] = face[1:9]
            coef_src[0:BLOCKS, k, 1] = jnp.where(low[None], face[2:10], face[0:8])

            @pl.when(lat == 0)
            def _():
                coef_src[BLOCKS, k, 0] = face[9]
                coef_src[BLOCKS, k, 1] = jnp.where(low, 0.0, face[8])

            @pl.when(lat > 0)
            def _():
                coef_src[BLOCKS, k, 0] = face[0]
                coef_src[BLOCKS, k, 1] = jnp.where(low, face[1], 0.0)

        def send_coef(t):
            b = lax.rem(z + 4 + t, BLOCKS + 1)
            remote(
                coef_src.at[b], coef.at[y, z], cf_send.at[0], cf_recv.at[z], *owner_of(b, y)
            ).start()

        over(BLOCKS + 1, send_coef)
        send_some(4, BLOCKS - 5)
        send_block(jnp.where(lat == 0, BLOCKS - 1, 0))
        send_block(jnp.int32(BLOCKS))

        for rim in rims:
            rim.wait_send()
        wait_bytes(cuts_ref, cut_send.at[0])

        @pl.when(z == LAST_RING)
        def _():
            wait_bytes(cuts_ref, cut_send.at[1])

        wait_bytes(lam_src, in_send.at[0])
        wait_bytes(coef_src, cf_send.at[0])
        wait_bytes(out, out_recv.at[0])

    @pl.when(jnp.logical_not(polar))
    def _():
        wait_rows()
        here = slice(8, 8 + WIDE)
        lane = iota((WIDE, LANES), 1)
        total = jnp.zeros((WIDE, LANES), F32)
        for p in range(PLANES):
            v = ext[p, here]
            u = jnp.where(lane < EDGE, v, pltpu.roll(v, 2 * EDGE, 1))
            if p:
                u = pltpu.roll(u, 8 * p, 1)
            total = jnp.where((lane // 8) == p, u, total)
        packed[...] = total
        to_left = remote(packed, packed_r, col_send.at[0], col_recv.at[0], lat, left)
        to_right = remote(packed, packed_l, col_send.at[1], col_recv.at[1], lat, right)
        to_left.start()
        to_right.start()
        @pl.when(is_owner)
        def _():
            def hand_on(t):
                ring = lax.rem(z + t, RINGS)
                wait_bytes(coef.at[y, ring], cf_recv.at[ring])
                for c in range(1, COLS):
                    remote(
                        coef.at[y, ring], coef.at[y, ring], pass_send.at[0], pass_recv.at[0],
                        lat, COLS * z + lax.rem(y + c, COLS),
                    ).start()

            over(RINGS, hand_on)

        to_left.wait_recv()
        to_right.wait_recv()

        def beyond(p):
            from_right = packed_r[...]
            if p:
                from_right = pltpu.roll(from_right, LANES - 8 * p, 1)
            from_left = pltpu.roll(packed_l[...], (LANES - 8 - 8 * p) % LANES, 1)
            return jnp.where(lane < LANES // 2, from_right, from_left)

        def east_of(x):
            near, far = (pltpu.roll(v, LANES - 1, 1) for v in x)
            last = lane == LANES - 1
            return jnp.where(last, far, near), jnp.where(last, near, far)

        def west_of(x):
            near, far = (pltpu.roll(v, 1, 1) for v in x)
            last = lane == 0
            return jnp.where(last, far, near), jnp.where(last, near, far)

        def north_of(x):
            return [pltpu.roll(v, WIDE - 1, 0) for v in x]

        def south_of(x):
            return [pltpu.roll(v, 1, 0) for v in x]

        kappa_e, speed_e, kappa_n, speed_n, open_m = (
            (ext[LEVELS + k, here], beyond(LEVELS + k)) for k in range(5)
        )

        def minus(kappa, speed):
            return [m * (-k - 0.5 * f) for m, k, f in zip(open_m, kappa, speed)]

        def plus(kappa, speed):
            return [m * (k - 0.5 * f) for m, k, f in zip(open_m, kappa, speed)]

        faces = (
            [a * b for a, b in zip(minus(kappa_e, speed_e), east_of(open_m))],
            [-a * b for a, b in zip(open_m, west_of(plus(kappa_e, speed_e)))],
            [a * b for a, b in zip(minus(kappa_n, speed_n), north_of(open_m))],
            [-a * b for a, b in zip(open_m, south_of(plus(kappa_n, speed_n)))],
        )
        for k in range(4):
            for side in range(2):
                wide_coef[k, side] = faces[k][side]

        def level(p):
            from_right = pltpu.roll(packed_r[...], LANES - 8 * p, 1)
            from_left = pltpu.roll(packed_l[...], LANES - 8 - 8 * p, 1)
            x = (ext[p, here], jnp.where(lane < LANES // 2, from_right, from_left))
            for _ in range(STEPS):
                new = list(x)
                for k, near in enumerate((east_of(x), west_of(x), north_of(x), south_of(x))):
                    for side in range(2):
                        new[side] = new[side] + wide_coef[k, side] * (x[side] - near[side])
                x = tuple(new)
            mid_out[p] = x[0][8 : 8 + ROWS]

        over(LEVELS, level)

        kept = pl.ds(pl.multiple_of(jnp.where(first_band, 8, 0), 8), ROWS - 8)
        shared = pl.ds(pl.multiple_of(jnp.where(first_band, 0, ROWS - 8), 8), 8)
        store_kept = pltpu.make_async_copy(mid_out.at[:, kept], out.at[:, kept], store_sem.at[0])
        store_shared = pltpu.make_async_copy(
            mid_out.at[:, shared], out.at[:, shared], store_sem.at[1]
        )
        store_kept.start()

        @pl.when(jnp.logical_not(beside))
        def _():
            store_shared.start()

        @pl.when(is_owner)
        def _():
            for load in table_loads:
                load.wait()
            high = wide_ref[...].astype(jnp.bfloat16)
            high_ref[...] = high
            low_ref[...] = (wide_ref[...] - high.astype(F32)).astype(jnp.bfloat16)
            wait_bytes(cuts_ref, cut_recv.at[0])
            cuts = cuts_ref[...].astype(jnp.int32)
            wait_bytes(lam, in_recv.at[0])

            def step(s):
                for half in range(2):
                    real, imag = filter_circles(
                        lam[:, 0, half], lam[:, 1, half], cuts[half], high_ref, low_ref, turn_ref
                    )
                    fil[:, 0, half] = real
                    fil[:, 1, half] = imag

                @pl.when(s == 0)
                def _():
                    wait_bytes(coef.at[pl.ds(0, COLS - 1)], pass_recv.at[0])

                lam[...] = circle_step(fil[...], coef)

            over(STEPS, step)

            my_levels = pl.ds(2 * pair, 2)

            @pl.when(jnp.logical_not(last_block))
            def _():
                rows = pl.ds(pl.multiple_of(8 * jnp.minimum(block, BLOCKS - 1), 8), 8)

                def send_out(t):
                    tile = lax.rem(lon + TILES // 2 + t, TILES)
                    remote(
                        lam.at[tile, :, 0], out.at[my_levels, rows], out_send.at[0],
                        out_recv.at[0], polar_lat, tile,
                    ).start()

                over(TILES, send_out)

            @pl.when(last_block)
            def _():
                def send_x(t):
                    tile = lax.rem(lon + TILES // 2 + t, TILES)
                    remote(
                        lam.at[tile, :, 0], row_x.at[my_levels], out_send.at[0], ox_recv.at[0],
                        beside_lat, tile,
                    ).start()

                over(TILES, send_x)

            wait_bytes(coef.at[pl.ds(0, COLS - 1)], pass_send.at[0])
            wait_bytes(lam.at[:, :, 0], out_send.at[0])

        to_left.wait_send()
        to_right.wait_send()

        @pl.when(beside)
        def _():
            wait_bytes(row_x, ox_recv.at[0])

            @pl.when(lat == 1)
            def _():
                mid_out[:, 0:8] = jnp.where(sub < EDGE, row_x[...], mid_out[:, 0:8])

            @pl.when(lat > 1)
            def _():
                mid_out[:, ROWS - 8 : ROWS] = jnp.where(
                    sub < EDGE, mid_out[:, ROWS - 8 : ROWS], row_x[...]
                )

            store_shared.start()

        store_kept.wait()
        store_shared.wait()

    @pl.when(lat > 0)
    def _():
        to_south.wait_send()

    @pl.when(lat < LATS - 1)
    def _():
        to_north.wait_send()


def shards(cotangent, diff_east, diff_north, flow_east, flow_north, sea_mask, cutoff):
    wide, turn = tables()
    hbm = pl.BlockSpec(memory_space=pltpu.HBM)
    dma = pltpu.SemaphoreType.DMA

    def room(*shape):
        return pltpu.VMEM(shape, F32)

    table = pltpu.VMEM((2 * LANES, 2 * LANES), jnp.bfloat16)
    return pl.pallas_call(
        kernel,
        out_shape=jax.ShapeDtypeStruct((LEVELS, ROWS, LANES), F32),
        in_specs=[hbm] * 9,
        out_specs=hbm,
        scratch_shapes=[
            pltpu.VMEM((ROWS, LANES), jnp.int32),
            pltpu.SMEM((ROWS,), jnp.int32),
            room(2 * LANES, 2 * LANES),
            table,
            table,
            room(72, 8, LANES),
            room(PLANES, EXT, LANES),
            room(BLOCKS + 1, LEVELS, 2, 8, LANES),
            room(BLOCKS + 1, 4, 2, 8, LANES),
            room(BLOCKS + 1, 2, 8, LANES),
            room(EXT, LANES),
            room(EXT, LANES),
            room(EXT, LANES),
            room(TILES, 2, 2, 8, LANES),
            room(TILES, 2, 2, 8, LANES),
            room(COLS, RINGS, 4, 2, 8, LANES),
            room(2, 8, LANES),
            room(LEVELS, 8, LANES),
            room(WIDE, LANES),
            room(WIDE, LANES),
            room(WIDE, LANES),
            room(4, 2, WIDE, LANES),
            room(LEVELS, ROWS, LANES),
            dma((9,)),
            dma((2,)), dma((2,)), dma((4,)), dma((4,)), dma((2,)), dma((1,)), dma((1,)), dma((1,)),
            dma((1,)), dma((RINGS,)), dma((1,)), dma((1,)), dma((1,)), dma((1,)), dma((1,)), dma((2,)),
        ],
        compiler_params=pltpu.CompilerParams(
            collective_id=0, has_side_effects=True, vmem_limit_bytes=63 * 1024 * 1024
        ),
    )(
        cotangent, diff_east, diff_north, flow_east, flow_north, sea_mask, cutoff,
        jnp.asarray(wide), jnp.asarray(turn),
    )


def solution(mesh):
    return jax.shard_map(
        shards,
        mesh=mesh,
        in_specs=(
            P(None, "lat", "lon"),
            P("lat", "lon"),
            P("lat", "lon"),
            P("lat", "lon"),
            P("lat", "lon"),
            P("lat", "lon"),
            P("lat"),
        ),
        out_specs=P(None, "lat", "lon"),
        check_vma=False,
    )
```

```python
import functools
import math

import jax
import jax.numpy as jnp
import numpy as np
from jax import lax
from jax.experimental import pallas as pl
from jax.experimental.pallas import tpu as pltpu
from jax.sharding import PartitionSpec as P

STEPS = 4
LEVELS = 8
ROWS = 64
LANES = 128
TILES = 32
NLON = TILES * LANES
BLOCKS = 8
PAIRS = 4
HALO = 16
EXT = ROWS + 2 * HALO
WIDE = ROWS + HALO
PLANES = LEVELS + 5
MASK = LEVELS + 4
EDGE = 4
LATS = 8
COLS = 4
RINGS = 8
LAST_RING = 4
EARLY = 3

F32 = jnp.float32


def tables():
    n = np.arange(LANES)
    angle = 2 * np.pi * (np.outer(n, n) % LANES) / LANES
    cos, sin = np.cos(angle), np.sin(angle)
    wide = np.block([[cos, -sin], [sin, cos]])
    q = np.arange(8)[:, None, None]
    c = np.arange(4)[None, :, None]
    first = 2 * np.pi * ((q * (n[None, None, :] + LANES * c)) % NLON) / NLON
    r = np.arange(4)[:, None]
    second = 2 * np.pi * ((r * n[None, :]) % 512) / 512

    def spread(values):
        values = values.reshape(-1, 1, LANES)
        return np.broadcast_to(values, (values.shape[0], 8, LANES)).astype(np.float32)

    turn = np.concatenate(
        [spread(np.cos(first)), spread(np.sin(first)), spread(np.cos(second)), spread(np.sin(second))]
    )
    return wide.astype(np.float32), turn


def cadd(x, y):
    return x[0] + y[0], x[1] + y[1]


def csub(x, y):
    return x[0] - y[0], x[1] - y[1]


def quarter(x, sign):
    if sign < 0:
        return x[1], -x[0]
    return -x[1], x[0]


def dft4(x, sign):
    even, odd = cadd(x[0], x[2]), csub(x[0], x[2])
    even2, odd2 = cadd(x[1], x[3]), quarter(csub(x[1], x[3]), sign)
    return [cadd(even, even2), cadd(odd, odd2), csub(even, even2), csub(odd, odd2)]


def dft8(x, sign):
    even = dft4([x[0], x[2], x[4], x[6]], sign)
    odd = dft4([x[1], x[3], x[5], x[7]], sign)
    half = math.sqrt(0.5)

    def eighth(v):
        rot = quarter(v, sign)
        return (v[0] + rot[0]) * half, (v[1] + rot[1]) * half

    odd[1] = eighth(odd[1])
    odd[2] = quarter(odd[2], sign)
    odd[3] = quarter(eighth(odd[3]), sign)
    return [cadd(e, o) for e, o in zip(even, odd)] + [csub(e, o) for e, o in zip(even, odd)]


def cmul(x, cos, sin, sign):
    if sign < 0:
        return x[0] * cos + x[1] * sin, x[1] * cos - x[0] * sin
    return x[0] * cos - x[1] * sin, x[1] * cos + x[0] * sin


def split_dot(left, high_ref, low_ref):
    high = left.astype(jnp.bfloat16)
    low = (left - high.astype(F32)).astype(jnp.bfloat16)
    dot = functools.partial(jnp.dot, preferred_element_type=F32)
    return dot(high, high_ref[...]) + (dot(low, high_ref[...]) + dot(high, low_ref[...]))


def filter_circles(real, imag, cuts, high_ref, low_ref, turn_ref):
    shape = (8, 4, 8, LANES)
    cos1 = turn_ref[0:32].reshape(shape)
    sin1 = turn_ref[32:64].reshape(shape)
    real, imag = real.reshape(shape), imag.reshape(shape)
    parts = dft8([(real[a], imag[a]) for a in range(8)], -1)
    parts = [cmul(parts[q], cos1[q], sin1[q], -1) for q in range(8)]
    real = jnp.stack([p[0] for p in parts])
    imag = jnp.stack([p[1] for p in parts])
    parts = dft4([(real[:, c], imag[:, c]) for c in range(4)], -1)
    parts = [parts[0]] + [
        cmul(parts[r], turn_ref[64 + r], turn_ref[68 + r], -1) for r in range(1, 4)
    ]
    real = jnp.concatenate([p[0] for p in parts]).reshape(256, LANES)
    imag = jnp.concatenate([p[1] for p in parts]).reshape(256, LANES)
    spec = split_dot(jnp.concatenate([real, imag], axis=1), high_ref, low_ref)
    wave = lax.broadcasted_iota(jnp.int32, (TILES, 8, LANES), 0) + TILES * lax.broadcasted_iota(
        jnp.int32, (TILES, 8, LANES), 2
    )
    wave = jnp.minimum(wave, NLON - wave)
    kept = jnp.where(wave <= cuts[None], 1.0 / NLON, 0.0).astype(F32).reshape(256, LANES)
    real = spec[:, :LANES] * kept
    imag = spec[:, LANES:] * kept
    back = split_dot(jnp.concatenate([imag, real], axis=1), high_ref, low_ref)
    real = back[:, LANES:].reshape(4, 8, 8, LANES)
    imag = back[:, :LANES].reshape(4, 8, 8, LANES)
    parts = [(real[0], imag[0])] + [
        cmul((real[r], imag[r]), turn_ref[64 + r], turn_ref[68 + r], 1) for r in range(1, 4)
    ]
    parts = dft4(parts, 1)
    real = jnp.stack([p[0] for p in parts], axis=1)
    imag = jnp.stack([p[1] for p in parts], axis=1)
    parts = [cmul((real[q], imag[q]), cos1[q], sin1[q], 1) for q in range(8)]
    parts = dft8(parts, 1)
    real = jnp.concatenate([p[0] for p in parts])
    imag = jnp.concatenate([p[1] for p in parts])
    return real, imag


def iota(shape, dim):
    return lax.broadcasted_iota(jnp.int32, shape, dim)


def circle_step(x, coef):
    shape = (TILES * 4, 8, LANES)
    full = (TILES, 2, 2, 8, LANES)
    lane = iota(shape, 2)
    row = iota(full, 3)
    flat = x.reshape(shape)
    east = pltpu.roll(flat, LANES - 1, 2)
    east = jnp.where(lane == LANES - 1, jnp.concatenate([east[4:], east[:4]]), east)
    west = pltpu.roll(flat, 1, 2)
    west = jnp.where(lane == 0, jnp.concatenate([west[-4:], west[:-4]]), west)

    def across(turned, edge):
        turned = turned.reshape(full)
        other = jnp.stack([turned[:, :, 1], turned[:, :, 0]], axis=2)
        return jnp.where(row == edge, other, turned)

    up = across(pltpu.roll(flat, 7, 1), 7)
    down = across(pltpu.roll(flat, 1, 1), 0)
    total = x
    for k, near in enumerate((east.reshape(full), west.reshape(full), up, down)):
        face = jnp.stack([coef[c, :, k] for c in range(COLS)], axis=1).reshape(TILES, 1, 2, 8, LANES)
        total = total + face * (x - near)
    return total


def kernel(
    cot, diff_east_in, diff_north_in, flow_east_in, flow_north_in, sea_in, cutoff_in, wide_in,
    turn_in,
    out, row_x,
    sea, cutoff, wide_ref, high_ref, low_ref, turn_ref,
    ext, lam_src, coef_src, cut_src, rim_e, rim_w, rim_src,
    lam, fil, coef, cuts_ref, packed, packed_l, packed_r, wide_coef, mid_out,
    load_sem, row_send, row_recv, col_send, col_recv, cut_send, cut_recv, in_send, in_recv,
    cf_send, cf_recv, pass_send, pass_recv, out_send, out_recv, ox_recv, store_sem,
):
    lon = lax.axis_index("lon")
    lat = lax.axis_index("lat")
    y = lax.rem(lon, 4)
    z = lon // 4
    first_band = lat < LATS // 2
    polar = jnp.logical_or(lat == 0, lat == LATS - 1)
    beside = jnp.logical_or(lat == 1, lat == LATS - 2)
    polar_lat = jnp.where(first_band, 0, LATS - 1)
    beside_lat = jnp.where(first_band, 1, LATS - 2)
    last_lat = jnp.where(first_band, 2, LATS - 3)
    last_block = jnp.logical_and(lat == last_lat, z == LAST_RING)
    is_owner = jnp.logical_or(beside, last_block)
    block = jnp.where(beside, z, BLOCKS)
    pair = y

    def owner_of(b, p):
        to_lat = jnp.where(b == BLOCKS, last_lat, beside_lat)
        return to_lat, COLS * jnp.where(b == BLOCKS, LAST_RING, b) + p

    main = pl.ds(HALO, ROWS)
    plane_loads = [
        pltpu.make_async_copy(src, dst, load_sem.at[k])
        for k, (src, dst) in enumerate(
            (
                (sea_in, sea),
                (diff_east_in, ext.at[LEVELS, main]),
                (flow_east_in, ext.at[LEVELS + 1, main]),
                (diff_north_in, ext.at[LEVELS + 2, main]),
                (flow_north_in, ext.at[LEVELS + 3, main]),
                (cot, ext.at[pl.ds(0, LEVELS), main]),
            )
        )
    ]
    cut_load = pltpu.make_async_copy(cutoff_in, cutoff, load_sem.at[6])
    table_loads = [
        pltpu.make_async_copy(turn_in, turn_ref, load_sem.at[7]),
        pltpu.make_async_copy(wide_in, wide_ref, load_sem.at[8]),
    ]
    for load in plane_loads:
        load.start()

    @pl.when(polar)
    def _():
        cut_load.start()

    @pl.when(is_owner)
    def _():
        for load in table_loads:
            load.start()

    barrier = pltpu.get_barrier_semaphore()

    def at(to_lat, to_lon):
        return {"lon": to_lon, "lat": to_lat}

    def hail(to_lat, to_lon):
        pl.semaphore_signal(
            barrier, inc=1, device_id=at(to_lat, to_lon), device_id_type=pl.DeviceIdType.MESH
        )

    def remote(src, dst, send, recv, to_lat, to_lon):
        return pltpu.make_async_remote_copy(
            src_ref=src, dst_ref=dst, send_sem=send, recv_sem=recv,
            device_id=at(to_lat, to_lon), device_id_type=pl.DeviceIdType.MESH,
        )

    def wait_bytes(ref, sem):
        pltpu.make_async_copy(ref, ref, sem).wait()

    def over(count, body):
        def go(k, carry):
            body(k)
            return carry

        lax.fori_loop(0, count, go, 0)

    def far_first(i):
        return lax.rem(z + 4 + ((i + 1) // 2) * (1 - 2 * lax.rem(i, 2)), RINGS)

    right = lax.rem(lon + 1, TILES)
    left = lax.rem(lon + TILES - 1, TILES)

    @pl.when(polar)
    def _():
        def greet(i):
            b = far_first(i)
            for p in range(PAIRS):
                hail(*owner_of(b, p))

        over(BLOCKS, greet)

    @pl.when(is_owner)
    def _():
        def greet(i):
            for c in range(COLS):
                hail(polar_lat, COLS * far_first(i) + lax.rem(y + c, COLS))

        over(RINGS, greet)
        for c in range(1, COLS):
            hail(lat, COLS * z + lax.rem(y + c, COLS))

    @pl.when(beside)
    def _():
        for p in range(PAIRS):
            hail(*owner_of(BLOCKS, p))

    hail(lat, left)
    hail(lat, right)

    @pl.when(lat > 0)
    def _():
        hail(lat - 1, lon)

    @pl.when(lat < LATS - 1)
    def _():
        hail(lat + 1, lon)

    for load in plane_loads:
        load.wait()
    ext[MASK, HALO : HALO + ROWS] = sea[...].astype(F32)
    sub = iota((LEVELS, 8, LANES), 1)

    def fill(b, tile):
        rows = 8 * tile
        lam_src[b, :, 0] = ext[0:LEVELS, rows : rows + 8]
        lam_src[b, :, 1] = jnp.where(
            sub < EDGE, ext[0:LEVELS, rows + 8 : rows + 16], ext[0:LEVELS, rows - 8 : rows]
        )

    def plus_face(kappa, rows):
        return ext[MASK, rows] * (ext[LEVELS + kappa, rows] - 0.5 * ext[LEVELS + kappa + 1, rows])

    def minus_face(kappa, rows):
        return -ext[MASK, rows] * (ext[LEVELS + kappa, rows] + 0.5 * ext[LEVELS + kappa + 1, rows])

    @pl.when(polar)
    def _():
        zeros = jnp.zeros((PLANES, 8, LANES), F32)
        ext[:, 0:8] = zeros
        ext[:, EXT - 8 : EXT] = zeros

        @pl.when(lat == 0)
        def _():
            ext[:, 8:16] = zeros
            rim_e[8:16] = zeros[0]
            rim_w[8:16] = zeros[0]
            for b in range(BLOCKS - 1):
                fill(b, b + 2)

        @pl.when(lat > 0)
        def _():
            ext[:, EXT - 16 : EXT - 8] = zeros
            rim_e[EXT - 16 : EXT - 8] = zeros[0]
            rim_w[EXT - 16 : EXT - 8] = zeros[0]
            for b in range(1, BLOCKS):
                fill(b, b + 2)

        rim_src[...] = jnp.zeros((EXT, LANES), F32)
        rim_src[HALO : HALO + ROWS] = plus_face(0, slice(HALO, HALO + ROWS))

        cut_load.wait()
        row = iota((8, LANES), 0)
        open_cut = jnp.full((8, LANES), float(NLON // 2), F32)
        cuts = [open_cut, open_cut]
        for b in range(BLOCKS):
            tile = open_cut
            for j in range(8):
                tile = jnp.where(row == j, cutoff[8 * b + j].astype(F32), tile)
            cuts.append(tile)
        cuts += [open_cut, open_cut]
        for b in range(BLOCKS):
            cut_src[b, 0] = cuts[b + 2]
            cut_src[b, 1] = jnp.where(row < EDGE, cuts[b + 3], cuts[b + 1])
        cut_src[BLOCKS, 0] = open_cut
        low_half = jnp.where(first_band, open_cut, cuts[2])
        high_half = jnp.where(first_band, cuts[BLOCKS + 1], open_cut)
        cut_src[BLOCKS, 1] = jnp.where(row < EDGE, low_half, high_half)

    peers = jnp.where(polar, 3 + 9 * PAIRS, 4)
    peers = peers + jnp.where(is_owner, TILES + COLS - 1, 0)
    pl.semaphore_wait(barrier, peers)

    low_rows = ext.at[:, pl.ds(HALO, 8)]
    high_rows = ext.at[:, pl.ds(HALO + ROWS - 8, 8)]
    south_rows = ext.at[:, pl.ds(HALO - 8, 8)]
    north_rows = ext.at[:, pl.ds(HALO + ROWS, 8)]
    to_south = remote(low_rows, north_rows, row_send.at[0], row_recv.at[0], lat - 1, lon)
    to_north = remote(high_rows, south_rows, row_send.at[1], row_recv.at[1], lat + 1, lon)

    @pl.when(lat > 0)
    def _():
        to_south.start()

    @pl.when(lat < LATS - 1)
    def _():
        to_north.start()

    def wait_rows():
        @pl.when(lat < LATS - 1)
        def _():
            to_south.wait_recv()

        @pl.when(lat > 0)
        def _():
            to_north.wait_recv()

    @pl.when(polar)
    def _():
        extra = pl.ds(pl.multiple_of(jnp.where(lat == 0, HALO + ROWS, HALO - 8), 8), 8)
        rims = [
            remote(ext.at[MASK, main], rim_e.at[main], col_send.at[0], col_recv.at[0], lat, left),
            remote(rim_src.at[main], rim_w.at[main], col_send.at[1], col_recv.at[1], lat, right),
            remote(ext.at[MASK, extra], rim_e.at[extra], col_send.at[2], col_recv.at[2], lat, left),
            remote(rim_src.at[extra], rim_w.at[extra], col_send.at[3], col_recv.at[3], lat, right),
        ]
        rims[0].start()
        rims[1].start()
        pltpu.make_async_remote_copy(
            src_ref=cut_src.at[z], dst_ref=cuts_ref, send_sem=cut_send.at[0],
            recv_sem=cut_recv.at[0], device_id=at(beside_lat, lon),
            device_id_type=pl.DeviceIdType.MESH,
        ).start()

        @pl.when(z == LAST_RING)
        def _():
            remote(
                cut_src.at[BLOCKS], cuts_ref, cut_send.at[1], cut_recv.at[0], last_lat, lon
            ).start()

        def send_block(b):
            for p in range(PAIRS):
                remote(
                    lam_src.at[b, pl.ds(2 * p, 2)], lam.at[lon], in_send.at[0], in_recv.at[0],
                    *owner_of(b, p),
                ).start()

        edge = jnp.where(lat == 0, BLOCKS - 1, 0)

        def send_early(i):
            @pl.when(far_first(i) != edge)
            def _():
                send_block(far_first(i))

        def send_skipped(i):
            @pl.when(far_first(i) == edge)
            def _():
                send_block(edge)

        over(EARLY, send_early)
        wait_rows()

        @pl.when(lat == 0)
        def _():
            rim_src[HALO + ROWS : HALO + ROWS + 8] = plus_face(
                0, slice(HALO + ROWS, HALO + ROWS + 8)
            )

        @pl.when(lat > 0)
        def _():
            rim_src[HALO - 8 : HALO] = plus_face(0, slice(HALO - 8, HALO))

        rims[2].start()
        rims[3].start()

        @pl.when(lat == 0)
        def _():
            fill(BLOCKS - 1, BLOCKS + 1)
            fill(BLOCKS, BLOCKS + 2)

        @pl.when(lat > 0)
        def _():
            fill(0, 2)
            fill(BLOCKS, 1)

        over(EARLY, send_skipped)
        send_block(jnp.int32(BLOCKS))
        over(2, lambda i: send_block(far_first(EARLY + i)))
        for rim in rims:
            rim.wait_recv()
        here = slice(8, 8 + WIDE)
        lane = iota((WIDE, LANES), 1)
        mine = ext[MASK, here]
        mask_east = jnp.where(
            lane == LANES - 1, pltpu.roll(rim_e[here], LANES - 1, 1), pltpu.roll(mine, LANES - 1, 1)
        )
        plus_west = jnp.where(
            lane == 0, pltpu.roll(rim_w[here], 1, 1), pltpu.roll(rim_src[here], 1, 1)
        )
        faces = (
            minus_face(0, here) * mask_east,
            -mine * plus_west,
            minus_face(2, here) * ext[MASK, 9 : 9 + WIDE],
            -mine * plus_face(2, slice(7, 7 + WIDE)),
        )
        low = iota((8, LANES), 0) < EDGE
        for k in range(4):
            face = faces[k].reshape(WIDE // 8, 8, LANES)
            coef_src[0:BLOCKS, k, 0] = face[1:9]
            coef_src[0:BLOCKS, k, 1] = jnp.where(low[None], face[2:10], face[0:8])

            @pl.when(lat == 0)
            def _():
                coef_src[BLOCKS, k, 0] = face[9]
                coef_src[BLOCKS, k, 1] = jnp.where(low, 0.0, face[8])

            @pl.when(lat > 0)
            def _():
                coef_src[BLOCKS, k, 0] = face[0]
                coef_src[BLOCKS, k, 1] = jnp.where(low, face[1], 0.0)

        def send_coef(b):
            remote(
                coef_src.at[b], coef.at[y, z], cf_send.at[0], cf_recv.at[z], *owner_of(b, y)
            ).start()

        send_coef(jnp.int32(BLOCKS))
        over(RINGS, lambda i: send_coef(far_first(i)))
        over(RINGS - EARLY - 2, lambda i: send_block(far_first(EARLY + 2 + i)))

        for rim in rims:
            rim.wait_send()
        wait_bytes(cuts_ref, cut_send.at[0])

        @pl.when(z == LAST_RING)
        def _():
            wait_bytes(cuts_ref, cut_send.at[1])

        wait_bytes(lam_src, in_send.at[0])
        wait_bytes(coef_src, cf_send.at[0])
        wait_bytes(out, out_recv.at[0])

    @pl.when(jnp.logical_not(polar))
    def _():
        wait_rows()
        here = slice(8, 8 + WIDE)
        lane = iota((WIDE, LANES), 1)
        total = jnp.zeros((WIDE, LANES), F32)
        for p in range(PLANES):
            v = ext[p, here]
            u = jnp.where(lane < EDGE, v, pltpu.roll(v, 2 * EDGE, 1))
            if p:
                u = pltpu.roll(u, 8 * p, 1)
            total = jnp.where((lane // 8) == p, u, total)
        packed[...] = total
        to_left = remote(packed, packed_r, col_send.at[0], col_recv.at[0], lat, left)
        to_right = remote(packed, packed_l, col_send.at[1], col_recv.at[1], lat, right)
        to_left.start()
        to_right.start()
        @pl.when(is_owner)
        def _():
            for load in table_loads:
                load.wait()
            high = wide_ref[...].astype(jnp.bfloat16)
            high_ref[...] = high
            low_ref[...] = (wide_ref[...] - high.astype(F32)).astype(jnp.bfloat16)

            def hand_on(t):
                ring = lax.rem(z + t, RINGS)
                wait_bytes(coef.at[y, ring], cf_recv.at[ring])
                for c in range(1, COLS):
                    remote(
                        coef.at[y, ring], coef.at[y, ring], pass_send.at[0], pass_recv.at[0],
                        lat, COLS * z + lax.rem(y + c, COLS),
                    ).start()

            over(RINGS, hand_on)
            wait_bytes(cuts_ref, cut_recv.at[0])
            cuts = cuts_ref[...].astype(jnp.int32)
            wait_bytes(lam, in_recv.at[0])

            def step(s):
                for half in range(2):
                    real, imag = filter_circles(
                        lam[:, 0, half], lam[:, 1, half], cuts[half], high_ref, low_ref, turn_ref
                    )
                    fil[:, 0, half] = real
                    fil[:, 1, half] = imag

                @pl.when(s == 0)
                def _():
                    wait_bytes(coef.at[pl.ds(0, COLS - 1)], pass_recv.at[0])

                lam[...] = circle_step(fil[...], coef)

            over(STEPS, step)

            my_levels = pl.ds(2 * pair, 2)

            @pl.when(jnp.logical_not(last_block))
            def _():
                rows = pl.ds(pl.multiple_of(8 * jnp.minimum(block, BLOCKS - 1), 8), 8)

                def send_out(i):
                    for c in range(COLS):
                        tile = COLS * far_first(i) + lax.rem(y + c, COLS)
                        remote(
                            lam.at[tile, :, 0], out.at[my_levels, rows], out_send.at[0],
                            out_recv.at[0], polar_lat, tile,
                        ).start()

                over(RINGS, send_out)

            @pl.when(last_block)
            def _():
                def send_x(i):
                    for c in range(COLS):
                        tile = COLS * far_first(i) + lax.rem(y + c, COLS)
                        remote(
                            lam.at[tile, :, 0], row_x.at[my_levels], out_send.at[0], ox_recv.at[0],
                            beside_lat, tile,
                        ).start()

                over(RINGS, send_x)

        to_left.wait_recv()
        to_right.wait_recv()

        def beyond(p):
            from_right = packed_r[...]
            if p:
                from_right = pltpu.roll(from_right, LANES - 8 * p, 1)
            from_left = pltpu.roll(packed_l[...], (LANES - 8 - 8 * p) % LANES, 1)
            return jnp.where(lane < LANES // 2, from_right, from_left)

        def east_of(x):
            near, far = (pltpu.roll(v, LANES - 1, 1) for v in x)
            last = lane == LANES - 1
            return jnp.where(last, far, near), jnp.where(last, near, far)

        def west_of(x):
            near, far = (pltpu.roll(v, 1, 1) for v in x)
            last = lane == 0
            return jnp.where(last, far, near), jnp.where(last, near, far)

        def north_of(x):
            return [pltpu.roll(v, WIDE - 1, 0) for v in x]

        def south_of(x):
            return [pltpu.roll(v, 1, 0) for v in x]

        kappa_e, speed_e, kappa_n, speed_n, open_m = (
            (ext[LEVELS + k, here], beyond(LEVELS + k)) for k in range(5)
        )

        def minus(kappa, speed):
            return [m * (-k - 0.5 * f) for m, k, f in zip(open_m, kappa, speed)]

        def plus(kappa, speed):
            return [m * (k - 0.5 * f) for m, k, f in zip(open_m, kappa, speed)]

        faces = (
            [a * b for a, b in zip(minus(kappa_e, speed_e), east_of(open_m))],
            [-a * b for a, b in zip(open_m, west_of(plus(kappa_e, speed_e)))],
            [a * b for a, b in zip(minus(kappa_n, speed_n), north_of(open_m))],
            [-a * b for a, b in zip(open_m, south_of(plus(kappa_n, speed_n)))],
        )
        for k in range(4):
            for side in range(2):
                wide_coef[k, side] = faces[k][side]

        def level(p):
            from_right = pltpu.roll(packed_r[...], LANES - 8 * p, 1)
            from_left = pltpu.roll(packed_l[...], LANES - 8 - 8 * p, 1)
            x = (ext[p, here], jnp.where(lane < LANES // 2, from_right, from_left))
            for _ in range(STEPS):
                new = list(x)
                for k, near in enumerate((east_of(x), west_of(x), north_of(x), south_of(x))):
                    for side in range(2):
                        new[side] = new[side] + wide_coef[k, side] * (x[side] - near[side])
                x = tuple(new)
            mid_out[p] = x[0][8 : 8 + ROWS]

        over(LEVELS, level)

        store = pltpu.make_async_copy(mid_out, out, store_sem.at[0])
        store.start()

        @pl.when(is_owner)
        def _():
            wait_bytes(coef.at[pl.ds(0, COLS - 1)], pass_send.at[0])
            wait_bytes(lam.at[:, :, 0], out_send.at[0])

        to_left.wait_send()
        to_right.wait_send()

        @pl.when(beside)
        def _():
            wait_bytes(row_x, ox_recv.at[0])

        store.wait()

    @pl.when(lat > 0)
    def _():
        to_south.wait_send()

    @pl.when(lat < LATS - 1)
    def _():
        to_north.wait_send()


def shards(cotangent, diff_east, diff_north, flow_east, flow_north, sea_mask, cutoff):
    wide, turn = tables()
    hbm = pl.BlockSpec(memory_space=pltpu.HBM)
    dma = pltpu.SemaphoreType.DMA

    def room(*shape):
        return pltpu.VMEM(shape, F32)

    table = pltpu.VMEM((2 * LANES, 2 * LANES), jnp.bfloat16)
    field, shared = pl.pallas_call(
        kernel,
        out_shape=[
            jax.ShapeDtypeStruct((LEVELS, ROWS, LANES), F32),
            jax.ShapeDtypeStruct((LEVELS, 8, LANES), F32),
        ],
        in_specs=[hbm] * 9,
        out_specs=[hbm, hbm],
        scratch_shapes=[
            pltpu.VMEM((ROWS, LANES), jnp.int32),
            pltpu.SMEM((ROWS,), jnp.int32),
            room(2 * LANES, 2 * LANES),
            table,
            table,
            room(72, 8, LANES),
            room(PLANES, EXT, LANES),
            room(BLOCKS + 1, LEVELS, 2, 8, LANES),
            room(BLOCKS + 1, 4, 2, 8, LANES),
            room(BLOCKS + 1, 2, 8, LANES),
            room(EXT, LANES),
            room(EXT, LANES),
            room(EXT, LANES),
            room(TILES, 2, 2, 8, LANES),
            room(TILES, 2, 2, 8, LANES),
            room(COLS, RINGS, 4, 2, 8, LANES),
            room(2, 8, LANES),
            room(WIDE, LANES),
            room(WIDE, LANES),
            room(WIDE, LANES),
            room(4, 2, WIDE, LANES),
            room(LEVELS, ROWS, LANES),
            dma((9,)),
            dma((2,)), dma((2,)), dma((4,)), dma((4,)), dma((2,)), dma((1,)), dma((1,)), dma((1,)),
            dma((1,)), dma((RINGS,)), dma((1,)), dma((1,)), dma((1,)), dma((1,)), dma((1,)), dma((1,)),
        ],
        compiler_params=pltpu.CompilerParams(
            collective_id=0, has_side_effects=True, vmem_limit_bytes=63 * 1024 * 1024
        ),
    )(
        cotangent, diff_east, diff_north, flow_east, flow_north, sea_mask, cutoff,
        jnp.asarray(wide), jnp.asarray(turn),
    )
    lat = lax.axis_index("lat")
    row = lax.broadcasted_iota(jnp.int32, field.shape, 1)
    taken = jnp.logical_or(
        jnp.logical_and(lat == 1, row < EDGE), jnp.logical_and(lat == LATS - 2, row >= ROWS - EDGE)
    )
    return jnp.where(taken, jnp.tile(shared, (1, ROWS // 8, 1)), field)


def solution(mesh):
    return jax.shard_map(
        shards,
        mesh=mesh,
        in_specs=(
            P(None, "lat", "lon"),
            P("lat", "lon"),
            P("lat", "lon"),
            P("lat", "lon"),
            P("lat", "lon"),
            P("lat", "lon"),
            P("lat"),
        ),
        out_specs=P(None, "lat", "lon"),
        check_vma=False,
    )
```

```python
import functools
import math

import jax
import jax.numpy as jnp
import numpy as np
from jax import lax
from jax.experimental import pallas as pl
from jax.experimental.pallas import tpu as pltpu
from jax.sharding import PartitionSpec as P

STEPS = 4
LEVELS = 8
ROWS = 64
LANES = 128
TILES = 32
NLON = TILES * LANES
BLOCKS = 8
PAIRS = 4
HALO = 16
EXT = ROWS + 2 * HALO
WIDE = ROWS + HALO
PLANES = LEVELS + 5
MASK = LEVELS + 4
EDGE = 4
LATS = 8
COLS = 4
RINGS = 8
LAST_RING = 4

F32 = jnp.float32


def tables():
    n = np.arange(LANES)
    angle = 2 * np.pi * (np.outer(n, n) % LANES) / LANES
    cos, sin = np.cos(angle), np.sin(angle)
    wide = np.block([[cos, -sin], [sin, cos]])
    q = np.arange(8)[:, None, None]
    c = np.arange(4)[None, :, None]
    first = 2 * np.pi * ((q * (n[None, None, :] + LANES * c)) % NLON) / NLON
    r = np.arange(4)[:, None]
    second = 2 * np.pi * ((r * n[None, :]) % 512) / 512

    def spread(values):
        values = values.reshape(-1, 1, LANES)
        return np.broadcast_to(values, (values.shape[0], 8, LANES)).astype(np.float32)

    turn = np.concatenate(
        [spread(np.cos(first)), spread(np.sin(first)), spread(np.cos(second)), spread(np.sin(second))]
    )
    return wide.astype(np.float32), turn


def cadd(x, y):
    return x[0] + y[0], x[1] + y[1]


def csub(x, y):
    return x[0] - y[0], x[1] - y[1]


def quarter(x, sign):
    if sign < 0:
        return x[1], -x[0]
    return -x[1], x[0]


def dft4(x, sign):
    even, odd = cadd(x[0], x[2]), csub(x[0], x[2])
    even2, odd2 = cadd(x[1], x[3]), quarter(csub(x[1], x[3]), sign)
    return [cadd(even, even2), cadd(odd, odd2), csub(even, even2), csub(odd, odd2)]


def dft8(x, sign):
    even = dft4([x[0], x[2], x[4], x[6]], sign)
    odd = dft4([x[1], x[3], x[5], x[7]], sign)
    half = math.sqrt(0.5)

    def eighth(v):
        rot = quarter(v, sign)
        return (v[0] + rot[0]) * half, (v[1] + rot[1]) * half

    odd[1] = eighth(odd[1])
    odd[2] = quarter(odd[2], sign)
    odd[3] = quarter(eighth(odd[3]), sign)
    return [cadd(e, o) for e, o in zip(even, odd)] + [csub(e, o) for e, o in zip(even, odd)]


def cmul(x, cos, sin, sign):
    if sign < 0:
        return x[0] * cos + x[1] * sin, x[1] * cos - x[0] * sin
    return x[0] * cos - x[1] * sin, x[1] * cos + x[0] * sin


def split_dot(left, high_ref, low_ref):
    high = left.astype(jnp.bfloat16)
    low = (left - high.astype(F32)).astype(jnp.bfloat16)
    dot = functools.partial(jnp.dot, preferred_element_type=F32)
    return dot(high, high_ref[...]) + (dot(low, high_ref[...]) + dot(high, low_ref[...]))


def filter_circles(real, imag, kept, high_ref, low_ref, turn_ref):
    shape = (8, 4, 8, LANES)
    cos1 = turn_ref[0:32].reshape(shape)
    sin1 = turn_ref[32:64].reshape(shape)
    real, imag = real.reshape(shape), imag.reshape(shape)
    parts = dft8([(real[a], imag[a]) for a in range(8)], -1)
    parts = [cmul(parts[q], cos1[q], sin1[q], -1) for q in range(8)]
    real = jnp.stack([p[0] for p in parts])
    imag = jnp.stack([p[1] for p in parts])
    parts = dft4([(real[:, c], imag[:, c]) for c in range(4)], -1)
    parts = [parts[0]] + [
        cmul(parts[r], turn_ref[64 + r], turn_ref[68 + r], -1) for r in range(1, 4)
    ]
    real = jnp.concatenate([p[0] for p in parts]).reshape(256, LANES)
    imag = jnp.concatenate([p[1] for p in parts]).reshape(256, LANES)
    spec = split_dot(jnp.concatenate([real, imag], axis=1), high_ref, low_ref)
    real = spec[:, :LANES] * kept
    imag = spec[:, LANES:] * kept
    back = split_dot(jnp.concatenate([imag, real], axis=1), high_ref, low_ref)
    real = back[:, LANES:].reshape(4, 8, 8, LANES)
    imag = back[:, :LANES].reshape(4, 8, 8, LANES)
    parts = [(real[0], imag[0])] + [
        cmul((real[r], imag[r]), turn_ref[64 + r], turn_ref[68 + r], 1) for r in range(1, 4)
    ]
    parts = dft4(parts, 1)
    real = jnp.stack([p[0] for p in parts], axis=1)
    imag = jnp.stack([p[1] for p in parts], axis=1)
    parts = [cmul((real[q], imag[q]), cos1[q], sin1[q], 1) for q in range(8)]
    parts = dft8(parts, 1)
    real = jnp.concatenate([p[0] for p in parts])
    imag = jnp.concatenate([p[1] for p in parts])
    return real, imag


def iota(shape, dim):
    return lax.broadcasted_iota(jnp.int32, shape, dim)


def circle_step(x, coef):
    shape = (TILES * 4, 8, LANES)
    full = (TILES, 2, 2, 8, LANES)
    lane = iota(shape, 2)
    row = iota(full, 3)
    flat = x.reshape(shape)
    east = pltpu.roll(flat, LANES - 1, 2)
    east = jnp.where(lane == LANES - 1, jnp.concatenate([east[4:], east[:4]]), east)
    west = pltpu.roll(flat, 1, 2)
    west = jnp.where(lane == 0, jnp.concatenate([west[-4:], west[:-4]]), west)

    def across(turned, edge):
        turned = turned.reshape(full)
        other = jnp.stack([turned[:, :, 1], turned[:, :, 0]], axis=2)
        return jnp.where(row == edge, other, turned)

    up = across(pltpu.roll(flat, 7, 1), 7)
    down = across(pltpu.roll(flat, 1, 1), 0)
    total = x
    for k, near in enumerate((east.reshape(full), west.reshape(full), up, down)):
        total = total + coef[:, k : k + 1] * (x - near)
    return total


def neighbour(x, step):
    shape = (TILES * 2, 8, LANES)
    lane = iota(shape, 2)
    turned = pltpu.roll(x.reshape(shape), step % LANES, 2)
    moved = jnp.concatenate([turned[-2 * step :], turned[: -2 * step]])
    edge = 0 if step > 0 else LANES - 1
    return jnp.where(lane == edge, moved, turned).reshape(x.shape)


def kernel(
    cot, diff_east_in, diff_north_in, flow_east_in, flow_north_in, sea_in, cutoff_in, wide_in,
    turn_in,
    out, row_x,
    sea, cutoff, wide_ref, high_ref, low_ref, turn_ref,
    ext, lam_src, coef_src, cut_src,
    lam, fil, coef, faces, kept_ref, cuts_ref, packed, packed_l, packed_r, wide_coef, mid_out,
    load_sem, row_send, row_recv, col_send, col_recv, cut_send, cut_recv, in_send, in_recv,
    cf_send, cf_recv, pass_send, pass_recv, out_send, out_recv, ox_recv, store_sem,
):
    lon = lax.axis_index("lon")
    lat = lax.axis_index("lat")
    y = lax.rem(lon, 4)
    z = lon // 4
    first_band = lat < LATS // 2
    polar = jnp.logical_or(lat == 0, lat == LATS - 1)
    beside = jnp.logical_or(lat == 1, lat == LATS - 2)
    polar_lat = jnp.where(first_band, 0, LATS - 1)
    beside_lat = jnp.where(first_band, 1, LATS - 2)
    last_lat = jnp.where(first_band, 2, LATS - 3)
    last_block = jnp.logical_and(lat == last_lat, z == LAST_RING)
    is_owner = jnp.logical_or(beside, last_block)
    block = jnp.where(beside, z, BLOCKS)
    pair = y

    def owner_of(b, p):
        to_lat = jnp.where(b == BLOCKS, last_lat, beside_lat)
        return to_lat, COLS * jnp.where(b == BLOCKS, LAST_RING, b) + p

    main = pl.ds(HALO, ROWS)
    plane_loads = [
        pltpu.make_async_copy(src, dst, load_sem.at[k])
        for k, (src, dst) in enumerate(
            (
                (sea_in, sea),
                (diff_east_in, ext.at[LEVELS, main]),
                (flow_east_in, ext.at[LEVELS + 1, main]),
                (diff_north_in, ext.at[LEVELS + 2, main]),
                (flow_north_in, ext.at[LEVELS + 3, main]),
                (cot, ext.at[pl.ds(0, LEVELS), main]),
            )
        )
    ]
    cut_load = pltpu.make_async_copy(cutoff_in, cutoff, load_sem.at[6])
    table_loads = [
        pltpu.make_async_copy(turn_in, turn_ref, load_sem.at[7]),
        pltpu.make_async_copy(wide_in, wide_ref, load_sem.at[8]),
    ]
    for load in plane_loads:
        load.start()

    @pl.when(polar)
    def _():
        cut_load.start()

    @pl.when(is_owner)
    def _():
        for load in table_loads:
            load.start()

    barrier = pltpu.get_barrier_semaphore()

    def at(to_lat, to_lon):
        return {"lon": to_lon, "lat": to_lat}

    def hail(to_lat, to_lon):
        pl.semaphore_signal(
            barrier, inc=1, device_id=at(to_lat, to_lon), device_id_type=pl.DeviceIdType.MESH
        )

    def remote(src, dst, send, recv, to_lat, to_lon):
        return pltpu.make_async_remote_copy(
            src_ref=src, dst_ref=dst, send_sem=send, recv_sem=recv,
            device_id=at(to_lat, to_lon), device_id_type=pl.DeviceIdType.MESH,
        )

    def wait_bytes(ref, sem):
        pltpu.make_async_copy(ref, ref, sem).wait()

    def over(count, body):
        def go(k, carry):
            body(k)
            return carry

        lax.fori_loop(0, count, go, 0)

    def far_first(i):
        return lax.rem(z + 4 + ((i + 1) // 2) * (1 - 2 * lax.rem(i, 2)), RINGS)

    right = lax.rem(lon + 1, TILES)
    left = lax.rem(lon + TILES - 1, TILES)

    @pl.when(polar)
    def _():
        def greet(i):
            b = far_first(i)
            for p in range(PAIRS):
                hail(*owner_of(b, p))

        over(BLOCKS, greet)

    @pl.when(is_owner)
    def _():
        def greet(i):
            for c in range(COLS):
                hail(polar_lat, COLS * far_first(i) + lax.rem(y + c, COLS))

        over(RINGS, greet)
        for c in range(1, COLS):
            hail(lat, COLS * z + lax.rem(y + c, COLS))

    @pl.when(beside)
    def _():
        for p in range(PAIRS):
            hail(*owner_of(BLOCKS, p))

    @pl.when(jnp.logical_not(polar))
    def _():
        hail(lat, left)
        hail(lat, right)

    @pl.when(lat > 0)
    def _():
        hail(lat - 1, lon)

    @pl.when(lat < LATS - 1)
    def _():
        hail(lat + 1, lon)

    for load in plane_loads:
        load.wait()
    ext[MASK, HALO : HALO + ROWS] = sea[...].astype(F32)
    sub = iota((LEVELS, 8, LANES), 1)

    def fill(b, tile):
        rows = 8 * tile
        lam_src[b, :, 0] = ext[0:LEVELS, rows : rows + 8]
        lam_src[b, :, 1] = jnp.where(
            sub < EDGE, ext[0:LEVELS, rows + 8 : rows + 16], ext[0:LEVELS, rows - 8 : rows]
        )

    def face_tiles(start, count):
        rows = pl.ds(pl.multiple_of(start, 8), 8 * count)
        mine = ext[MASK, rows]
        kappa_e, speed_e, kappa_n, speed_n = (ext[LEVELS + k, rows] for k in range(4))
        minus_n = mine * (-kappa_n - 0.5 * speed_n)
        plus_n = mine * (kappa_n - 0.5 * speed_n)
        planes = (
            mine * (-kappa_e - 0.5 * speed_e),
            mine * (kappa_e - 0.5 * speed_e),
            minus_n * pltpu.roll(mine, 8 * count - 1, 0),
            -mine * pltpu.roll(plus_n, 1, 0),
            mine,
        )
        return [plane.reshape(count, 8, LANES) for plane in planes]

    low = iota((1, 8, LANES), 1) < EDGE
    free = jnp.where(first_band, 0, 1)
    edge = jnp.where(first_band, BLOCKS - 1, 0)

    @pl.when(polar)
    def _():
        zeros = jnp.zeros((PLANES, 8, LANES), F32)
        ext[:, 0:8] = zeros
        ext[:, EXT - 8 : EXT] = zeros

        @pl.when(lat == 0)
        def _():
            ext[:, 8:16] = zeros
            for b in range(BLOCKS - 1):
                fill(b, b + 2)

        @pl.when(lat > 0)
        def _():
            ext[:, EXT - 16 : EXT - 8] = zeros
            for b in range(1, BLOCKS):
                fill(b, b + 2)

        for k, face in enumerate(face_tiles(jnp.where(first_band, 8, 16), BLOCKS + 1)):
            coef_src[pl.ds(free, BLOCKS - 1), k, 0] = face[1:8]
            coef_src[pl.ds(free, BLOCKS - 1), k, 1] = jnp.where(low, face[2:9], face[0:7])

        cut_load.wait()
        row = iota((8, LANES), 0)
        open_cut = jnp.full((8, LANES), float(NLON // 2), F32)
        cuts = [open_cut, open_cut]
        for b in range(BLOCKS):
            tile = open_cut
            for j in range(8):
                tile = jnp.where(row == j, cutoff[8 * b + j].astype(F32), tile)
            cuts.append(tile)
        cuts += [open_cut, open_cut]
        for b in range(BLOCKS):
            cut_src[b, 0] = cuts[b + 2]
            cut_src[b, 1] = jnp.where(row < EDGE, cuts[b + 3], cuts[b + 1])
        cut_src[BLOCKS, 0] = open_cut
        low_half = jnp.where(first_band, open_cut, cuts[2])
        high_half = jnp.where(first_band, cuts[BLOCKS + 1], open_cut)
        cut_src[BLOCKS, 1] = jnp.where(row < EDGE, low_half, high_half)

    peers = jnp.where(polar, 1 + 9 * PAIRS, 4)
    peers = peers + jnp.where(is_owner, TILES + COLS - 1, 0)
    pl.semaphore_wait(barrier, peers)

    low_rows = ext.at[:, pl.ds(HALO, 8)]
    high_rows = ext.at[:, pl.ds(HALO + ROWS - 8, 8)]
    south_rows = ext.at[:, pl.ds(HALO - 8, 8)]
    north_rows = ext.at[:, pl.ds(HALO + ROWS, 8)]
    to_south = remote(low_rows, north_rows, row_send.at[0], row_recv.at[0], lat - 1, lon)
    to_north = remote(high_rows, south_rows, row_send.at[1], row_recv.at[1], lat + 1, lon)

    @pl.when(lat > 0)
    def _():
        to_south.start()

    @pl.when(lat < LATS - 1)
    def _():
        to_north.start()

    def wait_rows():
        @pl.when(lat < LATS - 1)
        def _():
            to_south.wait_recv()

        @pl.when(lat > 0)
        def _():
            to_north.wait_recv()

    @pl.when(polar)
    def _():
        pltpu.make_async_remote_copy(
            src_ref=cut_src.at[z], dst_ref=cuts_ref, send_sem=cut_send.at[0],
            recv_sem=cut_recv.at[0], device_id=at(beside_lat, lon),
            device_id_type=pl.DeviceIdType.MESH,
        ).start()

        @pl.when(z == LAST_RING)
        def _():
            remote(
                cut_src.at[BLOCKS], cuts_ref, cut_send.at[1], cut_recv.at[0], last_lat, lon
            ).start()

        def send_block(b):
            for p in range(PAIRS):
                remote(
                    lam_src.at[b, pl.ds(2 * p, 2)], lam.at[lon], in_send.at[0], in_recv.at[0],
                    *owner_of(b, p),
                ).start()

        def send_coef(b):
            remote(
                coef_src.at[b], coef.at[y, z], cf_send.at[0], cf_recv.at[z], *owner_of(b, y)
            ).start()

        def send_free(i):
            @pl.when(far_first(i) != edge)
            def _():
                send_coef(far_first(i))

        over(RINGS, send_free)
        wait_rows()
        slots = (jnp.where(first_band, edge, BLOCKS), jnp.where(first_band, BLOCKS, edge))
        for k, face in enumerate(face_tiles(jnp.where(first_band, ROWS, 0), 4)):
            for j in range(2):
                coef_src[slots[j], k, 0] = face[1 + j]
                coef_src[slots[j], k, 1] = jnp.where(low[0], face[2 + j], face[j])

        send_coef(jnp.int32(BLOCKS))
        send_coef(edge)

        @pl.when(lat == 0)
        def _():
            fill(BLOCKS - 1, BLOCKS + 1)
            fill(BLOCKS, BLOCKS + 2)

        @pl.when(lat > 0)
        def _():
            fill(0, 2)
            fill(BLOCKS, 1)

        over(2, lambda i: send_block(far_first(i)))
        send_block(jnp.int32(BLOCKS))
        over(RINGS - 2, lambda i: send_block(far_first(2 + i)))

        wait_bytes(cuts_ref, cut_send.at[0])

        @pl.when(z == LAST_RING)
        def _():
            wait_bytes(cuts_ref, cut_send.at[1])

        wait_bytes(lam_src, in_send.at[0])
        wait_bytes(coef_src, cf_send.at[0])
        wait_bytes(out, out_recv.at[0])

    @pl.when(jnp.logical_not(polar))
    def _():
        wait_rows()
        here = slice(8, 8 + WIDE)
        lane = iota((WIDE, LANES), 1)
        total = jnp.zeros((WIDE, LANES), F32)
        for p in range(PLANES):
            v = ext[p, here]
            u = jnp.where(lane < EDGE, v, pltpu.roll(v, 2 * EDGE, 1))
            if p:
                u = pltpu.roll(u, 8 * p, 1)
            total = jnp.where((lane // 8) == p, u, total)
        packed[...] = total
        to_left = remote(packed, packed_r, col_send.at[0], col_recv.at[0], lat, left)
        to_right = remote(packed, packed_l, col_send.at[1], col_recv.at[1], lat, right)
        to_left.start()
        to_right.start()
        @pl.when(is_owner)
        def _():
            for load in table_loads:
                load.wait()
            high = wide_ref[...].astype(jnp.bfloat16)
            high_ref[...] = high
            low_ref[...] = (wide_ref[...] - high.astype(F32)).astype(jnp.bfloat16)

            def hand_on(t):
                ring = lax.rem(z + t, RINGS)
                wait_bytes(coef.at[y, ring], cf_recv.at[ring])
                for c in range(1, COLS):
                    remote(
                        coef.at[y, ring], coef.at[y, ring], pass_send.at[0], pass_recv.at[0],
                        lat, COLS * z + lax.rem(y + c, COLS),
                    ).start()

            over(RINGS, hand_on)
            wait_bytes(cuts_ref, cut_recv.at[0])
            cuts = cuts_ref[...].astype(jnp.int32)
            shape = (TILES, 8, LANES)
            wave = iota(shape, 0) + TILES * iota(shape, 2)
            wave = jnp.minimum(wave, NLON - wave)
            for half in range(2):
                kept_ref[half] = jnp.where(wave <= cuts[half][None], 1.0 / NLON, 0.0).astype(
                    F32
                ).reshape(2 * LANES, LANES)
            wait_bytes(lam, in_recv.at[0])

            def step(s):
                for half in range(2):
                    real, imag = filter_circles(
                        lam[:, 0, half], lam[:, 1, half], kept_ref[half], high_ref, low_ref, turn_ref
                    )
                    fil[:, 0, half] = real
                    fil[:, 1, half] = imag

                @pl.when(s == 0)
                def _():
                    wait_bytes(coef.at[pl.ds(0, COLS - 1)], pass_recv.at[0])

                    def circle(k):
                        parts = [coef[c, :, k] for c in range(COLS)]
                        return jnp.stack(parts, axis=1).reshape(TILES, 2, 8, LANES)

                    mine = circle(4)
                    faces[:, 0] = circle(0) * neighbour(mine, -1)
                    faces[:, 1] = -mine * neighbour(circle(1), 1)
                    faces[:, 2] = circle(2)
                    faces[:, 3] = circle(3)

                lam[...] = circle_step(fil[...], faces[...])

            over(STEPS, step)

            my_levels = pl.ds(2 * pair, 2)

            @pl.when(jnp.logical_not(last_block))
            def _():
                rows = pl.ds(pl.multiple_of(8 * jnp.minimum(block, BLOCKS - 1), 8), 8)

                def send_out(i):
                    for c in range(COLS):
                        tile = COLS * far_first(i) + lax.rem(y + c, COLS)
                        remote(
                            lam.at[tile, :, 0], out.at[my_levels, rows], out_send.at[0],
                            out_recv.at[0], polar_lat, tile,
                        ).start()

                over(RINGS, send_out)

            @pl.when(last_block)
            def _():
                def send_x(i):
                    for c in range(COLS):
                        tile = COLS * far_first(i) + lax.rem(y + c, COLS)
                        remote(
                            lam.at[tile, :, 0], row_x.at[my_levels], out_send.at[0], ox_recv.at[0],
                            beside_lat, tile,
                        ).start()

                over(RINGS, send_x)

        to_left.wait_recv()
        to_right.wait_recv()

        def beyond(p):
            from_right = packed_r[...]
            if p:
                from_right = pltpu.roll(from_right, LANES - 8 * p, 1)
            from_left = pltpu.roll(packed_l[...], (LANES - 8 - 8 * p) % LANES, 1)
            return jnp.where(lane < LANES // 2, from_right, from_left)

        def east_of(x):
            near, far = (pltpu.roll(v, LANES - 1, 1) for v in x)
            last = lane == LANES - 1
            return jnp.where(last, far, near), jnp.where(last, near, far)

        def west_of(x):
            near, far = (pltpu.roll(v, 1, 1) for v in x)
            last = lane == 0
            return jnp.where(last, far, near), jnp.where(last, near, far)

        def north_of(x):
            return [pltpu.roll(v, WIDE - 1, 0) for v in x]

        def south_of(x):
            return [pltpu.roll(v, 1, 0) for v in x]

        kappa_e, speed_e, kappa_n, speed_n, open_m = (
            (ext[LEVELS + k, here], beyond(LEVELS + k)) for k in range(5)
        )

        def minus(kappa, speed):
            return [m * (-k - 0.5 * f) for m, k, f in zip(open_m, kappa, speed)]

        def plus(kappa, speed):
            return [m * (k - 0.5 * f) for m, k, f in zip(open_m, kappa, speed)]

        wide_faces = (
            [a * b for a, b in zip(minus(kappa_e, speed_e), east_of(open_m))],
            [-a * b for a, b in zip(open_m, west_of(plus(kappa_e, speed_e)))],
            [a * b for a, b in zip(minus(kappa_n, speed_n), north_of(open_m))],
            [-a * b for a, b in zip(open_m, south_of(plus(kappa_n, speed_n)))],
        )
        for k in range(4):
            for side in range(2):
                wide_coef[k, side] = wide_faces[k][side]

        def level(p):
            from_right = pltpu.roll(packed_r[...], LANES - 8 * p, 1)
            from_left = pltpu.roll(packed_l[...], LANES - 8 - 8 * p, 1)
            x = (ext[p, here], jnp.where(lane < LANES // 2, from_right, from_left))
            for _ in range(STEPS):
                new = list(x)
                for k, near in enumerate((east_of(x), west_of(x), north_of(x), south_of(x))):
                    for side in range(2):
                        new[side] = new[side] + wide_coef[k, side] * (x[side] - near[side])
                x = tuple(new)
            mid_out[p] = x[0][8 : 8 + ROWS]

        over(LEVELS, level)

        store = pltpu.make_async_copy(mid_out, out, store_sem.at[0])
        store.start()

        @pl.when(is_owner)
        def _():
            wait_bytes(coef.at[pl.ds(0, COLS - 1)], pass_send.at[0])
            wait_bytes(lam.at[:, :, 0], out_send.at[0])

        to_left.wait_send()
        to_right.wait_send()

        @pl.when(beside)
        def _():
            wait_bytes(row_x, ox_recv.at[0])

        store.wait()

    @pl.when(lat > 0)
    def _():
        to_south.wait_send()

    @pl.when(lat < LATS - 1)
    def _():
        to_north.wait_send()


def shards(cotangent, diff_east, diff_north, flow_east, flow_north, sea_mask, cutoff):
    wide, turn = tables()
    hbm = pl.BlockSpec(memory_space=pltpu.HBM)
    dma = pltpu.SemaphoreType.DMA

    def room(*shape):
        return pltpu.VMEM(shape, F32)

    table = pltpu.VMEM((2 * LANES, 2 * LANES), jnp.bfloat16)
    field, shared = pl.pallas_call(
        kernel,
        out_shape=[
            jax.ShapeDtypeStruct((LEVELS, ROWS, LANES), F32),
            jax.ShapeDtypeStruct((LEVELS, 8, LANES), F32),
        ],
        in_specs=[hbm] * 9,
        out_specs=[hbm, hbm],
        scratch_shapes=[
            pltpu.VMEM((ROWS, LANES), jnp.int32),
            pltpu.SMEM((ROWS,), jnp.int32),
            room(2 * LANES, 2 * LANES),
            table,
            table,
            room(72, 8, LANES),
            room(PLANES, EXT, LANES),
            room(BLOCKS + 1, LEVELS, 2, 8, LANES),
            room(BLOCKS + 1, 5, 2, 8, LANES),
            room(BLOCKS + 1, 2, 8, LANES),
            room(TILES, 2, 2, 8, LANES),
            room(TILES, 2, 2, 8, LANES),
            room(COLS, RINGS, 5, 2, 8, LANES),
            room(TILES, 4, 2, 8, LANES),
            room(2, 2 * LANES, LANES),
            room(2, 8, LANES),
            room(WIDE, LANES),
            room(WIDE, LANES),
            room(WIDE, LANES),
            room(4, 2, WIDE, LANES),
            room(LEVELS, ROWS, LANES),
            dma((9,)),
            dma((2,)), dma((2,)), dma((2,)), dma((2,)), dma((2,)), dma((1,)), dma((1,)), dma((1,)),
            dma((1,)), dma((RINGS,)), dma((1,)), dma((1,)), dma((1,)), dma((1,)), dma((1,)), dma((1,)),
        ],
        compiler_params=pltpu.CompilerParams(
            collective_id=0, has_side_effects=True, vmem_limit_bytes=63 * 1024 * 1024
        ),
    )(
        cotangent, diff_east, diff_north, flow_east, flow_north, sea_mask, cutoff,
        jnp.asarray(wide), jnp.asarray(turn),
    )
    lat = lax.axis_index("lat")
    row = lax.broadcasted_iota(jnp.int32, field.shape, 1)
    taken = jnp.logical_or(
        jnp.logical_and(lat == 1, row < EDGE), jnp.logical_and(lat == LATS - 2, row >= ROWS - EDGE)
    )
    return jnp.where(taken, jnp.tile(shared, (1, ROWS // 8, 1)), field)


def solution(mesh):
    return jax.shard_map(
        shards,
        mesh=mesh,
        in_specs=(
            P(None, "lat", "lon"),
            P("lat", "lon"),
            P("lat", "lon"),
            P("lat", "lon"),
            P("lat", "lon"),
            P("lat", "lon"),
            P("lat"),
        ),
        out_specs=P(None, "lat", "lon"),
        check_vma=False,
    )
```

```python
import functools
import math

import jax
import jax.numpy as jnp
import numpy as np
from jax import lax
from jax.experimental import pallas as pl
from jax.experimental.pallas import tpu as pltpu
from jax.sharding import PartitionSpec as P

STEPS = 4
LEVELS = 8
ROWS = 64
LANES = 128
TILES = 32
NLON = TILES * LANES
BLOCKS = 8
PAIRS = 4
HALO = 16
EXT = ROWS + 2 * HALO
WIDE = ROWS + HALO
PLANES = LEVELS + 5
MASK = LEVELS + 4
EDGE = 4
LATS = 8
COLS = 4
RINGS = 8
LAST_RING = 4

F32 = jnp.float32


def tables():
    n = np.arange(LANES)
    angle = 2 * np.pi * (np.outer(n, n) % LANES) / LANES
    cos, sin = np.cos(angle), np.sin(angle)
    wide = np.block([[cos, -sin], [sin, cos]])
    q = np.arange(8)[:, None, None]
    c = np.arange(4)[None, :, None]
    first = 2 * np.pi * ((q * (n[None, None, :] + LANES * c)) % NLON) / NLON
    r = np.arange(4)[:, None]
    second = 2 * np.pi * ((r * n[None, :]) % 512) / 512

    def spread(values):
        values = values.reshape(-1, 1, LANES)
        return np.broadcast_to(values, (values.shape[0], 8, LANES)).astype(np.float32)

    turn = np.concatenate(
        [spread(np.cos(first)), spread(np.sin(first)), spread(np.cos(second)), spread(np.sin(second))]
    )
    return wide.astype(np.float32), turn


def cadd(x, y):
    return x[0] + y[0], x[1] + y[1]


def csub(x, y):
    return x[0] - y[0], x[1] - y[1]


def quarter(x, sign):
    if sign < 0:
        return x[1], -x[0]
    return -x[1], x[0]


def dft4(x, sign):
    even, odd = cadd(x[0], x[2]), csub(x[0], x[2])
    even2, odd2 = cadd(x[1], x[3]), quarter(csub(x[1], x[3]), sign)
    return [cadd(even, even2), cadd(odd, odd2), csub(even, even2), csub(odd, odd2)]


def dft8(x, sign):
    even = dft4([x[0], x[2], x[4], x[6]], sign)
    odd = dft4([x[1], x[3], x[5], x[7]], sign)
    half = math.sqrt(0.5)

    def eighth(v):
        rot = quarter(v, sign)
        return (v[0] + rot[0]) * half, (v[1] + rot[1]) * half

    odd[1] = eighth(odd[1])
    odd[2] = quarter(odd[2], sign)
    odd[3] = quarter(eighth(odd[3]), sign)
    return [cadd(e, o) for e, o in zip(even, odd)] + [csub(e, o) for e, o in zip(even, odd)]


def cmul(x, cos, sin, sign):
    if sign < 0:
        return x[0] * cos + x[1] * sin, x[1] * cos - x[0] * sin
    return x[0] * cos - x[1] * sin, x[1] * cos + x[0] * sin


def split_dot(left, high_ref, low_ref):
    high = left.astype(jnp.bfloat16)
    low = (left - high.astype(F32)).astype(jnp.bfloat16)
    dot = functools.partial(jnp.dot, preferred_element_type=F32)
    return dot(high, high_ref[...]) + (dot(low, high_ref[...]) + dot(high, low_ref[...]))


def filter_circles(real, imag, kept, high_ref, low_ref, turn_ref):
    shape = (8, 4, 8, LANES)
    cos1 = turn_ref[0:32].reshape(shape)
    sin1 = turn_ref[32:64].reshape(shape)
    real, imag = real.reshape(shape), imag.reshape(shape)
    parts = dft8([(real[a], imag[a]) for a in range(8)], -1)
    parts = [cmul(parts[q], cos1[q], sin1[q], -1) for q in range(8)]
    real = jnp.stack([p[0] for p in parts])
    imag = jnp.stack([p[1] for p in parts])
    parts = dft4([(real[:, c], imag[:, c]) for c in range(4)], -1)
    parts = [parts[0]] + [
        cmul(parts[r], turn_ref[64 + r], turn_ref[68 + r], -1) for r in range(1, 4)
    ]
    real = jnp.concatenate([p[0] for p in parts]).reshape(256, LANES)
    imag = jnp.concatenate([p[1] for p in parts]).reshape(256, LANES)
    spec = split_dot(jnp.concatenate([real, imag], axis=1), high_ref, low_ref)
    real = spec[:, :LANES] * kept
    imag = spec[:, LANES:] * kept
    back = split_dot(jnp.concatenate([imag, real], axis=1), high_ref, low_ref)
    real = back[:, LANES:].reshape(4, 8, 8, LANES)
    imag = back[:, :LANES].reshape(4, 8, 8, LANES)
    parts = [(real[0], imag[0])] + [
        cmul((real[r], imag[r]), turn_ref[64 + r], turn_ref[68 + r], 1) for r in range(1, 4)
    ]
    parts = dft4(parts, 1)
    real = jnp.stack([p[0] for p in parts], axis=1)
    imag = jnp.stack([p[1] for p in parts], axis=1)
    parts = [cmul((real[q], imag[q]), cos1[q], sin1[q], 1) for q in range(8)]
    parts = dft8(parts, 1)
    real = jnp.concatenate([p[0] for p in parts])
    imag = jnp.concatenate([p[1] for p in parts])
    return real, imag


def iota(shape, dim):
    return lax.broadcasted_iota(jnp.int32, shape, dim)


def circle_step(x, coef):
    shape = (TILES * 4, 8, LANES)
    full = (TILES, 2, 2, 8, LANES)
    lane = iota(shape, 2)
    row = iota(full, 3)
    flat = x.reshape(shape)
    east = pltpu.roll(flat, LANES - 1, 2)
    east = jnp.where(lane == LANES - 1, jnp.concatenate([east[4:], east[:4]]), east)
    west = pltpu.roll(flat, 1, 2)
    west = jnp.where(lane == 0, jnp.concatenate([west[-4:], west[:-4]]), west)

    def across(turned, edge):
        turned = turned.reshape(full)
        other = jnp.stack([turned[:, :, 1], turned[:, :, 0]], axis=2)
        return jnp.where(row == edge, other, turned)

    up = across(pltpu.roll(flat, 7, 1), 7)
    down = across(pltpu.roll(flat, 1, 1), 0)
    total = x
    for k, near in enumerate((east.reshape(full), west.reshape(full), up, down)):
        total = total + coef[:, k : k + 1] * (x - near)
    return total


def last_step(cells, before, after, coef):
    x = cells[:, :, 0]
    rim = cells[:, :, 1]
    count = x.shape[0]
    lane = iota(x.shape, 3)
    row = iota(x.shape, 2)

    def turn(v, step, dim):
        flat = pltpu.roll(v.reshape(-1, 8, LANES), step % v.shape[dim], dim - 1)
        return flat.reshape(v.shape)

    east = turn(x, -1, 3)
    next_east = turn(jnp.concatenate([x[1:], after[None]]), -1, 3)
    east = jnp.where(lane == LANES - 1, next_east, east)
    west = turn(x, 1, 3)
    next_west = turn(jnp.concatenate([before[None], x[: count - 1]]), 1, 3)
    west = jnp.where(lane == 0, next_west, west)
    up = jnp.where(row == 7, turn(rim, -1, 2), turn(x, -1, 2))
    down = jnp.where(row == 0, turn(rim, 1, 2), turn(x, 1, 2))
    total = x
    for k, near in enumerate((east, west, up, down)):
        total = total + coef[:, k : k + 1] * (x - near)
    return total


def neighbour(x, step):
    shape = (TILES * 2, 8, LANES)
    lane = iota(shape, 2)
    turned = pltpu.roll(x.reshape(shape), step % LANES, 2)
    moved = jnp.concatenate([turned[-2 * step :], turned[: -2 * step]])
    edge = 0 if step > 0 else LANES - 1
    return jnp.where(lane == edge, moved, turned).reshape(x.shape)


def kernel(
    cot, diff_east_in, diff_north_in, flow_east_in, flow_north_in, sea_in, cutoff_in, wide_in,
    turn_in,
    out, row_x,
    sea, cutoff, wide_ref, high_ref, low_ref, turn_ref,
    ext, lam_src, coef_src, cut_src,
    lam, fil, done, coef, faces, kept_ref, cuts_ref, packed, packed_l, packed_r, wide_coef, mid_out,
    load_sem, row_send, row_recv, col_send, col_recv, cut_send, cut_recv, in_send, in_recv,
    cf_send, cf_recv, pass_send, pass_recv, out_send, out_recv, ox_recv, store_sem,
):
    lon = lax.axis_index("lon")
    lat = lax.axis_index("lat")
    y = lax.rem(lon, 4)
    z = lon // 4
    first_band = lat < LATS // 2
    polar = jnp.logical_or(lat == 0, lat == LATS - 1)
    beside = jnp.logical_or(lat == 1, lat == LATS - 2)
    polar_lat = jnp.where(first_band, 0, LATS - 1)
    beside_lat = jnp.where(first_band, 1, LATS - 2)
    last_lat = jnp.where(first_band, 2, LATS - 3)
    last_block = jnp.logical_and(lat == last_lat, z == LAST_RING)
    is_owner = jnp.logical_or(beside, last_block)
    block = jnp.where(beside, z, BLOCKS)
    pair = y

    def owner_of(b, p):
        to_lat = jnp.where(b == BLOCKS, last_lat, beside_lat)
        return to_lat, COLS * jnp.where(b == BLOCKS, LAST_RING, b) + p

    main = pl.ds(HALO, ROWS)
    plane_loads = [
        pltpu.make_async_copy(src, dst, load_sem.at[k])
        for k, (src, dst) in enumerate(
            (
                (sea_in, sea),
                (diff_east_in, ext.at[LEVELS, main]),
                (flow_east_in, ext.at[LEVELS + 1, main]),
                (diff_north_in, ext.at[LEVELS + 2, main]),
                (flow_north_in, ext.at[LEVELS + 3, main]),
                (cot, ext.at[pl.ds(0, LEVELS), main]),
            )
        )
    ]
    cut_load = pltpu.make_async_copy(cutoff_in, cutoff, load_sem.at[6])
    table_loads = [
        pltpu.make_async_copy(turn_in, turn_ref, load_sem.at[7]),
        pltpu.make_async_copy(wide_in, wide_ref, load_sem.at[8]),
    ]
    for load in plane_loads:
        load.start()

    @pl.when(polar)
    def _():
        cut_load.start()

    @pl.when(is_owner)
    def _():
        for load in table_loads:
            load.start()

    barrier = pltpu.get_barrier_semaphore()

    def at(to_lat, to_lon):
        return {"lon": to_lon, "lat": to_lat}

    def hail(to_lat, to_lon):
        pl.semaphore_signal(
            barrier, inc=1, device_id=at(to_lat, to_lon), device_id_type=pl.DeviceIdType.MESH
        )

    def remote(src, dst, send, recv, to_lat, to_lon):
        return pltpu.make_async_remote_copy(
            src_ref=src, dst_ref=dst, send_sem=send, recv_sem=recv,
            device_id=at(to_lat, to_lon), device_id_type=pl.DeviceIdType.MESH,
        )

    def wait_bytes(ref, sem):
        pltpu.make_async_copy(ref, ref, sem).wait()

    def over(count, body):
        def go(k, carry):
            body(k)
            return carry

        lax.fori_loop(0, count, go, 0)

    def far_first(i):
        return lax.rem(z + 4 + ((i + 1) // 2) * (1 - 2 * lax.rem(i, 2)), RINGS)

    right = lax.rem(lon + 1, TILES)
    left = lax.rem(lon + TILES - 1, TILES)

    @pl.when(polar)
    def _():
        def greet(i):
            b = far_first(i)
            for p in range(PAIRS):
                hail(*owner_of(b, p))

        over(BLOCKS, greet)

    @pl.when(is_owner)
    def _():
        def greet(i):
            for c in range(COLS):
                hail(polar_lat, COLS * far_first(i) + lax.rem(y + c, COLS))

        over(RINGS, greet)
        for c in range(1, COLS):
            hail(lat, COLS * z + lax.rem(y + c, COLS))

    @pl.when(beside)
    def _():
        for p in range(PAIRS):
            hail(*owner_of(BLOCKS, p))

    @pl.when(jnp.logical_not(polar))
    def _():
        hail(lat, left)
        hail(lat, right)

    @pl.when(lat > 0)
    def _():
        hail(lat - 1, lon)

    @pl.when(lat < LATS - 1)
    def _():
        hail(lat + 1, lon)

    for load in plane_loads:
        load.wait()
    ext[MASK, HALO : HALO + ROWS] = sea[...].astype(F32)
    sub = iota((LEVELS, 8, LANES), 1)

    def fill(b, tile):
        rows = 8 * tile
        lam_src[b, :, 0] = ext[0:LEVELS, rows : rows + 8]
        lam_src[b, :, 1] = jnp.where(
            sub < EDGE, ext[0:LEVELS, rows + 8 : rows + 16], ext[0:LEVELS, rows - 8 : rows]
        )

    def face_tiles(start, count):
        rows = pl.ds(pl.multiple_of(start, 8), 8 * count)
        mine = ext[MASK, rows]
        kappa_e, speed_e, kappa_n, speed_n = (ext[LEVELS + k, rows] for k in range(4))
        minus_n = mine * (-kappa_n - 0.5 * speed_n)
        plus_n = mine * (kappa_n - 0.5 * speed_n)
        planes = (
            mine * (-kappa_e - 0.5 * speed_e),
            mine * (kappa_e - 0.5 * speed_e),
            minus_n * pltpu.roll(mine, 8 * count - 1, 0),
            -mine * pltpu.roll(plus_n, 1, 0),
            mine,
        )
        return [plane.reshape(count, 8, LANES) for plane in planes]

    low = iota((1, 8, LANES), 1) < EDGE
    free = jnp.where(first_band, 0, 1)
    edge = jnp.where(first_band, BLOCKS - 1, 0)

    @pl.when(polar)
    def _():
        zeros = jnp.zeros((PLANES, 8, LANES), F32)
        ext[:, 0:8] = zeros
        ext[:, EXT - 8 : EXT] = zeros

        @pl.when(lat == 0)
        def _():
            ext[:, 8:16] = zeros
            for b in range(BLOCKS - 1):
                fill(b, b + 2)

        @pl.when(lat > 0)
        def _():
            ext[:, EXT - 16 : EXT - 8] = zeros
            for b in range(1, BLOCKS):
                fill(b, b + 2)

        for k, face in enumerate(face_tiles(jnp.where(first_band, 8, 16), BLOCKS + 1)):
            coef_src[pl.ds(free, BLOCKS - 1), k, 0] = face[1:8]
            coef_src[pl.ds(free, BLOCKS - 1), k, 1] = jnp.where(low, face[2:9], face[0:7])

        cut_load.wait()
        row = iota((8, LANES), 0)
        open_cut = jnp.full((8, LANES), float(NLON // 2), F32)
        cuts = [open_cut, open_cut]
        for b in range(BLOCKS):
            tile = open_cut
            for j in range(8):
                tile = jnp.where(row == j, cutoff[8 * b + j].astype(F32), tile)
            cuts.append(tile)
        cuts += [open_cut, open_cut]
        for b in range(BLOCKS):
            cut_src[b, 0] = cuts[b + 2]
            cut_src[b, 1] = jnp.where(row < EDGE, cuts[b + 3], cuts[b + 1])
        cut_src[BLOCKS, 0] = open_cut
        low_half = jnp.where(first_band, open_cut, cuts[2])
        high_half = jnp.where(first_band, cuts[BLOCKS + 1], open_cut)
        cut_src[BLOCKS, 1] = jnp.where(row < EDGE, low_half, high_half)

    peers = jnp.where(polar, 1 + 9 * PAIRS, 4)
    peers = peers + jnp.where(is_owner, TILES + COLS - 1, 0)
    pl.semaphore_wait(barrier, peers)

    low_rows = ext.at[:, pl.ds(HALO, 8)]
    high_rows = ext.at[:, pl.ds(HALO + ROWS - 8, 8)]
    south_rows = ext.at[:, pl.ds(HALO - 8, 8)]
    north_rows = ext.at[:, pl.ds(HALO + ROWS, 8)]
    to_south = remote(low_rows, north_rows, row_send.at[0], row_recv.at[0], lat - 1, lon)
    to_north = remote(high_rows, south_rows, row_send.at[1], row_recv.at[1], lat + 1, lon)

    @pl.when(lat > 0)
    def _():
        to_south.start()

    @pl.when(lat < LATS - 1)
    def _():
        to_north.start()

    def wait_rows():
        @pl.when(lat < LATS - 1)
        def _():
            to_south.wait_recv()

        @pl.when(lat > 0)
        def _():
            to_north.wait_recv()

    @pl.when(polar)
    def _():
        def send_block(b):
            for p in range(PAIRS):
                remote(
                    lam_src.at[b, pl.ds(2 * p, 2)], lam.at[lon], in_send.at[0], in_recv.at[0],
                    *owner_of(b, p),
                ).start()

        def send_coef(b):
            remote(
                coef_src.at[b], coef.at[y, z], cf_send.at[0], cf_recv.at[z], *owner_of(b, y)
            ).start()

        def send_free(i):
            @pl.when(far_first(i) != edge)
            def _():
                send_coef(far_first(i))

        over(RINGS, send_free)
        pltpu.make_async_remote_copy(
            src_ref=cut_src.at[z], dst_ref=cuts_ref, send_sem=cut_send.at[0],
            recv_sem=cut_recv.at[0], device_id=at(beside_lat, lon),
            device_id_type=pl.DeviceIdType.MESH,
        ).start()

        @pl.when(z == LAST_RING)
        def _():
            remote(
                cut_src.at[BLOCKS], cuts_ref, cut_send.at[1], cut_recv.at[0], last_lat, lon
            ).start()

        wait_rows()
        slots = (jnp.where(first_band, edge, BLOCKS), jnp.where(first_band, BLOCKS, edge))
        for k, face in enumerate(face_tiles(jnp.where(first_band, ROWS, 0), 4)):
            for j in range(2):
                coef_src[slots[j], k, 0] = face[1 + j]
                coef_src[slots[j], k, 1] = jnp.where(low[0], face[2 + j], face[j])

        send_coef(jnp.int32(BLOCKS))
        send_coef(edge)

        @pl.when(lat == 0)
        def _():
            fill(BLOCKS - 1, BLOCKS + 1)
            fill(BLOCKS, BLOCKS + 2)

        @pl.when(lat > 0)
        def _():
            fill(0, 2)
            fill(BLOCKS, 1)

        send_block(jnp.int32(BLOCKS))
        over(RINGS, lambda i: send_block(far_first(i)))

        wait_bytes(cuts_ref, cut_send.at[0])

        @pl.when(z == LAST_RING)
        def _():
            wait_bytes(cuts_ref, cut_send.at[1])

        wait_bytes(lam_src, in_send.at[0])
        wait_bytes(coef_src, cf_send.at[0])
        wait_bytes(out, out_recv.at[0])

    @pl.when(jnp.logical_not(polar))
    def _():
        wait_rows()
        here = slice(8, 8 + WIDE)
        lane = iota((WIDE, LANES), 1)
        total = jnp.zeros((WIDE, LANES), F32)
        for p in range(PLANES):
            v = ext[p, here]
            u = jnp.where(lane < EDGE, v, pltpu.roll(v, 2 * EDGE, 1))
            if p:
                u = pltpu.roll(u, 8 * p, 1)
            total = jnp.where((lane // 8) == p, u, total)
        packed[...] = total
        to_left = remote(packed, packed_r, col_send.at[0], col_recv.at[0], lat, left)
        to_right = remote(packed, packed_l, col_send.at[1], col_recv.at[1], lat, right)
        to_left.start()
        to_right.start()
        @pl.when(is_owner)
        def _():
            for load in table_loads:
                load.wait()
            high = wide_ref[...].astype(jnp.bfloat16)
            high_ref[...] = high
            low_ref[...] = (wide_ref[...] - high.astype(F32)).astype(jnp.bfloat16)

            def hand_on(t):
                ring = lax.rem(z + t, RINGS)
                wait_bytes(coef.at[y, ring], cf_recv.at[ring])
                for c in range(1, COLS):
                    remote(
                        coef.at[y, ring], coef.at[y, ring], pass_send.at[0], pass_recv.at[0],
                        lat, COLS * z + lax.rem(y + c, COLS),
                    ).start()

            over(RINGS, hand_on)
            wait_bytes(cuts_ref, cut_recv.at[0])
            cuts = cuts_ref[...].astype(jnp.int32)
            shape = (TILES, 8, LANES)
            wave = iota(shape, 0) + TILES * iota(shape, 2)
            wave = jnp.minimum(wave, NLON - wave)
            for half in range(2):
                kept_ref[half] = jnp.where(wave <= cuts[half][None], 1.0 / NLON, 0.0).astype(
                    F32
                ).reshape(2 * LANES, LANES)
            wait_bytes(coef.at[pl.ds(0, COLS - 1)], pass_recv.at[0])

            def circle(k):
                parts = [coef[c, :, k] for c in range(COLS)]
                return jnp.stack(parts, axis=1).reshape(TILES, 2, 8, LANES)

            mine = circle(4)
            faces[:, 0] = circle(0) * neighbour(mine, -1)
            faces[:, 1] = -mine * neighbour(circle(1), 1)
            faces[:, 2] = circle(2)
            faces[:, 3] = circle(3)
            wait_bytes(lam, in_recv.at[0])

            def filtered():
                for half in range(2):
                    real, imag = filter_circles(
                        lam[:, 0, half], lam[:, 1, half], kept_ref[half], high_ref, low_ref,
                        turn_ref,
                    )
                    fil[:, 0, half] = real
                    fil[:, 1, half] = imag

            def step(s):
                filtered()
                lam[...] = circle_step(fil[...], faces[...])

            over(STEPS - 1, step)
            filtered()

            my_levels = pl.ds(2 * pair, 2)
            rows = pl.ds(pl.multiple_of(8 * jnp.minimum(block, BLOCKS - 1), 8), 8)

            def finish(i):
                ring = far_first(i)
                first = COLS * ring
                done[pl.ds(first, COLS)] = last_step(
                    fil[pl.ds(first, COLS)],
                    fil[lax.rem(first + TILES - 1, TILES), :, 0],
                    fil[lax.rem(first + COLS, TILES), :, 0],
                    faces[pl.ds(first, COLS), :, 0],
                )

                @pl.when(jnp.logical_not(last_block))
                def _():
                    for c in range(COLS):
                        tile = first + lax.rem(y + c, COLS)
                        remote(
                            done.at[tile], out.at[my_levels, rows], out_send.at[0],
                            out_recv.at[0], polar_lat, tile,
                        ).start()

                @pl.when(last_block)
                def _():
                    for c in range(COLS):
                        tile = first + lax.rem(y + c, COLS)
                        remote(
                            done.at[tile], row_x.at[my_levels], out_send.at[0], ox_recv.at[0],
                            beside_lat, tile,
                        ).start()

            over(RINGS, finish)

        to_left.wait_recv()
        to_right.wait_recv()

        def beyond(p):
            from_right = packed_r[...]
            if p:
                from_right = pltpu.roll(from_right, LANES - 8 * p, 1)
            from_left = pltpu.roll(packed_l[...], (LANES - 8 - 8 * p) % LANES, 1)
            return jnp.where(lane < LANES // 2, from_right, from_left)

        def east_of(x):
            near, far = (pltpu.roll(v, LANES - 1, 1) for v in x)
            last = lane == LANES - 1
            return jnp.where(last, far, near), jnp.where(last, near, far)

        def west_of(x):
            near, far = (pltpu.roll(v, 1, 1) for v in x)
            last = lane == 0
            return jnp.where(last, far, near), jnp.where(last, near, far)

        def north_of(x):
            return [pltpu.roll(v, WIDE - 1, 0) for v in x]

        def south_of(x):
            return [pltpu.roll(v, 1, 0) for v in x]

        kappa_e, speed_e, kappa_n, speed_n, open_m = (
            (ext[LEVELS + k, here], beyond(LEVELS + k)) for k in range(5)
        )

        def minus(kappa, speed):
            return [m * (-k - 0.5 * f) for m, k, f in zip(open_m, kappa, speed)]

        def plus(kappa, speed):
            return [m * (k - 0.5 * f) for m, k, f in zip(open_m, kappa, speed)]

        wide_faces = (
            [a * b for a, b in zip(minus(kappa_e, speed_e), east_of(open_m))],
            [-a * b for a, b in zip(open_m, west_of(plus(kappa_e, speed_e)))],
            [a * b for a, b in zip(minus(kappa_n, speed_n), north_of(open_m))],
            [-a * b for a, b in zip(open_m, south_of(plus(kappa_n, speed_n)))],
        )
        for k in range(4):
            for side in range(2):
                wide_coef[k, side] = wide_faces[k][side]

        def level(p):
            from_right = pltpu.roll(packed_r[...], LANES - 8 * p, 1)
            from_left = pltpu.roll(packed_l[...], LANES - 8 - 8 * p, 1)
            x = (ext[p, here], jnp.where(lane < LANES // 2, from_right, from_left))
            for _ in range(STEPS):
                new = list(x)
                for k, near in enumerate((east_of(x), west_of(x), north_of(x), south_of(x))):
                    for side in range(2):
                        new[side] = new[side] + wide_coef[k, side] * (x[side] - near[side])
                x = tuple(new)
            mid_out[p] = x[0][8 : 8 + ROWS]

        over(LEVELS, level)

        store = pltpu.make_async_copy(mid_out, out, store_sem.at[0])
        store.start()

        @pl.when(is_owner)
        def _():
            wait_bytes(coef.at[pl.ds(0, COLS - 1)], pass_send.at[0])
            wait_bytes(done, out_send.at[0])

        to_left.wait_send()
        to_right.wait_send()

        @pl.when(beside)
        def _():
            wait_bytes(row_x, ox_recv.at[0])

        store.wait()

    @pl.when(lat > 0)
    def _():
        to_south.wait_send()

    @pl.when(lat < LATS - 1)
    def _():
        to_north.wait_send()


def shards(cotangent, diff_east, diff_north, flow_east, flow_north, sea_mask, cutoff):
    wide, turn = tables()
    hbm = pl.BlockSpec(memory_space=pltpu.HBM)
    dma = pltpu.SemaphoreType.DMA

    def room(*shape):
        return pltpu.VMEM(shape, F32)

    table = pltpu.VMEM((2 * LANES, 2 * LANES), jnp.bfloat16)
    field, shared = pl.pallas_call(
        kernel,
        out_shape=[
            jax.ShapeDtypeStruct((LEVELS, ROWS, LANES), F32),
            jax.ShapeDtypeStruct((LEVELS, 8, LANES), F32),
        ],
        in_specs=[hbm] * 9,
        out_specs=[hbm, hbm],
        scratch_shapes=[
            pltpu.VMEM((ROWS, LANES), jnp.int32),
            pltpu.SMEM((ROWS,), jnp.int32),
            room(2 * LANES, 2 * LANES),
            table,
            table,
            room(72, 8, LANES),
            room(PLANES, EXT, LANES),
            room(BLOCKS + 1, LEVELS, 2, 8, LANES),
            room(BLOCKS + 1, 5, 2, 8, LANES),
            room(BLOCKS + 1, 2, 8, LANES),
            room(TILES, 2, 2, 8, LANES),
            room(TILES, 2, 2, 8, LANES),
            room(TILES, 2, 8, LANES),
            room(COLS, RINGS, 5, 2, 8, LANES),
            room(TILES, 4, 2, 8, LANES),
            room(2, 2 * LANES, LANES),
            room(2, 8, LANES),
            room(WIDE, LANES),
            room(WIDE, LANES),
            room(WIDE, LANES),
            room(4, 2, WIDE, LANES),
            room(LEVELS, ROWS, LANES),
            dma((9,)),
            dma((2,)), dma((2,)), dma((2,)), dma((2,)), dma((2,)), dma((1,)), dma((1,)), dma((1,)),
            dma((1,)), dma((RINGS,)), dma((1,)), dma((1,)), dma((1,)), dma((1,)), dma((1,)), dma((1,)),
        ],
        compiler_params=pltpu.CompilerParams(
            collective_id=0, has_side_effects=True, vmem_limit_bytes=63 * 1024 * 1024
        ),
    )(
        cotangent, diff_east, diff_north, flow_east, flow_north, sea_mask, cutoff,
        jnp.asarray(wide), jnp.asarray(turn),
    )
    lat = lax.axis_index("lat")
    row = lax.broadcasted_iota(jnp.int32, field.shape, 1)
    taken = jnp.logical_or(
        jnp.logical_and(lat == 1, row < EDGE), jnp.logical_and(lat == LATS - 2, row >= ROWS - EDGE)
    )
    return jnp.where(taken, jnp.tile(shared, (1, ROWS // 8, 1)), field)


def solution(mesh):
    return jax.shard_map(
        shards,
        mesh=mesh,
        in_specs=(
            P(None, "lat", "lon"),
            P("lat", "lon"),
            P("lat", "lon"),
            P("lat", "lon"),
            P("lat", "lon"),
            P("lat", "lon"),
            P("lat"),
        ),
        out_specs=P(None, "lat", "lon"),
        check_vma=False,
    )
```

```python
import functools
import math

import jax
import jax.numpy as jnp
import numpy as np
from jax import lax
from jax.experimental import pallas as pl
from jax.experimental.pallas import tpu as pltpu
from jax.sharding import PartitionSpec as P

STEPS = 4
LEVELS = 8
ROWS = 64
LANES = 128
TILES = 32
NLON = TILES * LANES
BLOCKS = 8
PAIRS = 4
HALO = 16
EXT = ROWS + 2 * HALO
WIDE = ROWS + HALO
PLANES = LEVELS + 5
MASK = LEVELS + 4
EDGE = 4
LATS = 8
COLS = 4
RINGS = 8
EXTRA = 3

F32 = jnp.float32


def tables():
    n = np.arange(LANES)
    angle = 2 * np.pi * (np.outer(n, n) % LANES) / LANES
    cos, sin = np.cos(angle), np.sin(angle)
    wide = np.block([[cos, -sin], [sin, cos]])
    q = np.arange(8)[:, None, None]
    c = np.arange(4)[None, :, None]
    first = 2 * np.pi * ((q * (n[None, None, :] + LANES * c)) % NLON) / NLON
    r = np.arange(4)[:, None]
    second = 2 * np.pi * ((r * n[None, :]) % 512) / 512

    def spread(values):
        values = values.reshape(-1, 1, LANES)
        return np.broadcast_to(values, (values.shape[0], 8, LANES)).astype(np.float32)

    turn = np.concatenate(
        [spread(np.cos(first)), spread(np.sin(first)), spread(np.cos(second)), spread(np.sin(second))]
    )
    return wide.astype(np.float32), turn


def cadd(x, y):
    return x[0] + y[0], x[1] + y[1]


def csub(x, y):
    return x[0] - y[0], x[1] - y[1]


def quarter(x, sign):
    if sign < 0:
        return x[1], -x[0]
    return -x[1], x[0]


def dft4(x, sign):
    even, odd = cadd(x[0], x[2]), csub(x[0], x[2])
    even2, odd2 = cadd(x[1], x[3]), quarter(csub(x[1], x[3]), sign)
    return [cadd(even, even2), cadd(odd, odd2), csub(even, even2), csub(odd, odd2)]


def dft8(x, sign):
    even = dft4([x[0], x[2], x[4], x[6]], sign)
    odd = dft4([x[1], x[3], x[5], x[7]], sign)
    half = math.sqrt(0.5)

    def eighth(v):
        rot = quarter(v, sign)
        return (v[0] + rot[0]) * half, (v[1] + rot[1]) * half

    odd[1] = eighth(odd[1])
    odd[2] = quarter(odd[2], sign)
    odd[3] = quarter(eighth(odd[3]), sign)
    return [cadd(e, o) for e, o in zip(even, odd)] + [csub(e, o) for e, o in zip(even, odd)]


def cmul(x, cos, sin, sign):
    if sign < 0:
        return x[0] * cos + x[1] * sin, x[1] * cos - x[0] * sin
    return x[0] * cos - x[1] * sin, x[1] * cos + x[0] * sin


def split_dot(left, high_ref, low_ref):
    high = left.astype(jnp.bfloat16)
    low = (left - high.astype(F32)).astype(jnp.bfloat16)
    dot = functools.partial(jnp.dot, preferred_element_type=F32)
    return dot(high, high_ref[...]) + (dot(low, high_ref[...]) + dot(high, low_ref[...]))


def filter_circles(real, imag, kept, high_ref, low_ref, turn_ref):
    shape = (8, 4, 8, LANES)
    cos1 = turn_ref[0:32].reshape(shape)
    sin1 = turn_ref[32:64].reshape(shape)
    real, imag = real.reshape(shape), imag.reshape(shape)
    parts = dft8([(real[a], imag[a]) for a in range(8)], -1)
    parts = [cmul(parts[q], cos1[q], sin1[q], -1) for q in range(8)]
    real = jnp.stack([p[0] for p in parts])
    imag = jnp.stack([p[1] for p in parts])
    parts = dft4([(real[:, c], imag[:, c]) for c in range(4)], -1)
    parts = [parts[0]] + [
        cmul(parts[r], turn_ref[64 + r], turn_ref[68 + r], -1) for r in range(1, 4)
    ]
    real = jnp.concatenate([p[0] for p in parts]).reshape(256, LANES)
    imag = jnp.concatenate([p[1] for p in parts]).reshape(256, LANES)
    spec = split_dot(jnp.concatenate([real, imag], axis=1), high_ref, low_ref)
    real = spec[:, :LANES] * kept
    imag = spec[:, LANES:] * kept
    back = split_dot(jnp.concatenate([imag, real], axis=1), high_ref, low_ref)
    real = back[:, LANES:].reshape(4, 8, 8, LANES)
    imag = back[:, :LANES].reshape(4, 8, 8, LANES)
    parts = [(real[0], imag[0])] + [
        cmul((real[r], imag[r]), turn_ref[64 + r], turn_ref[68 + r], 1) for r in range(1, 4)
    ]
    parts = dft4(parts, 1)
    real = jnp.stack([p[0] for p in parts], axis=1)
    imag = jnp.stack([p[1] for p in parts], axis=1)
    parts = [cmul((real[q], imag[q]), cos1[q], sin1[q], 1) for q in range(8)]
    parts = dft8(parts, 1)
    real = jnp.concatenate([p[0] for p in parts])
    imag = jnp.concatenate([p[1] for p in parts])
    return real, imag


def iota(shape, dim):
    return lax.broadcasted_iota(jnp.int32, shape, dim)


def circle_step(x, coef):
    shape = (TILES * 4, 8, LANES)
    full = (TILES, 2, 2, 8, LANES)
    lane = iota(shape, 2)
    row = iota(full, 3)
    flat = x.reshape(shape)
    east = pltpu.roll(flat, LANES - 1, 2)
    east = jnp.where(lane == LANES - 1, jnp.concatenate([east[4:], east[:4]]), east)
    west = pltpu.roll(flat, 1, 2)
    west = jnp.where(lane == 0, jnp.concatenate([west[-4:], west[:-4]]), west)

    def across(turned, edge):
        turned = turned.reshape(full)
        other = jnp.stack([turned[:, :, 1], turned[:, :, 0]], axis=2)
        return jnp.where(row == edge, other, turned)

    up = across(pltpu.roll(flat, 7, 1), 7)
    down = across(pltpu.roll(flat, 1, 1), 0)
    total = x
    for k, near in enumerate((east.reshape(full), west.reshape(full), up, down)):
        total = total + coef[:, k : k + 1] * (x - near)
    return total


def last_step(cells, before, after, coef):
    x = cells[:, :, 0]
    rim = cells[:, :, 1]
    count = x.shape[0]
    lane = iota(x.shape, 3)
    row = iota(x.shape, 2)

    def turn(v, step, dim):
        flat = pltpu.roll(v.reshape(-1, 8, LANES), step % v.shape[dim], dim - 1)
        return flat.reshape(v.shape)

    east = turn(x, -1, 3)
    next_east = turn(jnp.concatenate([x[1:], after[None]]), -1, 3)
    east = jnp.where(lane == LANES - 1, next_east, east)
    west = turn(x, 1, 3)
    next_west = turn(jnp.concatenate([before[None], x[: count - 1]]), 1, 3)
    west = jnp.where(lane == 0, next_west, west)
    up = jnp.where(row == 7, turn(rim, -1, 2), turn(x, -1, 2))
    down = jnp.where(row == 0, turn(rim, 1, 2), turn(x, 1, 2))
    total = x
    for k, near in enumerate((east, west, up, down)):
        total = total + coef[:, k : k + 1] * (x - near)
    return total


def neighbour(x, step):
    shape = (x.size // (8 * LANES), 8, LANES)
    width = shape[0] // TILES
    lane = iota(shape, 2)
    turned = pltpu.roll(x.reshape(shape), step % LANES, 2)
    moved = jnp.concatenate([turned[-width * step :], turned[: -width * step]])
    edge = 0 if step > 0 else LANES - 1
    return jnp.where(lane == edge, moved, turned).reshape(x.shape)


def edge_step(x, coef, extra, coef_x):
    full = (TILES, 2, 8, LANES)
    row = iota(full, 2)
    own, rim = x[:, :, 0], x[:, :, 1]

    def turn(v, step):
        return pltpu.roll(v.reshape(-1, 8, LANES), step, 1).reshape(v.shape)

    up_own = jnp.where(row == 7, turn(rim, 7), turn(own, 7))
    down_own = jnp.where(row == 0, turn(rim, 1), turn(own, 1))
    up_rim = jnp.where(row == 7, turn(own, 7), turn(rim, 7))
    up_rim = jnp.where(row == 3, jnp.stack([turn(extra, 3), turn(extra, 7)], axis=1), up_rim)
    down_rim = jnp.where(row == 0, turn(own, 1), turn(rim, 1))
    down_rim = jnp.where(row == 4, jnp.stack([turn(extra, 1), turn(extra, 5)], axis=1), down_rim)
    row = iota(extra.shape, 1)
    up_x = jnp.where(row == 3, turn(rim[:, 0], 7), turn(extra, 7))
    up_x = jnp.where(row == 7, turn(rim[:, 1], 3), up_x)
    down_x = jnp.where(row == 0, turn(rim[:, 0], 5), turn(extra, 1))
    down_x = jnp.where(row == 4, turn(rim[:, 1], 1), down_x)

    up = jnp.stack([up_own, up_rim], axis=2)
    down = jnp.stack([down_own, down_rim], axis=2)
    total = x
    for k, near in enumerate((neighbour(x, -1), neighbour(x, 1), up, down)):
        total = total + coef[:, k : k + 1] * (x - near)
    total_x = extra
    for k, near in enumerate((neighbour(extra, -1), neighbour(extra, 1), up_x, down_x)):
        total_x = total_x + coef_x[:, k] * (extra - near)
    return total, total_x


def kernel(
    cot, diff_east_in, diff_north_in, flow_east_in, flow_north_in, sea_in, cutoff_in, wide_in,
    turn_in,
    out, row_x,
    sea, cutoff, wide_ref, high_ref, low_ref, turn_ref,
    ext, lam_src, coef_src, cut_src, extra_src, strip_src, extra, strip, faces_x, done_x,
    lam, fil, done, coef, faces, kept_ref, cuts_ref, packed, packed_l, packed_r, wide_coef, mid_out,
    load_sem, row_send, row_recv, col_send, col_recv, cut_send, cut_recv, in_send, in_recv,
    cf_send, cf_recv, pass_send, pass_recv, out_send, out_recv, ox_recv, store_sem, lx_send, lx_recv,
    sx_send, sx_recv, px_send, px_recv, ox_send,
):
    lon = lax.axis_index("lon")
    lat = lax.axis_index("lat")
    y = lax.rem(lon, 4)
    z = lon // 4
    first_band = lat < LATS // 2
    polar = jnp.logical_or(lat == 0, lat == LATS - 1)
    beside = jnp.logical_or(lat == 1, lat == LATS - 2)
    polar_lat = jnp.where(first_band, 0, LATS - 1)
    beside_lat = jnp.where(first_band, 1, LATS - 2)
    edge = jnp.where(first_band, BLOCKS - 1, 0)
    is_edge = jnp.logical_and(beside, z == edge)
    pair = y

    def owner_of(b, p):
        return beside_lat, COLS * b + p

    main = pl.ds(HALO, ROWS)
    plane_loads = [
        pltpu.make_async_copy(src, dst, load_sem.at[k])
        for k, (src, dst) in enumerate(
            (
                (sea_in, sea),
                (diff_east_in, ext.at[LEVELS, main]),
                (flow_east_in, ext.at[LEVELS + 1, main]),
                (diff_north_in, ext.at[LEVELS + 2, main]),
                (flow_north_in, ext.at[LEVELS + 3, main]),
                (cot, ext.at[pl.ds(0, LEVELS), main]),
            )
        )
    ]
    cut_load = pltpu.make_async_copy(cutoff_in, cutoff, load_sem.at[6])
    table_loads = [
        pltpu.make_async_copy(turn_in, turn_ref, load_sem.at[7]),
        pltpu.make_async_copy(wide_in, wide_ref, load_sem.at[8]),
    ]
    for load in plane_loads:
        load.start()

    @pl.when(polar)
    def _():
        cut_load.start()

    @pl.when(beside)
    def _():
        for load in table_loads:
            load.start()

    barrier = pltpu.get_barrier_semaphore()

    def at(to_lat, to_lon):
        return {"lon": to_lon, "lat": to_lat}

    def hail(to_lat, to_lon):
        pl.semaphore_signal(
            barrier, inc=1, device_id=at(to_lat, to_lon), device_id_type=pl.DeviceIdType.MESH
        )

    def remote(src, dst, send, recv, to_lat, to_lon):
        return pltpu.make_async_remote_copy(
            src_ref=src, dst_ref=dst, send_sem=send, recv_sem=recv,
            device_id=at(to_lat, to_lon), device_id_type=pl.DeviceIdType.MESH,
        )

    def wait_bytes(ref, sem):
        pltpu.make_async_copy(ref, ref, sem).wait()

    def over(count, body):
        def go(k, carry):
            body(k)
            return carry

        lax.fori_loop(0, count, go, 0)

    def far_first(i):
        return lax.rem(z + 4 + ((i + 1) // 2) * (1 - 2 * lax.rem(i, 2)), RINGS)

    right = lax.rem(lon + 1, TILES)
    left = lax.rem(lon + TILES - 1, TILES)

    @pl.when(polar)
    def _():
        def greet(i):
            b = far_first(i)
            for p in range(PAIRS):
                hail(*owner_of(b, p))

        over(BLOCKS, greet)

    @pl.when(beside)
    def _():
        def greet(i):
            for c in range(COLS):
                hail(polar_lat, COLS * far_first(i) + lax.rem(y + c, COLS))

        over(RINGS, greet)
        for c in range(1, COLS):
            hail(lat, COLS * z + lax.rem(y + c, COLS))

    @pl.when(beside)
    def _():
        for p in range(PAIRS):
            @pl.when(COLS * edge + p != lon)
            def _():
                hail(lat, COLS * edge + p)

    @pl.when(jnp.logical_not(polar))
    def _():
        hail(lat, left)
        hail(lat, right)

    @pl.when(lat > 0)
    def _():
        hail(lat - 1, lon)

    @pl.when(lat < LATS - 1)
    def _():
        hail(lat + 1, lon)

    for load in plane_loads:
        load.wait()
    ext[MASK, HALO : HALO + ROWS] = sea[...].astype(F32)
    sub = iota((LEVELS, 8, LANES), 1)

    def fill(b, tile):
        rows = 8 * tile
        lam_src[b, :, 0] = ext[0:LEVELS, rows : rows + 8]
        lam_src[b, :, 1] = jnp.where(
            sub < EDGE, ext[0:LEVELS, rows + 8 : rows + 16], ext[0:LEVELS, rows - 8 : rows]
        )

    def face_tiles(start, count):
        rows = pl.ds(pl.multiple_of(start, 8), 8 * count)
        mine = ext[MASK, rows]
        kappa_e, speed_e, kappa_n, speed_n = (ext[LEVELS + k, rows] for k in range(4))
        minus_n = mine * (-kappa_n - 0.5 * speed_n)
        plus_n = mine * (kappa_n - 0.5 * speed_n)
        planes = (
            mine * (-kappa_e - 0.5 * speed_e),
            mine * (kappa_e - 0.5 * speed_e),
            minus_n * pltpu.roll(mine, 8 * count - 1, 0),
            -mine * pltpu.roll(plus_n, 1, 0),
            mine,
        )
        return [plane.reshape(count, 8, LANES) for plane in planes]

    low = iota((1, 8, LANES), 1) < EDGE
    free = jnp.where(first_band, 0, 1)
    @pl.when(polar)
    def _():
        zeros = jnp.zeros((PLANES, 8, LANES), F32)
        ext[:, 0:8] = zeros
        ext[:, EXT - 8 : EXT] = zeros

        @pl.when(lat == 0)
        def _():
            ext[:, 8:16] = zeros
            for b in range(BLOCKS - 1):
                fill(b, b + 2)

        @pl.when(lat > 0)
        def _():
            ext[:, EXT - 16 : EXT - 8] = zeros
            for b in range(1, BLOCKS):
                fill(b, b + 2)

        for k, face in enumerate(face_tiles(jnp.where(first_band, 8, 16), BLOCKS + 1)):
            coef_src[pl.ds(free, BLOCKS - 1), k, 0] = face[1:8]
            coef_src[pl.ds(free, BLOCKS - 1), k, 1] = jnp.where(low, face[2:9], face[0:7])

        cut_load.wait()
        row = iota((8, LANES), 0)
        open_cut = jnp.full((8, LANES), float(NLON // 2), F32)
        cuts = [open_cut, open_cut]
        for b in range(BLOCKS):
            tile = open_cut
            for j in range(8):
                tile = jnp.where(row == j, cutoff[8 * b + j].astype(F32), tile)
            cuts.append(tile)
        cuts += [open_cut, open_cut]
        for b in range(BLOCKS):
            cut_src[b, 0] = cuts[b + 2]
            cut_src[b, 1] = jnp.where(row < EDGE, cuts[b + 3], cuts[b + 1])

    peers = jnp.where(polar, 1 + BLOCKS * PAIRS, 4)
    peers = peers + jnp.where(beside, TILES + COLS - 1, 0)
    peers = peers + jnp.where(is_edge, TILES - 1, 0)
    pl.semaphore_wait(barrier, peers)

    low_rows = ext.at[:, pl.ds(HALO, 8)]
    high_rows = ext.at[:, pl.ds(HALO + ROWS - 8, 8)]
    south_rows = ext.at[:, pl.ds(HALO - 8, 8)]
    north_rows = ext.at[:, pl.ds(HALO + ROWS, 8)]
    to_south = remote(low_rows, north_rows, row_send.at[0], row_recv.at[0], lat - 1, lon)
    to_north = remote(high_rows, south_rows, row_send.at[1], row_recv.at[1], lat + 1, lon)

    @pl.when(lat > 0)
    def _():
        to_south.start()

    @pl.when(lat < LATS - 1)
    def _():
        to_north.start()

    def wait_rows():
        @pl.when(lat < LATS - 1)
        def _():
            to_south.wait_recv()

        @pl.when(lat > 0)
        def _():
            to_north.wait_recv()

    @pl.when(polar)
    def _():
        def send_block(b):
            for p in range(PAIRS):
                remote(
                    lam_src.at[b, pl.ds(2 * p, 2)], lam.at[lon], in_send.at[0], in_recv.at[0],
                    *owner_of(b, p),
                ).start()

        def send_coef(b):
            remote(
                coef_src.at[b], coef.at[y, z], cf_send.at[0], cf_recv.at[z], *owner_of(b, y)
            ).start()

        def send_free(i):
            @pl.when(far_first(i) != edge)
            def _():
                send_coef(far_first(i))

        over(RINGS, send_free)
        pltpu.make_async_remote_copy(
            src_ref=cut_src.at[z], dst_ref=cuts_ref, send_sem=cut_send.at[0],
            recv_sem=cut_recv.at[0], device_id=at(beside_lat, lon),
            device_id_type=pl.DeviceIdType.MESH,
        ).start()

        wait_rows()
        def halves(low_from, high_from):
            lower = jnp.where(first_band, pltpu.roll(low_from, 4, 1), low_from)
            upper = jnp.where(first_band, high_from, pltpu.roll(high_from, 4, 1))
            return jnp.where(low, lower, upper)

        strips = []
        for k, face in enumerate(face_tiles(jnp.where(first_band, ROWS, 0), 4)):
            coef_src[edge, k, 0] = jnp.where(first_band, face[1], face[2])
            coef_src[edge, k, 1] = jnp.where(
                low[0], jnp.where(first_band, face[2], face[3]), jnp.where(first_band, face[0], face[1])
            )
            strips.append(jnp.where(first_band, face[2], face[1])[None])
        for j in range(EXTRA):
            strip_src[j] = halves(strips[2 * j], strips[min(2 * j + 1, 4)])[0]
        send_coef(edge)
        remote(
            strip_src, strip.at[y, z], sx_send.at[0], sx_recv.at[0], *owner_of(edge, y)
        ).start()

        @pl.when(lat == 0)
        def _():
            fill(BLOCKS - 1, BLOCKS + 1)

        @pl.when(lat > 0)
        def _():
            fill(0, 2)

        beyond_rows = pl.ds(pl.multiple_of(jnp.where(first_band, HALO + ROWS, HALO - 8), 8), 8)
        outside = ext[pl.ds(0, LEVELS), beyond_rows]
        for p in range(PAIRS):
            extra_src[p] = halves(outside[2 * p : 2 * p + 1], outside[2 * p + 1 : 2 * p + 2])[0]
            remote(
                extra_src.at[p], extra.at[lon], lx_send.at[0], lx_recv.at[0], *owner_of(edge, p)
            ).start()
        over(RINGS, lambda i: send_block(far_first(i)))

        wait_bytes(cuts_ref, cut_send.at[0])

        wait_bytes(extra_src, lx_send.at[0])
        wait_bytes(strip_src, sx_send.at[0])
        wait_bytes(lam_src, in_send.at[0])
        wait_bytes(coef_src, cf_send.at[0])
        wait_bytes(out, out_recv.at[0])

    @pl.when(jnp.logical_not(polar))
    def _():
        wait_rows()
        here = slice(8, 8 + WIDE)
        lane = iota((WIDE, LANES), 1)
        total = jnp.zeros((WIDE, LANES), F32)
        for p in range(PLANES):
            v = ext[p, here]
            u = jnp.where(lane < EDGE, v, pltpu.roll(v, 2 * EDGE, 1))
            if p:
                u = pltpu.roll(u, 8 * p, 1)
            total = jnp.where((lane // 8) == p, u, total)
        packed[...] = total
        to_left = remote(packed, packed_r, col_send.at[0], col_recv.at[0], lat, left)
        to_right = remote(packed, packed_l, col_send.at[1], col_recv.at[1], lat, right)
        to_left.start()
        to_right.start()
        @pl.when(beside)
        def _():
            for load in table_loads:
                load.wait()
            high = wide_ref[...].astype(jnp.bfloat16)
            high_ref[...] = high
            low_ref[...] = (wide_ref[...] - high.astype(F32)).astype(jnp.bfloat16)

            def hand_on(t):
                ring = lax.rem(z + t, RINGS)
                wait_bytes(coef.at[y, ring], cf_recv.at[ring])
                for c in range(1, COLS):
                    remote(
                        coef.at[y, ring], coef.at[y, ring], pass_send.at[0], pass_recv.at[0],
                        lat, COLS * z + lax.rem(y + c, COLS),
                    ).start()

            over(RINGS, hand_on)

            @pl.when(is_edge)
            def _():
                wait_bytes(strip.at[y], sx_recv.at[0])
                for c in range(1, COLS):
                    remote(
                        strip.at[y], strip.at[y], px_send.at[0], px_recv.at[0],
                        lat, COLS * z + lax.rem(y + c, COLS),
                    ).start()

            wait_bytes(cuts_ref, cut_recv.at[0])
            cuts = cuts_ref[...].astype(jnp.int32)
            shape = (TILES, 8, LANES)
            wave = iota(shape, 0) + TILES * iota(shape, 2)
            wave = jnp.minimum(wave, NLON - wave)
            for half in range(2):
                kept_ref[half] = jnp.where(wave <= cuts[half][None], 1.0 / NLON, 0.0).astype(
                    F32
                ).reshape(2 * LANES, LANES)
            wait_bytes(lam, in_recv.at[0])

            @pl.when(is_edge)
            def _():
                wait_bytes(extra, lx_recv.at[0])

            def filtered():
                for half in range(2):
                    real, imag = filter_circles(
                        lam[:, 0, half], lam[:, 1, half], kept_ref[half], high_ref, low_ref,
                        turn_ref,
                    )
                    fil[:, 0, half] = real
                    fil[:, 1, half] = imag

            def step(s):
                filtered()

                @pl.when(s == 0)
                def _():
                    wait_bytes(coef.at[pl.ds(0, COLS - 1)], pass_recv.at[0])

                    def circle(k):
                        parts = [coef[c, :, k] for c in range(COLS)]
                        return jnp.stack(parts, axis=1).reshape(TILES, 2, 8, LANES)

                    mine = circle(4)
                    faces[:, 0] = circle(0) * neighbour(mine, -1)
                    faces[:, 1] = -mine * neighbour(circle(1), 1)
                    faces[:, 2] = circle(2)
                    faces[:, 3] = circle(3)

                @pl.when(jnp.logical_and(is_edge, s == 0))
                def _():
                    wait_bytes(strip.at[pl.ds(0, COLS - 1)], px_recv.at[0])

                    def circle(k):
                        parts = [strip[c, :, k // 2] for c in range(COLS)]
                        both = jnp.stack(parts, axis=1).reshape(TILES, 8, LANES)
                        turned = pltpu.roll(both, 4, 1)
                        lower = iota(both.shape, 1) < EDGE
                        if k % 2:
                            return jnp.where(lower, turned, both)
                        return jnp.where(lower, both, turned)

                    mine = circle(4)
                    faces_x[:, 0] = circle(0) * neighbour(mine, -1)
                    faces_x[:, 1] = -mine * neighbour(circle(1), 1)
                    faces_x[:, 2] = circle(2)
                    faces_x[:, 3] = circle(3)

                @pl.when(is_edge)
                def _():
                    lam[...], extra[...] = edge_step(
                        fil[...], faces[...], extra[...], faces_x[...]
                    )

                @pl.when(jnp.logical_not(is_edge))
                def _():
                    lam[...] = circle_step(fil[...], faces[...])

            over(STEPS - 1, step)
            filtered()

            my_levels = pl.ds(2 * pair, 2)
            rows = pl.ds(pl.multiple_of(8 * z, 8), 8)

            @pl.when(is_edge)
            def _():
                total, _ = edge_step(fil[...], faces[...], extra[...], faces_x[...])
                done[...] = total[:, :, 0]
                done_x[...] = total[:, :, 1]

            def finish(i):
                ring = far_first(i)
                first = COLS * ring

                @pl.when(jnp.logical_not(is_edge))
                def _():
                    done[pl.ds(first, COLS)] = last_step(
                        fil[pl.ds(first, COLS)],
                        fil[lax.rem(first + TILES - 1, TILES), :, 0],
                        fil[lax.rem(first + COLS, TILES), :, 0],
                        faces[pl.ds(first, COLS), :, 0],
                    )

                for c in range(COLS):
                    tile = first + lax.rem(y + c, COLS)
                    remote(
                        done.at[tile], out.at[my_levels, rows], out_send.at[0],
                        out_recv.at[0], polar_lat, tile,
                    ).start()

                    @pl.when(jnp.logical_and(is_edge, tile != lon))
                    def _():
                        remote(
                            done_x.at[tile], row_x.at[my_levels], ox_send.at[0], ox_recv.at[0],
                            beside_lat, tile,
                        ).start()

                    @pl.when(jnp.logical_and(is_edge, tile == lon))
                    def _():
                        pltpu.make_async_copy(
                            done_x.at[tile], row_x.at[my_levels], ox_recv.at[0]
                        ).start()

            over(RINGS, finish)

        to_left.wait_recv()
        to_right.wait_recv()

        def beyond(p):
            from_right = packed_r[...]
            if p:
                from_right = pltpu.roll(from_right, LANES - 8 * p, 1)
            from_left = pltpu.roll(packed_l[...], (LANES - 8 - 8 * p) % LANES, 1)
            return jnp.where(lane < LANES // 2, from_right, from_left)

        def east_of(x):
            near, far = (pltpu.roll(v, LANES - 1, 1) for v in x)
            last = lane == LANES - 1
            return jnp.where(last, far, near), jnp.where(last, near, far)

        def west_of(x):
            near, far = (pltpu.roll(v, 1, 1) for v in x)
            last = lane == 0
            return jnp.where(last, far, near), jnp.where(last, near, far)

        def north_of(x):
            return [pltpu.roll(v, WIDE - 1, 0) for v in x]

        def south_of(x):
            return [pltpu.roll(v, 1, 0) for v in x]

        kappa_e, speed_e, kappa_n, speed_n, open_m = (
            (ext[LEVELS + k, here], beyond(LEVELS + k)) for k in range(5)
        )

        def minus(kappa, speed):
            return [m * (-k - 0.5 * f) for m, k, f in zip(open_m, kappa, speed)]

        def plus(kappa, speed):
            return [m * (k - 0.5 * f) for m, k, f in zip(open_m, kappa, speed)]

        wide_faces = (
            [a * b for a, b in zip(minus(kappa_e, speed_e), east_of(open_m))],
            [-a * b for a, b in zip(open_m, west_of(plus(kappa_e, speed_e)))],
            [a * b for a, b in zip(minus(kappa_n, speed_n), north_of(open_m))],
            [-a * b for a, b in zip(open_m, south_of(plus(kappa_n, speed_n)))],
        )
        for k in range(4):
            for side in range(2):
                wide_coef[k, side] = wide_faces[k][side]

        def level(p):
            from_right = pltpu.roll(packed_r[...], LANES - 8 * p, 1)
            from_left = pltpu.roll(packed_l[...], LANES - 8 - 8 * p, 1)
            x = (ext[p, here], jnp.where(lane < LANES // 2, from_right, from_left))
            for _ in range(STEPS):
                new = list(x)
                for k, near in enumerate((east_of(x), west_of(x), north_of(x), south_of(x))):
                    for side in range(2):
                        new[side] = new[side] + wide_coef[k, side] * (x[side] - near[side])
                x = tuple(new)
            mid_out[p] = x[0][8 : 8 + ROWS]

        over(LEVELS, level)

        store = pltpu.make_async_copy(mid_out, out, store_sem.at[0])
        store.start()

        @pl.when(beside)
        def _():
            wait_bytes(coef.at[pl.ds(0, COLS - 1)], pass_send.at[0])
            wait_bytes(done, out_send.at[0])

            @pl.when(is_edge)
            def _():
                wait_bytes(strip.at[pl.ds(0, COLS - 1)], px_send.at[0])
                wait_bytes(done_x.at[pl.ds(0, TILES - 1)], ox_send.at[0])


        to_left.wait_send()
        to_right.wait_send()

        @pl.when(beside)
        def _():
            wait_bytes(row_x, ox_recv.at[0])

        store.wait()

    @pl.when(lat > 0)
    def _():
        to_south.wait_send()

    @pl.when(lat < LATS - 1)
    def _():
        to_north.wait_send()


def shards(cotangent, diff_east, diff_north, flow_east, flow_north, sea_mask, cutoff):
    wide, turn = tables()
    hbm = pl.BlockSpec(memory_space=pltpu.HBM)
    dma = pltpu.SemaphoreType.DMA

    def room(*shape):
        return pltpu.VMEM(shape, F32)

    table = pltpu.VMEM((2 * LANES, 2 * LANES), jnp.bfloat16)
    field, shared = pl.pallas_call(
        kernel,
        out_shape=[
            jax.ShapeDtypeStruct((LEVELS, ROWS, LANES), F32),
            jax.ShapeDtypeStruct((LEVELS, 8, LANES), F32),
        ],
        in_specs=[hbm] * 9,
        out_specs=[hbm, hbm],
        scratch_shapes=[
            pltpu.VMEM((ROWS, LANES), jnp.int32),
            pltpu.SMEM((ROWS,), jnp.int32),
            room(2 * LANES, 2 * LANES),
            table,
            table,
            room(72, 8, LANES),
            room(PLANES, EXT, LANES),
            room(BLOCKS, LEVELS, 2, 8, LANES),
            room(BLOCKS, 5, 2, 8, LANES),
            room(BLOCKS, 2, 8, LANES),
            room(PAIRS, 8, LANES),
            room(EXTRA, 8, LANES),
            room(TILES, 8, LANES),
            room(COLS, RINGS, EXTRA, 8, LANES),
            room(TILES, 4, 8, LANES),
            room(TILES, 2, 8, LANES),
            room(TILES, 2, 2, 8, LANES),
            room(TILES, 2, 2, 8, LANES),
            room(TILES, 2, 8, LANES),
            room(COLS, RINGS, 5, 2, 8, LANES),
            room(TILES, 4, 2, 8, LANES),
            room(2, 2 * LANES, LANES),
            room(2, 8, LANES),
            room(WIDE, LANES),
            room(WIDE, LANES),
            room(WIDE, LANES),
            room(4, 2, WIDE, LANES),
            room(LEVELS, ROWS, LANES),
            dma((9,)),
            dma((2,)), dma((2,)), dma((2,)), dma((2,)), dma((2,)), dma((1,)), dma((1,)), dma((1,)),
            dma((1,)), dma((RINGS,)), dma((1,)), dma((1,)), dma((1,)), dma((1,)), dma((1,)), dma((1,)),
            dma((1,)), dma((1,)), dma((1,)), dma((1,)), dma((1,)), dma((1,)), dma((1,)),
        ],
        compiler_params=pltpu.CompilerParams(
            collective_id=0, has_side_effects=True, vmem_limit_bytes=63 * 1024 * 1024
        ),
    )(
        cotangent, diff_east, diff_north, flow_east, flow_north, sea_mask, cutoff,
        jnp.asarray(wide), jnp.asarray(turn),
    )
    lat = lax.axis_index("lat")
    row = lax.broadcasted_iota(jnp.int32, field.shape, 1)
    taken = jnp.logical_or(
        jnp.logical_and(lat == 1, row < EDGE), jnp.logical_and(lat == LATS - 2, row >= ROWS - EDGE)
    )
    return jnp.where(taken, jnp.tile(shared, (1, ROWS // 8, 1)), field)


def solution(mesh):
    return jax.shard_map(
        shards,
        mesh=mesh,
        in_specs=(
            P(None, "lat", "lon"),
            P("lat", "lon"),
            P("lat", "lon"),
            P("lat", "lon"),
            P("lat", "lon"),
            P("lat", "lon"),
            P("lat"),
        ),
        out_specs=P(None, "lat", "lon"),
        check_vma=False,
    )
```

```python
import functools
import math

import jax
import jax.numpy as jnp
import numpy as np
from jax import lax
from jax.experimental import pallas as pl
from jax.experimental.pallas import tpu as pltpu
from jax.sharding import PartitionSpec as P

STEPS = 4
LEVELS = 8
ROWS = 64
LANES = 128
TILES = 32
NLON = TILES * LANES
BLOCKS = 8
PAIRS = 4
HALO = 16
EXT = ROWS + 2 * HALO
WIDE = ROWS + HALO
PLANES = LEVELS + 5
MASK = LEVELS + 4
EDGE = 4
LATS = 8
COLS = 4
RINGS = 8
EXTRA = 3

F32 = jnp.float32


def tables():
    n = np.arange(LANES)
    angle = 2 * np.pi * (np.outer(n, n) % LANES) / LANES
    cos, sin = np.cos(angle), np.sin(angle)
    wide = np.block([[cos, -sin], [sin, cos]])
    q = np.arange(8)[:, None, None]
    c = np.arange(4)[None, :, None]
    first = 2 * np.pi * ((q * (n[None, None, :] + LANES * c)) % NLON) / NLON
    r = np.arange(4)[:, None]
    second = 2 * np.pi * ((r * n[None, :]) % 512) / 512

    def spread(values):
        values = values.reshape(-1, 1, LANES)
        return np.broadcast_to(values, (values.shape[0], 8, LANES)).astype(np.float32)

    turn = np.concatenate(
        [spread(np.cos(first)), spread(np.sin(first)), spread(np.cos(second)), spread(np.sin(second))]
    )
    return wide.astype(np.float32), turn


def cadd(x, y):
    return x[0] + y[0], x[1] + y[1]


def csub(x, y):
    return x[0] - y[0], x[1] - y[1]


def quarter(x, sign):
    if sign < 0:
        return x[1], -x[0]
    return -x[1], x[0]


def dft4(x, sign):
    even, odd = cadd(x[0], x[2]), csub(x[0], x[2])
    even2, odd2 = cadd(x[1], x[3]), quarter(csub(x[1], x[3]), sign)
    return [cadd(even, even2), cadd(odd, odd2), csub(even, even2), csub(odd, odd2)]


def dft8(x, sign):
    even = dft4([x[0], x[2], x[4], x[6]], sign)
    odd = dft4([x[1], x[3], x[5], x[7]], sign)
    half = math.sqrt(0.5)

    def eighth(v):
        rot = quarter(v, sign)
        return (v[0] + rot[0]) * half, (v[1] + rot[1]) * half

    odd[1] = eighth(odd[1])
    odd[2] = quarter(odd[2], sign)
    odd[3] = quarter(eighth(odd[3]), sign)
    return [cadd(e, o) for e, o in zip(even, odd)] + [csub(e, o) for e, o in zip(even, odd)]


def cmul(x, cos, sin, sign):
    if sign < 0:
        return x[0] * cos + x[1] * sin, x[1] * cos - x[0] * sin
    return x[0] * cos - x[1] * sin, x[1] * cos + x[0] * sin


def split_dot(left, high_ref, low_ref):
    high = left.astype(jnp.bfloat16)
    low = (left - high.astype(F32)).astype(jnp.bfloat16)
    dot = functools.partial(jnp.dot, preferred_element_type=F32)
    return dot(high, high_ref[...]) + (dot(low, high_ref[...]) + dot(high, low_ref[...]))


def filter_circles(real, imag, kept, high_ref, low_ref, turn_ref):
    shape = (8, 4, 8, LANES)
    cos1 = turn_ref[0:32].reshape(shape)
    sin1 = turn_ref[32:64].reshape(shape)
    real, imag = real.reshape(shape), imag.reshape(shape)
    parts = dft8([(real[a], imag[a]) for a in range(8)], -1)
    parts = [cmul(parts[q], cos1[q], sin1[q], -1) for q in range(8)]
    real = jnp.stack([p[0] for p in parts])
    imag = jnp.stack([p[1] for p in parts])
    parts = dft4([(real[:, c], imag[:, c]) for c in range(4)], -1)
    parts = [parts[0]] + [
        cmul(parts[r], turn_ref[64 + r], turn_ref[68 + r], -1) for r in range(1, 4)
    ]
    real = jnp.concatenate([p[0] for p in parts]).reshape(256, LANES)
    imag = jnp.concatenate([p[1] for p in parts]).reshape(256, LANES)
    spec = split_dot(jnp.concatenate([real, imag], axis=1), high_ref, low_ref)
    real = spec[:, :LANES] * kept
    imag = spec[:, LANES:] * kept
    back = split_dot(jnp.concatenate([imag, real], axis=1), high_ref, low_ref)
    real = back[:, LANES:].reshape(4, 8, 8, LANES)
    imag = back[:, :LANES].reshape(4, 8, 8, LANES)
    parts = [(real[0], imag[0])] + [
        cmul((real[r], imag[r]), turn_ref[64 + r], turn_ref[68 + r], 1) for r in range(1, 4)
    ]
    parts = dft4(parts, 1)
    real = jnp.stack([p[0] for p in parts], axis=1)
    imag = jnp.stack([p[1] for p in parts], axis=1)
    parts = [cmul((real[q], imag[q]), cos1[q], sin1[q], 1) for q in range(8)]
    parts = dft8(parts, 1)
    real = jnp.concatenate([p[0] for p in parts])
    imag = jnp.concatenate([p[1] for p in parts])
    return real, imag


def iota(shape, dim):
    return lax.broadcasted_iota(jnp.int32, shape, dim)


def circle_step(x, coef):
    shape = (TILES * 4, 8, LANES)
    full = (TILES, 2, 2, 8, LANES)
    lane = iota(shape, 2)
    row = iota(full, 3)
    flat = x.reshape(shape)
    east = pltpu.roll(flat, LANES - 1, 2)
    east = jnp.where(lane == LANES - 1, jnp.concatenate([east[4:], east[:4]]), east)
    west = pltpu.roll(flat, 1, 2)
    west = jnp.where(lane == 0, jnp.concatenate([west[-4:], west[:-4]]), west)

    def across(turned, edge):
        turned = turned.reshape(full)
        other = jnp.stack([turned[:, :, 1], turned[:, :, 0]], axis=2)
        return jnp.where(row == edge, other, turned)

    up = across(pltpu.roll(flat, 7, 1), 7)
    down = across(pltpu.roll(flat, 1, 1), 0)
    total = x
    for k, near in enumerate((east.reshape(full), west.reshape(full), up, down)):
        total = total + coef[:, k : k + 1] * (x - near)
    return total


def last_step(cells, before, after, coef):
    x = cells[:, :, 0]
    rim = cells[:, :, 1]
    count = x.shape[0]
    lane = iota(x.shape, 3)
    row = iota(x.shape, 2)

    def turn(v, step, dim):
        flat = pltpu.roll(v.reshape(-1, 8, LANES), step % v.shape[dim], dim - 1)
        return flat.reshape(v.shape)

    east = turn(x, -1, 3)
    next_east = turn(jnp.concatenate([x[1:], after[None]]), -1, 3)
    east = jnp.where(lane == LANES - 1, next_east, east)
    west = turn(x, 1, 3)
    next_west = turn(jnp.concatenate([before[None], x[: count - 1]]), 1, 3)
    west = jnp.where(lane == 0, next_west, west)
    up = jnp.where(row == 7, turn(rim, -1, 2), turn(x, -1, 2))
    down = jnp.where(row == 0, turn(rim, 1, 2), turn(x, 1, 2))
    total = x
    for k, near in enumerate((east, west, up, down)):
        total = total + coef[:, k : k + 1] * (x - near)
    return total


def neighbour(x, step):
    shape = (x.size // (8 * LANES), 8, LANES)
    width = shape[0] // TILES
    lane = iota(shape, 2)
    turned = pltpu.roll(x.reshape(shape), step % LANES, 2)
    moved = jnp.concatenate([turned[-width * step :], turned[: -width * step]])
    edge = 0 if step > 0 else LANES - 1
    return jnp.where(lane == edge, moved, turned).reshape(x.shape)


def edge_step(x, coef, extra, coef_x):
    full = (TILES, 2, 8, LANES)
    row = iota(full, 2)
    own, rim = x[:, :, 0], x[:, :, 1]

    def turn(v, step):
        return pltpu.roll(v.reshape(-1, 8, LANES), step, 1).reshape(v.shape)

    up_own = jnp.where(row == 7, turn(rim, 7), turn(own, 7))
    down_own = jnp.where(row == 0, turn(rim, 1), turn(own, 1))
    up_rim = jnp.where(row == 7, turn(own, 7), turn(rim, 7))
    up_rim = jnp.where(row == 3, jnp.stack([turn(extra, 3), turn(extra, 7)], axis=1), up_rim)
    down_rim = jnp.where(row == 0, turn(own, 1), turn(rim, 1))
    down_rim = jnp.where(row == 4, jnp.stack([turn(extra, 1), turn(extra, 5)], axis=1), down_rim)
    row = iota(extra.shape, 1)
    up_x = jnp.where(row == 3, turn(rim[:, 0], 7), turn(extra, 7))
    up_x = jnp.where(row == 7, turn(rim[:, 1], 3), up_x)
    down_x = jnp.where(row == 0, turn(rim[:, 0], 5), turn(extra, 1))
    down_x = jnp.where(row == 4, turn(rim[:, 1], 1), down_x)

    up = jnp.stack([up_own, up_rim], axis=2)
    down = jnp.stack([down_own, down_rim], axis=2)
    total = x
    for k, near in enumerate((neighbour(x, -1), neighbour(x, 1), up, down)):
        total = total + coef[:, k : k + 1] * (x - near)
    total_x = extra
    for k, near in enumerate((neighbour(extra, -1), neighbour(extra, 1), up_x, down_x)):
        total_x = total_x + coef_x[:, k] * (extra - near)
    return total, total_x


def kernel(
    cot, diff_east_in, diff_north_in, flow_east_in, flow_north_in, sea_in, cutoff_in, wide_in,
    turn_in,
    out, row_x,
    sea, cutoff, wide_ref, high_ref, low_ref, turn_ref,
    ext, lam_src, coef_src, cut_src, extra_src, strip_src, extra, strip, faces_x, done_x,
    lam, fil, done, coef, faces, kept_ref, cuts_ref, packed, packed_l, packed_r, wide_coef, mid_out,
    load_sem, row_send, row_recv, col_send, col_recv, cut_send, cut_recv, in_send, in_recv,
    cf_send, cf_recv, pass_send, pass_recv, out_send, out_recv, ox_recv, store_sem, lx_send, lx_recv,
    sx_send, sx_recv, px_send, px_recv, ox_send,
):
    lon = lax.axis_index("lon")
    lat = lax.axis_index("lat")
    y = lax.rem(lon, 4)
    z = lon // 4
    first_band = lat < LATS // 2
    polar = jnp.logical_or(lat == 0, lat == LATS - 1)
    beside = jnp.logical_or(lat == 1, lat == LATS - 2)
    polar_lat = jnp.where(first_band, 0, LATS - 1)
    beside_lat = jnp.where(first_band, 1, LATS - 2)
    edge = jnp.where(first_band, BLOCKS - 1, 0)
    is_edge = jnp.logical_and(beside, z == edge)
    pair = y

    def owner_of(b, p):
        return beside_lat, COLS * b + p

    main = pl.ds(HALO, ROWS)
    plane_loads = [
        pltpu.make_async_copy(src, dst, load_sem.at[k])
        for k, (src, dst) in enumerate(
            (
                (sea_in, sea),
                (diff_east_in, ext.at[LEVELS, main]),
                (flow_east_in, ext.at[LEVELS + 1, main]),
                (diff_north_in, ext.at[LEVELS + 2, main]),
                (flow_north_in, ext.at[LEVELS + 3, main]),
                (cot, ext.at[pl.ds(0, LEVELS), main]),
            )
        )
    ]
    cut_load = pltpu.make_async_copy(cutoff_in, cutoff, load_sem.at[6])
    table_loads = [
        pltpu.make_async_copy(turn_in, turn_ref, load_sem.at[7]),
        pltpu.make_async_copy(wide_in, wide_ref, load_sem.at[8]),
    ]
    for load in plane_loads:
        load.start()

    @pl.when(polar)
    def _():
        cut_load.start()

    @pl.when(beside)
    def _():
        for load in table_loads:
            load.start()

    barrier = pltpu.get_barrier_semaphore()

    def at(to_lat, to_lon):
        return {"lon": to_lon, "lat": to_lat}

    def hail(to_lat, to_lon):
        pl.semaphore_signal(
            barrier, inc=1, device_id=at(to_lat, to_lon), device_id_type=pl.DeviceIdType.MESH
        )

    def remote(src, dst, send, recv, to_lat, to_lon):
        return pltpu.make_async_remote_copy(
            src_ref=src, dst_ref=dst, send_sem=send, recv_sem=recv,
            device_id=at(to_lat, to_lon), device_id_type=pl.DeviceIdType.MESH,
        )

    def wait_bytes(ref, sem):
        pltpu.make_async_copy(ref, ref, sem).wait()

    def over(count, body):
        def go(k, carry):
            body(k)
            return carry

        lax.fori_loop(0, count, go, 0)

    def far_first(i):
        return lax.rem(z + 4 + ((i + 1) // 2) * (1 - 2 * lax.rem(i, 2)), RINGS)

    right = lax.rem(lon + 1, TILES)
    left = lax.rem(lon + TILES - 1, TILES)

    @pl.when(polar)
    def _():
        def greet(i):
            b = far_first(i)
            for p in range(PAIRS):
                hail(*owner_of(b, p))

        over(BLOCKS, greet)

    @pl.when(beside)
    def _():
        def greet(i):
            for c in range(COLS):
                hail(polar_lat, COLS * far_first(i) + lax.rem(y + c, COLS))

        over(RINGS, greet)
        for c in range(1, COLS):
            hail(lat, COLS * z + lax.rem(y + c, COLS))

    @pl.when(beside)
    def _():
        for p in range(PAIRS):
            @pl.when(COLS * edge + p != lon)
            def _():
                hail(lat, COLS * edge + p)

    @pl.when(jnp.logical_not(polar))
    def _():
        hail(lat, left)
        hail(lat, right)

    @pl.when(lat > 0)
    def _():
        hail(lat - 1, lon)

    @pl.when(lat < LATS - 1)
    def _():
        hail(lat + 1, lon)

    for load in plane_loads:
        load.wait()
    ext[MASK, HALO : HALO + ROWS] = sea[...].astype(F32)
    sub = iota((LEVELS, 8, LANES), 1)

    def fill(b, tile):
        rows = 8 * tile
        lam_src[b, :, 0] = ext[0:LEVELS, rows : rows + 8]
        lam_src[b, :, 1] = jnp.where(
            sub < EDGE, ext[0:LEVELS, rows + 8 : rows + 16], ext[0:LEVELS, rows - 8 : rows]
        )

    def face_tiles(start, count):
        rows = pl.ds(pl.multiple_of(start, 8), 8 * count)
        mine = ext[MASK, rows]
        kappa_e, speed_e, kappa_n, speed_n = (ext[LEVELS + k, rows] for k in range(4))
        minus_n = mine * (-kappa_n - 0.5 * speed_n)
        plus_n = mine * (kappa_n - 0.5 * speed_n)
        planes = (
            mine * (-kappa_e - 0.5 * speed_e),
            mine * (kappa_e - 0.5 * speed_e),
            minus_n * pltpu.roll(mine, 8 * count - 1, 0),
            -mine * pltpu.roll(plus_n, 1, 0),
            mine,
        )
        return [plane.reshape(count, 8, LANES) for plane in planes]

    low = iota((1, 8, LANES), 1) < EDGE
    free = jnp.where(first_band, 0, 1)
    @pl.when(polar)
    def _():
        zeros = jnp.zeros((PLANES, 8, LANES), F32)
        ext[:, 0:8] = zeros
        ext[:, EXT - 8 : EXT] = zeros

        @pl.when(lat == 0)
        def _():
            ext[:, 8:16] = zeros
            for b in range(BLOCKS - 1):
                fill(b, b + 2)

        @pl.when(lat > 0)
        def _():
            ext[:, EXT - 16 : EXT - 8] = zeros
            for b in range(1, BLOCKS):
                fill(b, b + 2)

        for k, face in enumerate(face_tiles(jnp.where(first_band, 8, 16), BLOCKS + 1)):
            coef_src[pl.ds(free, BLOCKS - 1), k, 0] = face[1:8]
            coef_src[pl.ds(free, BLOCKS - 1), k, 1] = jnp.where(low, face[2:9], face[0:7])

        cut_load.wait()
        row = iota((8, LANES), 0)
        open_cut = jnp.full((8, LANES), float(NLON // 2), F32)
        cuts = [open_cut, open_cut]
        for b in range(BLOCKS):
            tile = open_cut
            for j in range(8):
                tile = jnp.where(row == j, cutoff[8 * b + j].astype(F32), tile)
            cuts.append(tile)
        cuts += [open_cut, open_cut]
        for b in range(BLOCKS):
            cut_src[b, 0] = cuts[b + 2]
            cut_src[b, 1] = jnp.where(row < EDGE, cuts[b + 3], cuts[b + 1])

    peers = jnp.where(polar, 1 + BLOCKS * PAIRS, 4)
    peers = peers + jnp.where(beside, TILES + COLS - 1, 0)
    peers = peers + jnp.where(is_edge, TILES - 1, 0)
    pl.semaphore_wait(barrier, peers)

    low_rows = ext.at[:, pl.ds(HALO, 8)]
    high_rows = ext.at[:, pl.ds(HALO + ROWS - 8, 8)]
    south_rows = ext.at[:, pl.ds(HALO - 8, 8)]
    north_rows = ext.at[:, pl.ds(HALO + ROWS, 8)]
    to_south = remote(low_rows, north_rows, row_send.at[0], row_recv.at[0], lat - 1, lon)
    to_north = remote(high_rows, south_rows, row_send.at[1], row_recv.at[1], lat + 1, lon)

    @pl.when(lat > 0)
    def _():
        to_south.start()

    @pl.when(lat < LATS - 1)
    def _():
        to_north.start()

    def wait_rows():
        @pl.when(lat < LATS - 1)
        def _():
            to_south.wait_recv()

        @pl.when(lat > 0)
        def _():
            to_north.wait_recv()

    @pl.when(polar)
    def _():
        def send_block(b):
            for p in range(PAIRS):
                remote(
                    lam_src.at[b, pl.ds(2 * p, 2)], lam.at[lon], in_send.at[0], in_recv.at[0],
                    *owner_of(b, p),
                ).start()

        def send_coef(b):
            remote(
                coef_src.at[b], coef.at[y, z], cf_send.at[0], cf_recv.at[z], *owner_of(b, y)
            ).start()

        def send_free(i):
            @pl.when(far_first(i) != edge)
            def _():
                send_coef(far_first(i))

        over(RINGS, lambda i: send_free(RINGS - 1 - i))
        pltpu.make_async_remote_copy(
            src_ref=cut_src.at[z], dst_ref=cuts_ref, send_sem=cut_send.at[0],
            recv_sem=cut_recv.at[0], device_id=at(beside_lat, lon),
            device_id_type=pl.DeviceIdType.MESH,
        ).start()

        wait_rows()
        def halves(low_from, high_from):
            lower = jnp.where(first_band, pltpu.roll(low_from, 4, 1), low_from)
            upper = jnp.where(first_band, high_from, pltpu.roll(high_from, 4, 1))
            return jnp.where(low, lower, upper)

        strips = []
        for k, face in enumerate(face_tiles(jnp.where(first_band, ROWS, 0), 4)):
            coef_src[edge, k, 0] = jnp.where(first_band, face[1], face[2])
            coef_src[edge, k, 1] = jnp.where(
                low[0], jnp.where(first_band, face[2], face[3]), jnp.where(first_band, face[0], face[1])
            )
            strips.append(jnp.where(first_band, face[2], face[1])[None])
        for j in range(EXTRA):
            strip_src[j] = halves(strips[2 * j], strips[min(2 * j + 1, 4)])[0]
        send_coef(edge)
        remote(
            strip_src, strip.at[y, z], sx_send.at[0], sx_recv.at[0], *owner_of(edge, y)
        ).start()

        @pl.when(lat == 0)
        def _():
            fill(BLOCKS - 1, BLOCKS + 1)

        @pl.when(lat > 0)
        def _():
            fill(0, 2)

        beyond_rows = pl.ds(pl.multiple_of(jnp.where(first_band, HALO + ROWS, HALO - 8), 8), 8)
        outside = ext[pl.ds(0, LEVELS), beyond_rows]
        for p in range(PAIRS):
            extra_src[p] = halves(outside[2 * p : 2 * p + 1], outside[2 * p + 1 : 2 * p + 2])[0]
            remote(
                extra_src.at[p], extra.at[lon], lx_send.at[0], lx_recv.at[0], *owner_of(edge, p)
            ).start()
        over(RINGS, lambda i: send_block(far_first(RINGS - 1 - i)))

        wait_bytes(cuts_ref, cut_send.at[0])

        wait_bytes(extra_src, lx_send.at[0])
        wait_bytes(strip_src, sx_send.at[0])
        wait_bytes(lam_src, in_send.at[0])
        wait_bytes(coef_src, cf_send.at[0])
        wait_bytes(out, out_recv.at[0])

    @pl.when(jnp.logical_not(polar))
    def _():
        wait_rows()
        here = slice(8, 8 + WIDE)
        lane = iota((WIDE, LANES), 1)
        total = jnp.zeros((WIDE, LANES), F32)
        for p in range(PLANES):
            v = ext[p, here]
            u = jnp.where(lane < EDGE, v, pltpu.roll(v, 2 * EDGE, 1))
            if p:
                u = pltpu.roll(u, 8 * p, 1)
            total = jnp.where((lane // 8) == p, u, total)
        packed[...] = total
        to_left = remote(packed, packed_r, col_send.at[0], col_recv.at[0], lat, left)
        to_right = remote(packed, packed_l, col_send.at[1], col_recv.at[1], lat, right)
        to_left.start()
        to_right.start()
        @pl.when(beside)
        def _():
            for load in table_loads:
                load.wait()
            high = wide_ref[...].astype(jnp.bfloat16)
            high_ref[...] = high
            low_ref[...] = (wide_ref[...] - high.astype(F32)).astype(jnp.bfloat16)

            def hand_on(t):
                ring = far_first(RINGS - 1 - t)
                wait_bytes(coef.at[y, ring], cf_recv.at[ring])
                for c in range(1, COLS):
                    remote(
                        coef.at[y, ring], coef.at[y, ring], pass_send.at[0], pass_recv.at[0],
                        lat, COLS * z + lax.rem(y + c, COLS),
                    ).start()

            over(RINGS, hand_on)

            @pl.when(is_edge)
            def _():
                wait_bytes(strip.at[y], sx_recv.at[0])
                for c in range(1, COLS):
                    remote(
                        strip.at[y], strip.at[y], px_send.at[0], px_recv.at[0],
                        lat, COLS * z + lax.rem(y + c, COLS),
                    ).start()

            wait_bytes(cuts_ref, cut_recv.at[0])
            cuts = cuts_ref[...].astype(jnp.int32)
            shape = (TILES, 8, LANES)
            wave = iota(shape, 0) + TILES * iota(shape, 2)
            wave = jnp.minimum(wave, NLON - wave)
            for half in range(2):
                kept_ref[half] = jnp.where(wave <= cuts[half][None], 1.0 / NLON, 0.0).astype(
                    F32
                ).reshape(2 * LANES, LANES)
            wait_bytes(lam, in_recv.at[0])

            @pl.when(is_edge)
            def _():
                wait_bytes(extra, lx_recv.at[0])

            def filtered():
                for half in range(2):
                    real, imag = filter_circles(
                        lam[:, 0, half], lam[:, 1, half], kept_ref[half], high_ref, low_ref,
                        turn_ref,
                    )
                    fil[:, 0, half] = real
                    fil[:, 1, half] = imag

            def step(s):
                filtered()

                @pl.when(s == 0)
                def _():
                    wait_bytes(coef.at[pl.ds(0, COLS - 1)], pass_recv.at[0])

                    def circle(k):
                        parts = [coef[c, :, k] for c in range(COLS)]
                        return jnp.stack(parts, axis=1).reshape(TILES, 2, 8, LANES)

                    mine = circle(4)
                    faces[:, 0] = circle(0) * neighbour(mine, -1)
                    faces[:, 1] = -mine * neighbour(circle(1), 1)
                    faces[:, 2] = circle(2)
                    faces[:, 3] = circle(3)

                @pl.when(jnp.logical_and(is_edge, s == 0))
                def _():
                    wait_bytes(strip.at[pl.ds(0, COLS - 1)], px_recv.at[0])

                    def circle(k):
                        parts = [strip[c, :, k // 2] for c in range(COLS)]
                        both = jnp.stack(parts, axis=1).reshape(TILES, 8, LANES)
                        turned = pltpu.roll(both, 4, 1)
                        lower = iota(both.shape, 1) < EDGE
                        if k % 2:
                            return jnp.where(lower, turned, both)
                        return jnp.where(lower, both, turned)

                    mine = circle(4)
                    faces_x[:, 0] = circle(0) * neighbour(mine, -1)
                    faces_x[:, 1] = -mine * neighbour(circle(1), 1)
                    faces_x[:, 2] = circle(2)
                    faces_x[:, 3] = circle(3)

                @pl.when(is_edge)
                def _():
                    lam[...], extra[...] = edge_step(
                        fil[...], faces[...], extra[...], faces_x[...]
                    )

                @pl.when(jnp.logical_not(is_edge))
                def _():
                    lam[...] = circle_step(fil[...], faces[...])

            over(STEPS - 1, step)
            filtered()

            my_levels = pl.ds(2 * pair, 2)
            rows = pl.ds(pl.multiple_of(8 * z, 8), 8)

            @pl.when(is_edge)
            def _():
                total, _ = edge_step(fil[...], faces[...], extra[...], faces_x[...])
                done[...] = total[:, :, 0]
                done_x[...] = total[:, :, 1]

            def finish(i):
                ring = far_first(RINGS - 1 - i)
                first = COLS * ring

                @pl.when(jnp.logical_not(is_edge))
                def _():
                    done[pl.ds(first, COLS)] = last_step(
                        fil[pl.ds(first, COLS)],
                        fil[lax.rem(first + TILES - 1, TILES), :, 0],
                        fil[lax.rem(first + COLS, TILES), :, 0],
                        faces[pl.ds(first, COLS), :, 0],
                    )

                for c in range(COLS):
                    tile = first + lax.rem(y + c, COLS)
                    remote(
                        done.at[tile], out.at[my_levels, rows], out_send.at[0],
                        out_recv.at[0], polar_lat, tile,
                    ).start()

                    @pl.when(jnp.logical_and(is_edge, tile != lon))
                    def _():
                        remote(
                            done_x.at[tile], row_x.at[my_levels], ox_send.at[0], ox_recv.at[0],
                            beside_lat, tile,
                        ).start()

                    @pl.when(jnp.logical_and(is_edge, tile == lon))
                    def _():
                        pltpu.make_async_copy(
                            done_x.at[tile], row_x.at[my_levels], ox_recv.at[0]
                        ).start()

            over(RINGS, finish)

        to_left.wait_recv()
        to_right.wait_recv()

        def beyond(p):
            from_right = packed_r[...]
            if p:
                from_right = pltpu.roll(from_right, LANES - 8 * p, 1)
            from_left = pltpu.roll(packed_l[...], (LANES - 8 - 8 * p) % LANES, 1)
            return jnp.where(lane < LANES // 2, from_right, from_left)

        def east_of(x):
            near, far = (pltpu.roll(v, LANES - 1, 1) for v in x)
            last = lane == LANES - 1
            return jnp.where(last, far, near), jnp.where(last, near, far)

        def west_of(x):
            near, far = (pltpu.roll(v, 1, 1) for v in x)
            last = lane == 0
            return jnp.where(last, far, near), jnp.where(last, near, far)

        def north_of(x):
            return [pltpu.roll(v, WIDE - 1, 0) for v in x]

        def south_of(x):
            return [pltpu.roll(v, 1, 0) for v in x]

        kappa_e, speed_e, kappa_n, speed_n, open_m = (
            (ext[LEVELS + k, here], beyond(LEVELS + k)) for k in range(5)
        )

        def minus(kappa, speed):
            return [m * (-k - 0.5 * f) for m, k, f in zip(open_m, kappa, speed)]

        def plus(kappa, speed):
            return [m * (k - 0.5 * f) for m, k, f in zip(open_m, kappa, speed)]

        wide_faces = (
            [a * b for a, b in zip(minus(kappa_e, speed_e), east_of(open_m))],
            [-a * b for a, b in zip(open_m, west_of(plus(kappa_e, speed_e)))],
            [a * b for a, b in zip(minus(kappa_n, speed_n), north_of(open_m))],
            [-a * b for a, b in zip(open_m, south_of(plus(kappa_n, speed_n)))],
        )
        for k in range(4):
            for side in range(2):
                wide_coef[k, side] = wide_faces[k][side]

        def level(p):
            from_right = pltpu.roll(packed_r[...], LANES - 8 * p, 1)
            from_left = pltpu.roll(packed_l[...], LANES - 8 - 8 * p, 1)
            x = (ext[p, here], jnp.where(lane < LANES // 2, from_right, from_left))
            for _ in range(STEPS):
                new = list(x)
                for k, near in enumerate((east_of(x), west_of(x), north_of(x), south_of(x))):
                    for side in range(2):
                        new[side] = new[side] + wide_coef[k, side] * (x[side] - near[side])
                x = tuple(new)
            mid_out[p] = x[0][8 : 8 + ROWS]

        over(LEVELS, level)

        store = pltpu.make_async_copy(mid_out, out, store_sem.at[0])
        store.start()

        @pl.when(beside)
        def _():
            wait_bytes(coef.at[pl.ds(0, COLS - 1)], pass_send.at[0])
            wait_bytes(done, out_send.at[0])

            @pl.when(is_edge)
            def _():
                wait_bytes(strip.at[pl.ds(0, COLS - 1)], px_send.at[0])
                wait_bytes(done_x.at[pl.ds(0, TILES - 1)], ox_send.at[0])


        to_left.wait_send()
        to_right.wait_send()

        @pl.when(beside)
        def _():
            wait_bytes(row_x, ox_recv.at[0])

        store.wait()

    @pl.when(lat > 0)
    def _():
        to_south.wait_send()

    @pl.when(lat < LATS - 1)
    def _():
        to_north.wait_send()


def shards(cotangent, diff_east, diff_north, flow_east, flow_north, sea_mask, cutoff):
    wide, turn = tables()
    hbm = pl.BlockSpec(memory_space=pltpu.HBM)
    dma = pltpu.SemaphoreType.DMA

    def room(*shape):
        return pltpu.VMEM(shape, F32)

    table = pltpu.VMEM((2 * LANES, 2 * LANES), jnp.bfloat16)
    field, shared = pl.pallas_call(
        kernel,
        out_shape=[
            jax.ShapeDtypeStruct((LEVELS, ROWS, LANES), F32),
            jax.ShapeDtypeStruct((LEVELS, 8, LANES), F32),
        ],
        in_specs=[hbm] * 9,
        out_specs=[hbm, hbm],
        scratch_shapes=[
            pltpu.VMEM((ROWS, LANES), jnp.int32),
            pltpu.SMEM((ROWS,), jnp.int32),
            room(2 * LANES, 2 * LANES),
            table,
            table,
            room(72, 8, LANES),
            room(PLANES, EXT, LANES),
            room(BLOCKS, LEVELS, 2, 8, LANES),
            room(BLOCKS, 5, 2, 8, LANES),
            room(BLOCKS, 2, 8, LANES),
            room(PAIRS, 8, LANES),
            room(EXTRA, 8, LANES),
            room(TILES, 8, LANES),
            room(COLS, RINGS, EXTRA, 8, LANES),
            room(TILES, 4, 8, LANES),
            room(TILES, 2, 8, LANES),
            room(TILES, 2, 2, 8, LANES),
            room(TILES, 2, 2, 8, LANES),
            room(TILES, 2, 8, LANES),
            room(COLS, RINGS, 5, 2, 8, LANES),
            room(TILES, 4, 2, 8, LANES),
            room(2, 2 * LANES, LANES),
            room(2, 8, LANES),
            room(WIDE, LANES),
            room(WIDE, LANES),
            room(WIDE, LANES),
            room(4, 2, WIDE, LANES),
            room(LEVELS, ROWS, LANES),
            dma((9,)),
            dma((2,)), dma((2,)), dma((2,)), dma((2,)), dma((2,)), dma((1,)), dma((1,)), dma((1,)),
            dma((1,)), dma((RINGS,)), dma((1,)), dma((1,)), dma((1,)), dma((1,)), dma((1,)), dma((1,)),
            dma((1,)), dma((1,)), dma((1,)), dma((1,)), dma((1,)), dma((1,)), dma((1,)),
        ],
        compiler_params=pltpu.CompilerParams(
            collective_id=0, has_side_effects=True, vmem_limit_bytes=63 * 1024 * 1024
        ),
    )(
        cotangent, diff_east, diff_north, flow_east, flow_north, sea_mask, cutoff,
        jnp.asarray(wide), jnp.asarray(turn),
    )
    lat = lax.axis_index("lat")
    row = lax.broadcasted_iota(jnp.int32, field.shape, 1)
    taken = jnp.logical_or(
        jnp.logical_and(lat == 1, row < EDGE), jnp.logical_and(lat == LATS - 2, row >= ROWS - EDGE)
    )
    return jnp.where(taken, jnp.tile(shared, (1, ROWS // 8, 1)), field)


def solution(mesh):
    return jax.shard_map(
        shards,
        mesh=mesh,
        in_specs=(
            P(None, "lat", "lon"),
            P("lat", "lon"),
            P("lat", "lon"),
            P("lat", "lon"),
            P("lat", "lon"),
            P("lat", "lon"),
            P("lat"),
        ),
        out_specs=P(None, "lat", "lon"),
        check_vma=False,
    )
```

```python
import functools
import math

import jax
import jax.numpy as jnp
import numpy as np
from jax import lax
from jax.experimental import pallas as pl
from jax.experimental.pallas import tpu as pltpu
from jax.sharding import PartitionSpec as P

STEPS = 4
LEVELS = 8
ROWS = 64
LANES = 128
TILES = 32
NLON = TILES * LANES
BLOCKS = 8
PAIRS = 4
HALO = 16
EXT = ROWS + 2 * HALO
WIDE = ROWS + HALO
PLANES = LEVELS + 5
MASK = LEVELS + 4
EDGE = 4
LATS = 8
COLS = 4
RINGS = 8
EXTRA = 3

F32 = jnp.float32


def tables():
    n = np.arange(LANES)
    angle = 2 * np.pi * (np.outer(n, n) % LANES) / LANES
    cos, sin = np.cos(angle), np.sin(angle)
    wide = np.block([[cos, -sin], [sin, cos]])
    q = np.arange(8)[:, None, None]
    c = np.arange(4)[None, :, None]
    first = 2 * np.pi * ((q * (n[None, None, :] + LANES * c)) % NLON) / NLON
    r = np.arange(4)[:, None]
    second = 2 * np.pi * ((r * n[None, :]) % 512) / 512

    def spread(values):
        values = values.reshape(-1, 1, LANES)
        return np.broadcast_to(values, (values.shape[0], 8, LANES)).astype(np.float32)

    turn = np.concatenate(
        [spread(np.cos(first)), spread(np.sin(first)), spread(np.cos(second)), spread(np.sin(second))]
    )
    return wide.astype(np.float32), turn


def cadd(x, y):
    return x[0] + y[0], x[1] + y[1]


def csub(x, y):
    return x[0] - y[0], x[1] - y[1]


def quarter(x, sign):
    if sign < 0:
        return x[1], -x[0]
    return -x[1], x[0]


def dft4(x, sign):
    even, odd = cadd(x[0], x[2]), csub(x[0], x[2])
    even2, odd2 = cadd(x[1], x[3]), quarter(csub(x[1], x[3]), sign)
    return [cadd(even, even2), cadd(odd, odd2), csub(even, even2), csub(odd, odd2)]


def dft8(x, sign):
    even = dft4([x[0], x[2], x[4], x[6]], sign)
    odd = dft4([x[1], x[3], x[5], x[7]], sign)
    half = math.sqrt(0.5)

    def eighth(v):
        rot = quarter(v, sign)
        return (v[0] + rot[0]) * half, (v[1] + rot[1]) * half

    odd[1] = eighth(odd[1])
    odd[2] = quarter(odd[2], sign)
    odd[3] = quarter(eighth(odd[3]), sign)
    return [cadd(e, o) for e, o in zip(even, odd)] + [csub(e, o) for e, o in zip(even, odd)]


def cmul(x, cos, sin, sign):
    if sign < 0:
        return x[0] * cos + x[1] * sin, x[1] * cos - x[0] * sin
    return x[0] * cos - x[1] * sin, x[1] * cos + x[0] * sin


def split_dot(left, high_ref, low_ref):
    high = left.astype(jnp.bfloat16)
    low = (left - high.astype(F32)).astype(jnp.bfloat16)
    dot = functools.partial(jnp.dot, preferred_element_type=F32)
    return dot(high, high_ref[...]) + (dot(low, high_ref[...]) + dot(high, low_ref[...]))


def filter_circles(real, imag, kept, high_ref, low_ref, turn_ref):
    shape = (8, 4, 8, LANES)
    cos1 = turn_ref[0:32].reshape(shape)
    sin1 = turn_ref[32:64].reshape(shape)
    real, imag = real.reshape(shape), imag.reshape(shape)
    parts = dft8([(real[a], imag[a]) for a in range(8)], -1)
    parts = [cmul(parts[q], cos1[q], sin1[q], -1) for q in range(8)]
    real = jnp.stack([p[0] for p in parts])
    imag = jnp.stack([p[1] for p in parts])
    parts = dft4([(real[:, c], imag[:, c]) for c in range(4)], -1)
    parts = [parts[0]] + [
        cmul(parts[r], turn_ref[64 + r], turn_ref[68 + r], -1) for r in range(1, 4)
    ]
    real = jnp.concatenate([p[0] for p in parts]).reshape(256, LANES)
    imag = jnp.concatenate([p[1] for p in parts]).reshape(256, LANES)
    spec = split_dot(jnp.concatenate([real, imag], axis=1), high_ref, low_ref)
    real = spec[:, :LANES] * kept
    imag = spec[:, LANES:] * kept
    back = split_dot(jnp.concatenate([imag, real], axis=1), high_ref, low_ref)
    real = back[:, LANES:].reshape(4, 8, 8, LANES)
    imag = back[:, :LANES].reshape(4, 8, 8, LANES)
    parts = [(real[0], imag[0])] + [
        cmul((real[r], imag[r]), turn_ref[64 + r], turn_ref[68 + r], 1) for r in range(1, 4)
    ]
    parts = dft4(parts, 1)
    real = jnp.stack([p[0] for p in parts], axis=1)
    imag = jnp.stack([p[1] for p in parts], axis=1)
    parts = [cmul((real[q], imag[q]), cos1[q], sin1[q], 1) for q in range(8)]
    parts = dft8(parts, 1)
    real = jnp.concatenate([p[0] for p in parts])
    imag = jnp.concatenate([p[1] for p in parts])
    return real, imag


def iota(shape, dim):
    return lax.broadcasted_iota(jnp.int32, shape, dim)


def circle_step(x, coef):
    shape = (TILES * 4, 8, LANES)
    full = (TILES, 2, 2, 8, LANES)
    lane = iota(shape, 2)
    row = iota(full, 3)
    flat = x.reshape(shape)
    east = pltpu.roll(flat, LANES - 1, 2)
    east = jnp.where(lane == LANES - 1, jnp.concatenate([east[4:], east[:4]]), east)
    west = pltpu.roll(flat, 1, 2)
    west = jnp.where(lane == 0, jnp.concatenate([west[-4:], west[:-4]]), west)

    def across(turned, edge):
        turned = turned.reshape(full)
        other = jnp.stack([turned[:, :, 1], turned[:, :, 0]], axis=2)
        return jnp.where(row == edge, other, turned)

    up = across(pltpu.roll(flat, 7, 1), 7)
    down = across(pltpu.roll(flat, 1, 1), 0)
    total = x
    for k, near in enumerate((east.reshape(full), west.reshape(full), up, down)):
        total = total + coef[:, k : k + 1] * (x - near)
    return total


def last_step(cells, before, after, coef):
    x = cells[:, :, 0]
    rim = cells[:, :, 1]
    count = x.shape[0]
    lane = iota(x.shape, 3)
    row = iota(x.shape, 2)

    def turn(v, step, dim):
        flat = pltpu.roll(v.reshape(-1, 8, LANES), step % v.shape[dim], dim - 1)
        return flat.reshape(v.shape)

    east = turn(x, -1, 3)
    next_east = turn(jnp.concatenate([x[1:], after[None]]), -1, 3)
    east = jnp.where(lane == LANES - 1, next_east, east)
    west = turn(x, 1, 3)
    next_west = turn(jnp.concatenate([before[None], x[: count - 1]]), 1, 3)
    west = jnp.where(lane == 0, next_west, west)
    up = jnp.where(row == 7, turn(rim, -1, 2), turn(x, -1, 2))
    down = jnp.where(row == 0, turn(rim, 1, 2), turn(x, 1, 2))
    total = x
    for k, near in enumerate((east, west, up, down)):
        total = total + coef[:, k : k + 1] * (x - near)
    return total


def neighbour(x, step):
    shape = (x.size // (8 * LANES), 8, LANES)
    width = shape[0] // TILES
    lane = iota(shape, 2)
    turned = pltpu.roll(x.reshape(shape), step % LANES, 2)
    moved = jnp.concatenate([turned[-width * step :], turned[: -width * step]])
    edge = 0 if step > 0 else LANES - 1
    return jnp.where(lane == edge, moved, turned).reshape(x.shape)


def edge_step(x, coef, extra, coef_x):
    full = (TILES, 2, 8, LANES)
    row = iota(full, 2)
    own, rim = x[:, :, 0], x[:, :, 1]

    def turn(v, step):
        return pltpu.roll(v.reshape(-1, 8, LANES), step, 1).reshape(v.shape)

    up_own = jnp.where(row == 7, turn(rim, 7), turn(own, 7))
    down_own = jnp.where(row == 0, turn(rim, 1), turn(own, 1))
    up_rim = jnp.where(row == 7, turn(own, 7), turn(rim, 7))
    up_rim = jnp.where(row == 3, jnp.stack([turn(extra, 3), turn(extra, 7)], axis=1), up_rim)
    down_rim = jnp.where(row == 0, turn(own, 1), turn(rim, 1))
    down_rim = jnp.where(row == 4, jnp.stack([turn(extra, 1), turn(extra, 5)], axis=1), down_rim)
    row = iota(extra.shape, 1)
    up_x = jnp.where(row == 3, turn(rim[:, 0], 7), turn(extra, 7))
    up_x = jnp.where(row == 7, turn(rim[:, 1], 3), up_x)
    down_x = jnp.where(row == 0, turn(rim[:, 0], 5), turn(extra, 1))
    down_x = jnp.where(row == 4, turn(rim[:, 1], 1), down_x)

    up = jnp.stack([up_own, up_rim], axis=2)
    down = jnp.stack([down_own, down_rim], axis=2)
    total = x
    for k, near in enumerate((neighbour(x, -1), neighbour(x, 1), up, down)):
        total = total + coef[:, k : k + 1] * (x - near)
    total_x = extra
    for k, near in enumerate((neighbour(extra, -1), neighbour(extra, 1), up_x, down_x)):
        total_x = total_x + coef_x[:, k] * (extra - near)
    return total, total_x


def kernel(
    cot, diff_east_in, diff_north_in, flow_east_in, flow_north_in, sea_in, cutoff_in, wide_in,
    turn_in,
    out, row_x,
    sea, cutoff, wide_ref, high_ref, low_ref, turn_ref,
    ext, lam_src, coef_src, cut_src, extra_src, strip_src, extra, strip, faces_x, done_x,
    lam, fil, done, coef, faces, kept_ref, cuts_ref, packed, packed_l, packed_r, wide_coef, mid_out,
    load_sem, row_send, row_recv, col_send, col_recv, cut_send, cut_recv, in_send, in_recv,
    cf_send, cf_recv, pass_send, pass_recv, out_send, out_recv, ox_recv, store_sem, lx_send, lx_recv,
    sx_send, sx_recv, px_send, px_recv, ox_send,
):
    lon = lax.axis_index("lon")
    lat = lax.axis_index("lat")
    y = lax.rem(lon, 4)
    z = lon // 4
    first_band = lat < LATS // 2
    polar = jnp.logical_or(lat == 0, lat == LATS - 1)
    beside = jnp.logical_or(lat == 1, lat == LATS - 2)
    polar_lat = jnp.where(first_band, 0, LATS - 1)
    beside_lat = jnp.where(first_band, 1, LATS - 2)
    edge = jnp.where(first_band, BLOCKS - 1, 0)

    def flip(b):
        return jnp.where(first_band, b, BLOCKS - 1 - b)

    is_edge = jnp.logical_and(beside, z == BLOCKS - 1)
    pair = y

    def owner_of(b, p):
        return beside_lat, COLS * flip(b) + p

    main = pl.ds(HALO, ROWS)
    plane_loads = [
        pltpu.make_async_copy(src, dst, load_sem.at[k])
        for k, (src, dst) in enumerate(
            (
                (sea_in, sea),
                (diff_east_in, ext.at[LEVELS, main]),
                (flow_east_in, ext.at[LEVELS + 1, main]),
                (diff_north_in, ext.at[LEVELS + 2, main]),
                (flow_north_in, ext.at[LEVELS + 3, main]),
                (cot, ext.at[pl.ds(0, LEVELS), main]),
            )
        )
    ]
    cut_load = pltpu.make_async_copy(cutoff_in, cutoff, load_sem.at[6])
    table_loads = [
        pltpu.make_async_copy(turn_in, turn_ref, load_sem.at[7]),
        pltpu.make_async_copy(wide_in, wide_ref, load_sem.at[8]),
    ]
    for load in plane_loads:
        load.start()

    @pl.when(polar)
    def _():
        cut_load.start()

    @pl.when(beside)
    def _():
        for load in table_loads:
            load.start()

    barrier = pltpu.get_barrier_semaphore()

    def at(to_lat, to_lon):
        return {"lon": to_lon, "lat": to_lat}

    def hail(to_lat, to_lon):
        pl.semaphore_signal(
            barrier, inc=1, device_id=at(to_lat, to_lon), device_id_type=pl.DeviceIdType.MESH
        )

    def remote(src, dst, send, recv, to_lat, to_lon):
        return pltpu.make_async_remote_copy(
            src_ref=src, dst_ref=dst, send_sem=send, recv_sem=recv,
            device_id=at(to_lat, to_lon), device_id_type=pl.DeviceIdType.MESH,
        )

    def wait_bytes(ref, sem):
        pltpu.make_async_copy(ref, ref, sem).wait()

    def over(count, body):
        def go(k, carry):
            body(k)
            return carry

        lax.fori_loop(0, count, go, 0)

    def far_first(i):
        return lax.rem(z + 4 + ((i + 1) // 2) * (1 - 2 * lax.rem(i, 2)), RINGS)

    right = lax.rem(lon + 1, TILES)
    left = lax.rem(lon + TILES - 1, TILES)

    @pl.when(polar)
    def _():
        def greet(i):
            b = flip(far_first(i))
            for p in range(PAIRS):
                hail(*owner_of(b, p))

        over(BLOCKS, greet)

    @pl.when(beside)
    def _():
        def greet(i):
            for c in range(COLS):
                hail(polar_lat, COLS * far_first(i) + lax.rem(y + c, COLS))

        over(RINGS, greet)
        for c in range(1, COLS):
            hail(lat, COLS * z + lax.rem(y + c, COLS))

    @pl.when(beside)
    def _():
        for p in range(PAIRS):
            @pl.when(COLS * (BLOCKS - 1) + p != lon)
            def _():
                hail(lat, COLS * (BLOCKS - 1) + p)

    @pl.when(jnp.logical_not(polar))
    def _():
        hail(lat, left)
        hail(lat, right)

    @pl.when(lat > 0)
    def _():
        hail(lat - 1, lon)

    @pl.when(lat < LATS - 1)
    def _():
        hail(lat + 1, lon)

    for load in plane_loads:
        load.wait()
    ext[MASK, HALO : HALO + ROWS] = sea[...].astype(F32)
    sub = iota((LEVELS, 8, LANES), 1)

    def fill(b, tile):
        rows = 8 * tile
        lam_src[b, :, 0] = ext[0:LEVELS, rows : rows + 8]
        lam_src[b, :, 1] = jnp.where(
            sub < EDGE, ext[0:LEVELS, rows + 8 : rows + 16], ext[0:LEVELS, rows - 8 : rows]
        )

    def face_tiles(start, count):
        rows = pl.ds(pl.multiple_of(start, 8), 8 * count)
        mine = ext[MASK, rows]
        kappa_e, speed_e, kappa_n, speed_n = (ext[LEVELS + k, rows] for k in range(4))
        minus_n = mine * (-kappa_n - 0.5 * speed_n)
        plus_n = mine * (kappa_n - 0.5 * speed_n)
        planes = (
            mine * (-kappa_e - 0.5 * speed_e),
            mine * (kappa_e - 0.5 * speed_e),
            minus_n * pltpu.roll(mine, 8 * count - 1, 0),
            -mine * pltpu.roll(plus_n, 1, 0),
            mine,
        )
        return [plane.reshape(count, 8, LANES) for plane in planes]

    low = iota((1, 8, LANES), 1) < EDGE
    free = jnp.where(first_band, 0, 1)
    @pl.when(polar)
    def _():
        zeros = jnp.zeros((PLANES, 8, LANES), F32)
        ext[:, 0:8] = zeros
        ext[:, EXT - 8 : EXT] = zeros

        @pl.when(lat == 0)
        def _():
            ext[:, 8:16] = zeros
            for b in range(BLOCKS - 1):
                fill(b, b + 2)

        @pl.when(lat > 0)
        def _():
            ext[:, EXT - 16 : EXT - 8] = zeros
            for b in range(1, BLOCKS):
                fill(b, b + 2)

        for k, face in enumerate(face_tiles(jnp.where(first_band, 8, 16), BLOCKS + 1)):
            coef_src[pl.ds(free, BLOCKS - 1), k, 0] = face[1:8]
            coef_src[pl.ds(free, BLOCKS - 1), k, 1] = jnp.where(low, face[2:9], face[0:7])

        cut_load.wait()
        row = iota((8, LANES), 0)
        open_cut = jnp.full((8, LANES), float(NLON // 2), F32)
        cuts = [open_cut, open_cut]
        for b in range(BLOCKS):
            tile = open_cut
            for j in range(8):
                tile = jnp.where(row == j, cutoff[8 * b + j].astype(F32), tile)
            cuts.append(tile)
        cuts += [open_cut, open_cut]
        for b in range(BLOCKS):
            cut_src[b, 0] = cuts[b + 2]
            cut_src[b, 1] = jnp.where(row < EDGE, cuts[b + 3], cuts[b + 1])

    peers = jnp.where(polar, 1 + BLOCKS * PAIRS, 4)
    peers = peers + jnp.where(beside, TILES + COLS - 1, 0)
    peers = peers + jnp.where(is_edge, TILES - 1, 0)
    pl.semaphore_wait(barrier, peers)

    low_rows = ext.at[:, pl.ds(HALO, 8)]
    high_rows = ext.at[:, pl.ds(HALO + ROWS - 8, 8)]
    south_rows = ext.at[:, pl.ds(HALO - 8, 8)]
    north_rows = ext.at[:, pl.ds(HALO + ROWS, 8)]
    to_south = remote(low_rows, north_rows, row_send.at[0], row_recv.at[0], lat - 1, lon)
    to_north = remote(high_rows, south_rows, row_send.at[1], row_recv.at[1], lat + 1, lon)

    @pl.when(lat > 0)
    def _():
        to_south.start()

    @pl.when(lat < LATS - 1)
    def _():
        to_north.start()

    def wait_rows():
        @pl.when(lat < LATS - 1)
        def _():
            to_south.wait_recv()

        @pl.when(lat > 0)
        def _():
            to_north.wait_recv()

    @pl.when(polar)
    def _():
        def send_block(b):
            for p in range(PAIRS):
                remote(
                    lam_src.at[b, pl.ds(2 * p, 2)], lam.at[lon], in_send.at[0], in_recv.at[0],
                    *owner_of(b, p),
                ).start()

        def send_coef(b):
            remote(
                coef_src.at[b], coef.at[y, z], cf_send.at[0], cf_recv.at[z], *owner_of(b, y)
            ).start()

        def send_free(i):
            b = flip(far_first(i))

            @pl.when(b != edge)
            def _():
                send_coef(b)

        over(RINGS, lambda i: send_free(RINGS - 1 - i))
        pltpu.make_async_remote_copy(
            src_ref=cut_src.at[flip(z)], dst_ref=cuts_ref, send_sem=cut_send.at[0],
            recv_sem=cut_recv.at[0], device_id=at(beside_lat, lon),
            device_id_type=pl.DeviceIdType.MESH,
        ).start()

        wait_rows()
        def halves(low_from, high_from):
            lower = jnp.where(first_band, pltpu.roll(low_from, 4, 1), low_from)
            upper = jnp.where(first_band, high_from, pltpu.roll(high_from, 4, 1))
            return jnp.where(low, lower, upper)

        strips = []
        for k, face in enumerate(face_tiles(jnp.where(first_band, ROWS, 0), 4)):
            coef_src[edge, k, 0] = jnp.where(first_band, face[1], face[2])
            coef_src[edge, k, 1] = jnp.where(
                low[0], jnp.where(first_band, face[2], face[3]), jnp.where(first_band, face[0], face[1])
            )
            strips.append(jnp.where(first_band, face[2], face[1])[None])
        for j in range(EXTRA):
            strip_src[j] = halves(strips[2 * j], strips[min(2 * j + 1, 4)])[0]
        send_coef(edge)
        remote(
            strip_src, strip.at[y, z], sx_send.at[0], sx_recv.at[0], *owner_of(edge, y)
        ).start()

        @pl.when(lat == 0)
        def _():
            fill(BLOCKS - 1, BLOCKS + 1)

        @pl.when(lat > 0)
        def _():
            fill(0, 2)

        beyond_rows = pl.ds(pl.multiple_of(jnp.where(first_band, HALO + ROWS, HALO - 8), 8), 8)
        outside = ext[pl.ds(0, LEVELS), beyond_rows]
        for p in range(PAIRS):
            extra_src[p] = halves(outside[2 * p : 2 * p + 1], outside[2 * p + 1 : 2 * p + 2])[0]
            remote(
                extra_src.at[p], extra.at[lon], lx_send.at[0], lx_recv.at[0], *owner_of(edge, p)
            ).start()
        over(RINGS, lambda i: send_block(flip(far_first(RINGS - 1 - i))))

        wait_bytes(cuts_ref, cut_send.at[0])

        wait_bytes(extra_src, lx_send.at[0])
        wait_bytes(strip_src, sx_send.at[0])
        wait_bytes(lam_src, in_send.at[0])
        wait_bytes(coef_src, cf_send.at[0])
        wait_bytes(out, out_recv.at[0])

    @pl.when(jnp.logical_not(polar))
    def _():
        wait_rows()
        here = slice(8, 8 + WIDE)
        lane = iota((WIDE, LANES), 1)
        total = jnp.zeros((WIDE, LANES), F32)
        for p in range(PLANES):
            v = ext[p, here]
            u = jnp.where(lane < EDGE, v, pltpu.roll(v, 2 * EDGE, 1))
            if p:
                u = pltpu.roll(u, 8 * p, 1)
            total = jnp.where((lane // 8) == p, u, total)
        packed[...] = total
        to_left = remote(packed, packed_r, col_send.at[0], col_recv.at[0], lat, left)
        to_right = remote(packed, packed_l, col_send.at[1], col_recv.at[1], lat, right)
        to_left.start()
        to_right.start()
        @pl.when(beside)
        def _():
            for load in table_loads:
                load.wait()
            high = wide_ref[...].astype(jnp.bfloat16)
            high_ref[...] = high
            low_ref[...] = (wide_ref[...] - high.astype(F32)).astype(jnp.bfloat16)

            def hand_on(t):
                ring = far_first(RINGS - 1 - t)
                wait_bytes(coef.at[y, ring], cf_recv.at[ring])
                for c in range(1, COLS):
                    remote(
                        coef.at[y, ring], coef.at[y, ring], pass_send.at[0], pass_recv.at[0],
                        lat, COLS * z + lax.rem(y + c, COLS),
                    ).start()

            over(RINGS, hand_on)

            @pl.when(is_edge)
            def _():
                wait_bytes(strip.at[y], sx_recv.at[0])
                for c in range(1, COLS):
                    remote(
                        strip.at[y], strip.at[y], px_send.at[0], px_recv.at[0],
                        lat, COLS * z + lax.rem(y + c, COLS),
                    ).start()

            wait_bytes(cuts_ref, cut_recv.at[0])
            cuts = cuts_ref[...].astype(jnp.int32)
            shape = (TILES, 8, LANES)
            wave = iota(shape, 0) + TILES * iota(shape, 2)
            wave = jnp.minimum(wave, NLON - wave)
            for half in range(2):
                kept_ref[half] = jnp.where(wave <= cuts[half][None], 1.0 / NLON, 0.0).astype(
                    F32
                ).reshape(2 * LANES, LANES)
            wait_bytes(lam, in_recv.at[0])

            @pl.when(is_edge)
            def _():
                wait_bytes(extra, lx_recv.at[0])

            def filtered():
                for half in range(2):
                    real, imag = filter_circles(
                        lam[:, 0, half], lam[:, 1, half], kept_ref[half], high_ref, low_ref,
                        turn_ref,
                    )
                    fil[:, 0, half] = real
                    fil[:, 1, half] = imag

            def step(s):
                filtered()

                @pl.when(s == 0)
                def _():
                    wait_bytes(coef.at[pl.ds(0, COLS - 1)], pass_recv.at[0])

                    def circle(k):
                        parts = [coef[c, :, k] for c in range(COLS)]
                        return jnp.stack(parts, axis=1).reshape(TILES, 2, 8, LANES)

                    mine = circle(4)
                    faces[:, 0] = circle(0) * neighbour(mine, -1)
                    faces[:, 1] = -mine * neighbour(circle(1), 1)
                    faces[:, 2] = circle(2)
                    faces[:, 3] = circle(3)

                @pl.when(jnp.logical_and(is_edge, s == 0))
                def _():
                    wait_bytes(strip.at[pl.ds(0, COLS - 1)], px_recv.at[0])

                    def circle(k):
                        parts = [strip[c, :, k // 2] for c in range(COLS)]
                        both = jnp.stack(parts, axis=1).reshape(TILES, 8, LANES)
                        turned = pltpu.roll(both, 4, 1)
                        lower = iota(both.shape, 1) < EDGE
                        if k % 2:
                            return jnp.where(lower, turned, both)
                        return jnp.where(lower, both, turned)

                    mine = circle(4)
                    faces_x[:, 0] = circle(0) * neighbour(mine, -1)
                    faces_x[:, 1] = -mine * neighbour(circle(1), 1)
                    faces_x[:, 2] = circle(2)
                    faces_x[:, 3] = circle(3)

                @pl.when(is_edge)
                def _():
                    lam[...], extra[...] = edge_step(
                        fil[...], faces[...], extra[...], faces_x[...]
                    )

                @pl.when(jnp.logical_not(is_edge))
                def _():
                    lam[...] = circle_step(fil[...], faces[...])

            over(STEPS - 1, step)
            filtered()

            my_levels = pl.ds(2 * pair, 2)
            rows = pl.ds(pl.multiple_of(8 * flip(z), 8), 8)

            @pl.when(is_edge)
            def _():
                total, _ = edge_step(fil[...], faces[...], extra[...], faces_x[...])
                done[...] = total[:, :, 0]
                done_x[...] = total[:, :, 1]

            def finish(i):
                ring = i
                first = COLS * ring

                @pl.when(jnp.logical_not(is_edge))
                def _():
                    done[pl.ds(first, COLS)] = last_step(
                        fil[pl.ds(first, COLS)],
                        fil[lax.rem(first + TILES - 1, TILES), :, 0],
                        fil[lax.rem(first + COLS, TILES), :, 0],
                        faces[pl.ds(first, COLS), :, 0],
                    )

                for c in range(COLS):
                    tile = first + lax.rem(y + c, COLS)
                    remote(
                        done.at[tile], out.at[my_levels, rows], out_send.at[0],
                        out_recv.at[0], polar_lat, tile,
                    ).start()

                    @pl.when(jnp.logical_and(is_edge, tile != lon))
                    def _():
                        remote(
                            done_x.at[tile], row_x.at[my_levels], ox_send.at[0], ox_recv.at[0],
                            beside_lat, tile,
                        ).start()

                    @pl.when(jnp.logical_and(is_edge, tile == lon))
                    def _():
                        pltpu.make_async_copy(
                            done_x.at[tile], row_x.at[my_levels], ox_recv.at[0]
                        ).start()

            over(RINGS, finish)

        to_left.wait_recv()
        to_right.wait_recv()

        def beyond(p):
            from_right = packed_r[...]
            if p:
                from_right = pltpu.roll(from_right, LANES - 8 * p, 1)
            from_left = pltpu.roll(packed_l[...], (LANES - 8 - 8 * p) % LANES, 1)
            return jnp.where(lane < LANES // 2, from_right, from_left)

        def east_of(x):
            near, far = (pltpu.roll(v, LANES - 1, 1) for v in x)
            last = lane == LANES - 1
            return jnp.where(last, far, near), jnp.where(last, near, far)

        def west_of(x):
            near, far = (pltpu.roll(v, 1, 1) for v in x)
            last = lane == 0
            return jnp.where(last, far, near), jnp.where(last, near, far)

        def north_of(x):
            return [pltpu.roll(v, WIDE - 1, 0) for v in x]

        def south_of(x):
            return [pltpu.roll(v, 1, 0) for v in x]

        kappa_e, speed_e, kappa_n, speed_n, open_m = (
            (ext[LEVELS + k, here], beyond(LEVELS + k)) for k in range(5)
        )

        def minus(kappa, speed):
            return [m * (-k - 0.5 * f) for m, k, f in zip(open_m, kappa, speed)]

        def plus(kappa, speed):
            return [m * (k - 0.5 * f) for m, k, f in zip(open_m, kappa, speed)]

        wide_faces = (
            [a * b for a, b in zip(minus(kappa_e, speed_e), east_of(open_m))],
            [-a * b for a, b in zip(open_m, west_of(plus(kappa_e, speed_e)))],
            [a * b for a, b in zip(minus(kappa_n, speed_n), north_of(open_m))],
            [-a * b for a, b in zip(open_m, south_of(plus(kappa_n, speed_n)))],
        )
        for k in range(4):
            for side in range(2):
                wide_coef[k, side] = wide_faces[k][side]

        def level(p):
            from_right = pltpu.roll(packed_r[...], LANES - 8 * p, 1)
            from_left = pltpu.roll(packed_l[...], LANES - 8 - 8 * p, 1)
            x = (ext[p, here], jnp.where(lane < LANES // 2, from_right, from_left))
            for _ in range(STEPS):
                new = list(x)
                for k, near in enumerate((east_of(x), west_of(x), north_of(x), south_of(x))):
                    for side in range(2):
                        new[side] = new[side] + wide_coef[k, side] * (x[side] - near[side])
                x = tuple(new)
            mid_out[p] = x[0][8 : 8 + ROWS]

        over(LEVELS, level)

        store = pltpu.make_async_copy(mid_out, out, store_sem.at[0])
        store.start()

        @pl.when(beside)
        def _():
            wait_bytes(coef.at[pl.ds(0, COLS - 1)], pass_send.at[0])
            wait_bytes(done, out_send.at[0])

            @pl.when(is_edge)
            def _():
                wait_bytes(strip.at[pl.ds(0, COLS - 1)], px_send.at[0])
                wait_bytes(done_x.at[pl.ds(0, TILES - 1)], ox_send.at[0])


        to_left.wait_send()
        to_right.wait_send()

        @pl.when(beside)
        def _():
            wait_bytes(row_x, ox_recv.at[0])

        store.wait()

    @pl.when(lat > 0)
    def _():
        to_south.wait_send()

    @pl.when(lat < LATS - 1)
    def _():
        to_north.wait_send()


def shards(cotangent, diff_east, diff_north, flow_east, flow_north, sea_mask, cutoff):
    wide, turn = tables()
    hbm = pl.BlockSpec(memory_space=pltpu.HBM)
    dma = pltpu.SemaphoreType.DMA

    def room(*shape):
        return pltpu.VMEM(shape, F32)

    table = pltpu.VMEM((2 * LANES, 2 * LANES), jnp.bfloat16)
    field, shared = pl.pallas_call(
        kernel,
        out_shape=[
            jax.ShapeDtypeStruct((LEVELS, ROWS, LANES), F32),
            jax.ShapeDtypeStruct((LEVELS, 8, LANES), F32),
        ],
        in_specs=[hbm] * 9,
        out_specs=[hbm, hbm],
        scratch_shapes=[
            pltpu.VMEM((ROWS, LANES), jnp.int32),
            pltpu.SMEM((ROWS,), jnp.int32),
            room(2 * LANES, 2 * LANES),
            table,
            table,
            room(72, 8, LANES),
            room(PLANES, EXT, LANES),
            room(BLOCKS, LEVELS, 2, 8, LANES),
            room(BLOCKS, 5, 2, 8, LANES),
            room(BLOCKS, 2, 8, LANES),
            room(PAIRS, 8, LANES),
            room(EXTRA, 8, LANES),
            room(TILES, 8, LANES),
            room(COLS, RINGS, EXTRA, 8, LANES),
            room(TILES, 4, 8, LANES),
            room(TILES, 2, 8, LANES),
            room(TILES, 2, 2, 8, LANES),
            room(TILES, 2, 2, 8, LANES),
            room(TILES, 2, 8, LANES),
            room(COLS, RINGS, 5, 2, 8, LANES),
            room(TILES, 4, 2, 8, LANES),
            room(2, 2 * LANES, LANES),
            room(2, 8, LANES),
            room(WIDE, LANES),
            room(WIDE, LANES),
            room(WIDE, LANES),
            room(4, 2, WIDE, LANES),
            room(LEVELS, ROWS, LANES),
            dma((9,)),
            dma((2,)), dma((2,)), dma((2,)), dma((2,)), dma((2,)), dma((1,)), dma((1,)), dma((1,)),
            dma((1,)), dma((RINGS,)), dma((1,)), dma((1,)), dma((1,)), dma((1,)), dma((1,)), dma((1,)),
            dma((1,)), dma((1,)), dma((1,)), dma((1,)), dma((1,)), dma((1,)), dma((1,)),
        ],
        compiler_params=pltpu.CompilerParams(
            collective_id=0, has_side_effects=True, vmem_limit_bytes=63 * 1024 * 1024
        ),
    )(
        cotangent, diff_east, diff_north, flow_east, flow_north, sea_mask, cutoff,
        jnp.asarray(wide), jnp.asarray(turn),
    )
    lat = lax.axis_index("lat")
    row = lax.broadcasted_iota(jnp.int32, field.shape, 1)
    taken = jnp.logical_or(
        jnp.logical_and(lat == 1, row < EDGE), jnp.logical_and(lat == LATS - 2, row >= ROWS - EDGE)
    )
    return jnp.where(taken, jnp.tile(shared, (1, ROWS // 8, 1)), field)


def solution(mesh):
    return jax.shard_map(
        shards,
        mesh=mesh,
        in_specs=(
            P(None, "lat", "lon"),
            P("lat", "lon"),
            P("lat", "lon"),
            P("lat", "lon"),
            P("lat", "lon"),
            P("lat", "lon"),
            P("lat"),
        ),
        out_specs=P(None, "lat", "lon"),
        check_vma=False,
    )
```

```python
import functools
import math

import jax
import jax.numpy as jnp
import numpy as np
from jax import lax
from jax.experimental import pallas as pl
from jax.experimental.pallas import tpu as pltpu
from jax.sharding import PartitionSpec as P

STEPS = 4
LEVELS = 8
ROWS = 64
LANES = 128
TILES = 32
NLON = TILES * LANES
BLOCKS = 8
PAIRS = 4
HALO = 16
EXT = ROWS + 2 * HALO
WIDE = ROWS + HALO
PLANES = LEVELS + 5
MASK = LEVELS + 4
EDGE = 4
LATS = 8
COLS = 4
RINGS = 8
EXTRA = 3

F32 = jnp.float32


def tables():
    n = np.arange(LANES)
    angle = 2 * np.pi * (np.outer(n, n) % LANES) / LANES
    cos, sin = np.cos(angle), np.sin(angle)
    wide = np.block([[cos, -sin], [sin, cos]])
    q = np.arange(8)[:, None, None]
    c = np.arange(4)[None, :, None]
    first = 2 * np.pi * ((q * (n[None, None, :] + LANES * c)) % NLON) / NLON
    r = np.arange(4)[:, None]
    second = 2 * np.pi * ((r * n[None, :]) % 512) / 512

    def spread(values):
        values = values.reshape(-1, 1, LANES)
        return np.broadcast_to(values, (values.shape[0], 8, LANES)).astype(np.float32)

    turn = np.concatenate(
        [spread(np.cos(first)), spread(np.sin(first)), spread(np.cos(second)), spread(np.sin(second))]
    )
    return wide.astype(np.float32), turn


def cadd(x, y):
    return x[0] + y[0], x[1] + y[1]


def csub(x, y):
    return x[0] - y[0], x[1] - y[1]


def quarter(x, sign):
    if sign < 0:
        return x[1], -x[0]
    return -x[1], x[0]


def dft4(x, sign):
    even, odd = cadd(x[0], x[2]), csub(x[0], x[2])
    even2, odd2 = cadd(x[1], x[3]), quarter(csub(x[1], x[3]), sign)
    return [cadd(even, even2), cadd(odd, odd2), csub(even, even2), csub(odd, odd2)]


def dft8(x, sign):
    even = dft4([x[0], x[2], x[4], x[6]], sign)
    odd = dft4([x[1], x[3], x[5], x[7]], sign)
    half = math.sqrt(0.5)

    def eighth(v):
        rot = quarter(v, sign)
        return (v[0] + rot[0]) * half, (v[1] + rot[1]) * half

    odd[1] = eighth(odd[1])
    odd[2] = quarter(odd[2], sign)
    odd[3] = quarter(eighth(odd[3]), sign)
    return [cadd(e, o) for e, o in zip(even, odd)] + [csub(e, o) for e, o in zip(even, odd)]


def cmul(x, cos, sin, sign):
    if sign < 0:
        return x[0] * cos + x[1] * sin, x[1] * cos - x[0] * sin
    return x[0] * cos - x[1] * sin, x[1] * cos + x[0] * sin


def split_dot(left, high_ref, low_ref):
    high = left.astype(jnp.bfloat16)
    low = (left - high.astype(F32)).astype(jnp.bfloat16)
    dot = functools.partial(jnp.dot, preferred_element_type=F32)
    return dot(high, high_ref[...]) + (dot(low, high_ref[...]) + dot(high, low_ref[...]))


def filter_circles(real, imag, kept, high_ref, low_ref, turn_ref):
    shape = (8, 4, 8, LANES)
    cos1 = turn_ref[0:32].reshape(shape)
    sin1 = turn_ref[32:64].reshape(shape)
    real, imag = real.reshape(shape), imag.reshape(shape)
    parts = dft8([(real[a], imag[a]) for a in range(8)], -1)
    parts = [cmul(parts[q], cos1[q], sin1[q], -1) for q in range(8)]
    real = jnp.stack([p[0] for p in parts])
    imag = jnp.stack([p[1] for p in parts])
    parts = dft4([(real[:, c], imag[:, c]) for c in range(4)], -1)
    parts = [parts[0]] + [
        cmul(parts[r], turn_ref[64 + r], turn_ref[68 + r], -1) for r in range(1, 4)
    ]
    real = jnp.concatenate([p[0] for p in parts]).reshape(256, LANES)
    imag = jnp.concatenate([p[1] for p in parts]).reshape(256, LANES)
    spec = split_dot(jnp.concatenate([real, imag], axis=1), high_ref, low_ref)
    real = spec[:, :LANES] * kept
    imag = spec[:, LANES:] * kept
    back = split_dot(jnp.concatenate([imag, real], axis=1), high_ref, low_ref)
    real = back[:, LANES:].reshape(4, 8, 8, LANES)
    imag = back[:, :LANES].reshape(4, 8, 8, LANES)
    parts = [(real[0], imag[0])] + [
        cmul((real[r], imag[r]), turn_ref[64 + r], turn_ref[68 + r], 1) for r in range(1, 4)
    ]
    parts = dft4(parts, 1)
    real = jnp.stack([p[0] for p in parts], axis=1)
    imag = jnp.stack([p[1] for p in parts], axis=1)
    parts = [cmul((real[q], imag[q]), cos1[q], sin1[q], 1) for q in range(8)]
    parts = dft8(parts, 1)
    real = jnp.concatenate([p[0] for p in parts])
    imag = jnp.concatenate([p[1] for p in parts])
    return real, imag


def iota(shape, dim):
    return lax.broadcasted_iota(jnp.int32, shape, dim)


def circle_step(x, coef):
    shape = (TILES * 4, 8, LANES)
    full = (TILES, 2, 2, 8, LANES)
    lane = iota(shape, 2)
    row = iota(full, 3)
    flat = x.reshape(shape)
    east = pltpu.roll(flat, LANES - 1, 2)
    east = jnp.where(lane == LANES - 1, jnp.concatenate([east[4:], east[:4]]), east)
    west = pltpu.roll(flat, 1, 2)
    west = jnp.where(lane == 0, jnp.concatenate([west[-4:], west[:-4]]), west)

    def across(turned, edge):
        turned = turned.reshape(full)
        other = jnp.stack([turned[:, :, 1], turned[:, :, 0]], axis=2)
        return jnp.where(row == edge, other, turned)

    up = across(pltpu.roll(flat, 7, 1), 7)
    down = across(pltpu.roll(flat, 1, 1), 0)
    total = x
    for k, near in enumerate((east.reshape(full), west.reshape(full), up, down)):
        total = total + coef[:, k : k + 1] * (x - near)
    return total


def last_step(cells, before, after, coef):
    x = cells[:, :, 0]
    rim = cells[:, :, 1]
    count = x.shape[0]
    lane = iota(x.shape, 3)
    row = iota(x.shape, 2)

    def turn(v, step, dim):
        flat = pltpu.roll(v.reshape(-1, 8, LANES), step % v.shape[dim], dim - 1)
        return flat.reshape(v.shape)

    east = turn(x, -1, 3)
    next_east = turn(jnp.concatenate([x[1:], after[None]]), -1, 3)
    east = jnp.where(lane == LANES - 1, next_east, east)
    west = turn(x, 1, 3)
    next_west = turn(jnp.concatenate([before[None], x[: count - 1]]), 1, 3)
    west = jnp.where(lane == 0, next_west, west)
    up = jnp.where(row == 7, turn(rim, -1, 2), turn(x, -1, 2))
    down = jnp.where(row == 0, turn(rim, 1, 2), turn(x, 1, 2))
    total = x
    for k, near in enumerate((east, west, up, down)):
        total = total + coef[:, k : k + 1] * (x - near)
    return total


def neighbour(x, step):
    shape = (x.size // (8 * LANES), 8, LANES)
    width = shape[0] // TILES
    lane = iota(shape, 2)
    turned = pltpu.roll(x.reshape(shape), step % LANES, 2)
    moved = jnp.concatenate([turned[-width * step :], turned[: -width * step]])
    edge = 0 if step > 0 else LANES - 1
    return jnp.where(lane == edge, moved, turned).reshape(x.shape)


def edge_step(x, coef, extra, coef_x):
    full = (TILES, 2, 8, LANES)
    row = iota(full, 2)
    own, rim = x[:, :, 0], x[:, :, 1]

    def turn(v, step):
        return pltpu.roll(v.reshape(-1, 8, LANES), step, 1).reshape(v.shape)

    up_own = jnp.where(row == 7, turn(rim, 7), turn(own, 7))
    down_own = jnp.where(row == 0, turn(rim, 1), turn(own, 1))
    up_rim = jnp.where(row == 7, turn(own, 7), turn(rim, 7))
    up_rim = jnp.where(row == 3, jnp.stack([turn(extra, 3), turn(extra, 7)], axis=1), up_rim)
    down_rim = jnp.where(row == 0, turn(own, 1), turn(rim, 1))
    down_rim = jnp.where(row == 4, jnp.stack([turn(extra, 1), turn(extra, 5)], axis=1), down_rim)
    row = iota(extra.shape, 1)
    up_x = jnp.where(row == 3, turn(rim[:, 0], 7), turn(extra, 7))
    up_x = jnp.where(row == 7, turn(rim[:, 1], 3), up_x)
    down_x = jnp.where(row == 0, turn(rim[:, 0], 5), turn(extra, 1))
    down_x = jnp.where(row == 4, turn(rim[:, 1], 1), down_x)

    up = jnp.stack([up_own, up_rim], axis=2)
    down = jnp.stack([down_own, down_rim], axis=2)
    total = x
    for k, near in enumerate((neighbour(x, -1), neighbour(x, 1), up, down)):
        total = total + coef[:, k : k + 1] * (x - near)
    total_x = extra
    for k, near in enumerate((neighbour(extra, -1), neighbour(extra, 1), up_x, down_x)):
        total_x = total_x + coef_x[:, k] * (extra - near)
    return total, total_x


def kernel(
    cot, diff_east_in, diff_north_in, flow_east_in, flow_north_in, sea_in, cutoff_in, wide_in,
    turn_in,
    out, row_x,
    sea, cutoff, wide_ref, high_ref, low_ref, turn_ref,
    ext, lam_src, coef_src, cut_src, extra_src, strip_src, extra, strip, faces_x, done_x,
    lam, fil, done, coef, faces, kept_ref, cuts_ref, packed, packed_l, packed_r, wide_coef, mid_out,
    load_sem, row_send, row_recv, col_send, col_recv, cut_send, cut_recv, in_send, in_recv,
    cf_send, cf_recv, pass_send, pass_recv, out_send, out_recv, ox_recv, store_sem, lx_send, lx_recv,
    sx_send, sx_recv, px_send, px_recv, ox_send,
):
    lon = lax.axis_index("lon")
    lat = lax.axis_index("lat")
    y = lax.rem(lon, 4)
    z = lon // 4
    first_band = lat < LATS // 2
    polar = jnp.logical_or(lat == 0, lat == LATS - 1)
    beside = jnp.logical_or(lat == 1, lat == LATS - 2)
    polar_lat = jnp.where(first_band, 0, LATS - 1)
    beside_lat = jnp.where(first_band, 1, LATS - 2)
    edge = jnp.where(first_band, BLOCKS - 1, 0)
    is_edge = jnp.logical_and(beside, z == edge)
    pair = y

    def owner_of(b, p):
        return beside_lat, COLS * b + p

    main = pl.ds(HALO, ROWS)
    plane_loads = [
        pltpu.make_async_copy(src, dst, load_sem.at[k])
        for k, (src, dst) in enumerate(
            (
                (sea_in, sea),
                (diff_east_in, ext.at[LEVELS, main]),
                (flow_east_in, ext.at[LEVELS + 1, main]),
                (diff_north_in, ext.at[LEVELS + 2, main]),
                (flow_north_in, ext.at[LEVELS + 3, main]),
                (cot, ext.at[pl.ds(0, LEVELS), main]),
            )
        )
    ]
    cut_load = pltpu.make_async_copy(cutoff_in, cutoff, load_sem.at[6])
    table_loads = [
        pltpu.make_async_copy(turn_in, turn_ref, load_sem.at[7]),
        pltpu.make_async_copy(wide_in, wide_ref, load_sem.at[8]),
    ]
    for load in plane_loads:
        load.start()

    @pl.when(polar)
    def _():
        cut_load.start()

    @pl.when(beside)
    def _():
        for load in table_loads:
            load.start()

    barrier = pltpu.get_barrier_semaphore()

    def at(to_lat, to_lon):
        return {"lon": to_lon, "lat": to_lat}

    def hail(to_lat, to_lon):
        pl.semaphore_signal(
            barrier, inc=1, device_id=at(to_lat, to_lon), device_id_type=pl.DeviceIdType.MESH
        )

    def remote(src, dst, send, recv, to_lat, to_lon):
        return pltpu.make_async_remote_copy(
            src_ref=src, dst_ref=dst, send_sem=send, recv_sem=recv,
            device_id=at(to_lat, to_lon), device_id_type=pl.DeviceIdType.MESH,
        )

    def wait_bytes(ref, sem):
        pltpu.make_async_copy(ref, ref, sem).wait()

    def over(count, body):
        def go(k, carry):
            body(k)
            return carry

        lax.fori_loop(0, count, go, 0)

    def far_first(i):
        return lax.rem(z + 4 + ((i + 1) // 2) * (1 - 2 * lax.rem(i, 2)), RINGS)

    right = lax.rem(lon + 1, TILES)
    left = lax.rem(lon + TILES - 1, TILES)

    @pl.when(polar)
    def _():
        def greet(i):
            b = far_first(i)
            for p in range(PAIRS):
                hail(*owner_of(b, p))

        over(BLOCKS, greet)

    @pl.when(beside)
    def _():
        def greet(i):
            for c in range(COLS):
                hail(polar_lat, COLS * far_first(i) + lax.rem(y + c, COLS))

        over(RINGS, greet)
        for c in range(1, COLS):
            hail(lat, COLS * z + lax.rem(y + c, COLS))

    @pl.when(beside)
    def _():
        for p in range(PAIRS):
            @pl.when(COLS * edge + p != lon)
            def _():
                hail(lat, COLS * edge + p)

    @pl.when(jnp.logical_not(polar))
    def _():
        hail(lat, left)
        hail(lat, right)

    @pl.when(lat > 0)
    def _():
        hail(lat - 1, lon)

    @pl.when(lat < LATS - 1)
    def _():
        hail(lat + 1, lon)

    for load in plane_loads:
        load.wait()
    ext[MASK, HALO : HALO + ROWS] = sea[...].astype(F32)
    sub = iota((LEVELS, 8, LANES), 1)

    def fill(b, tile):
        rows = 8 * tile
        lam_src[b, :, 0] = ext[0:LEVELS, rows : rows + 8]
        lam_src[b, :, 1] = jnp.where(
            sub < EDGE, ext[0:LEVELS, rows + 8 : rows + 16], ext[0:LEVELS, rows - 8 : rows]
        )

    def face_tiles(start, count):
        rows = pl.ds(pl.multiple_of(start, 8), 8 * count)
        mine = ext[MASK, rows]
        kappa_e, speed_e, kappa_n, speed_n = (ext[LEVELS + k, rows] for k in range(4))
        minus_n = mine * (-kappa_n - 0.5 * speed_n)
        plus_n = mine * (kappa_n - 0.5 * speed_n)
        planes = (
            mine * (-kappa_e - 0.5 * speed_e),
            mine * (kappa_e - 0.5 * speed_e),
            minus_n * pltpu.roll(mine, 8 * count - 1, 0),
            -mine * pltpu.roll(plus_n, 1, 0),
            mine,
        )
        return [plane.reshape(count, 8, LANES) for plane in planes]

    low = iota((1, 8, LANES), 1) < EDGE
    free = jnp.where(first_band, 0, 1)
    @pl.when(polar)
    def _():
        zeros = jnp.zeros((PLANES, 8, LANES), F32)
        ext[:, 0:8] = zeros
        ext[:, EXT - 8 : EXT] = zeros

        @pl.when(lat == 0)
        def _():
            ext[:, 8:16] = zeros
            for b in range(BLOCKS - 1):
                fill(b, b + 2)

        @pl.when(lat > 0)
        def _():
            ext[:, EXT - 16 : EXT - 8] = zeros
            for b in range(1, BLOCKS):
                fill(b, b + 2)

        for k, face in enumerate(face_tiles(jnp.where(first_band, 8, 16), BLOCKS + 1)):
            coef_src[pl.ds(free, BLOCKS - 1), k, 0] = face[1:8]
            coef_src[pl.ds(free, BLOCKS - 1), k, 1] = jnp.where(low, face[2:9], face[0:7])

        cut_load.wait()
        row = iota((8, LANES), 0)
        open_cut = jnp.full((8, LANES), float(NLON // 2), F32)
        cuts = [open_cut, open_cut]
        for b in range(BLOCKS):
            tile = open_cut
            for j in range(8):
                tile = jnp.where(row == j, cutoff[8 * b + j].astype(F32), tile)
            cuts.append(tile)
        cuts += [open_cut, open_cut]
        for b in range(BLOCKS):
            cut_src[b, 0] = cuts[b + 2]
            cut_src[b, 1] = jnp.where(row < EDGE, cuts[b + 3], cuts[b + 1])

    peers = jnp.where(polar, 1 + BLOCKS * PAIRS, 4)
    peers = peers + jnp.where(beside, TILES + COLS - 1, 0)
    peers = peers + jnp.where(is_edge, TILES - 1, 0)
    pl.semaphore_wait(barrier, peers)

    low_rows = ext.at[:, pl.ds(HALO, 8)]
    high_rows = ext.at[:, pl.ds(HALO + ROWS - 8, 8)]
    south_rows = ext.at[:, pl.ds(HALO - 8, 8)]
    north_rows = ext.at[:, pl.ds(HALO + ROWS, 8)]
    to_south = remote(low_rows, north_rows, row_send.at[0], row_recv.at[0], lat - 1, lon)
    to_north = remote(high_rows, south_rows, row_send.at[1], row_recv.at[1], lat + 1, lon)

    @pl.when(lat > 0)
    def _():
        to_south.start()

    @pl.when(lat < LATS - 1)
    def _():
        to_north.start()

    def wait_rows():
        @pl.when(lat < LATS - 1)
        def _():
            to_south.wait_recv()

        @pl.when(lat > 0)
        def _():
            to_north.wait_recv()

    @pl.when(polar)
    def _():
        def send_block(b):
            for p in range(PAIRS):
                remote(
                    lam_src.at[b, pl.ds(2 * p, 2)], lam.at[lon], in_send.at[0], in_recv.at[0],
                    *owner_of(b, p),
                ).start()

        def send_coef(b):
            remote(
                coef_src.at[b], coef.at[y, z], cf_send.at[0], cf_recv.at[z], *owner_of(b, y)
            ).start()

        def send_free(i):
            @pl.when(far_first(i) != edge)
            def _():
                send_coef(far_first(i))

        over(RINGS, lambda i: send_free(RINGS - 1 - i))
        pltpu.make_async_remote_copy(
            src_ref=cut_src.at[z], dst_ref=cuts_ref, send_sem=cut_send.at[0],
            recv_sem=cut_recv.at[0], device_id=at(beside_lat, lon),
            device_id_type=pl.DeviceIdType.MESH,
        ).start()

        wait_rows()
        def halves(low_from, high_from):
            lower = jnp.where(first_band, pltpu.roll(low_from, 4, 1), low_from)
            upper = jnp.where(first_band, high_from, pltpu.roll(high_from, 4, 1))
            return jnp.where(low, lower, upper)

        strips = []
        for k, face in enumerate(face_tiles(jnp.where(first_band, ROWS, 0), 4)):
            coef_src[edge, k, 0] = jnp.where(first_band, face[1], face[2])
            coef_src[edge, k, 1] = jnp.where(
                low[0], jnp.where(first_band, face[2], face[3]), jnp.where(first_band, face[0], face[1])
            )
            strips.append(jnp.where(first_band, face[2], face[1])[None])
        for j in range(EXTRA):
            strip_src[j] = halves(strips[2 * j], strips[min(2 * j + 1, 4)])[0]
        send_coef(edge)
        remote(
            strip_src, strip.at[y, z], sx_send.at[0], sx_recv.at[0], *owner_of(edge, y)
        ).start()

        @pl.when(lat == 0)
        def _():
            fill(BLOCKS - 1, BLOCKS + 1)

        @pl.when(lat > 0)
        def _():
            fill(0, 2)

        beyond_rows = pl.ds(pl.multiple_of(jnp.where(first_band, HALO + ROWS, HALO - 8), 8), 8)
        outside = ext[pl.ds(0, LEVELS), beyond_rows]
        for p in range(PAIRS):
            extra_src[p] = halves(outside[2 * p : 2 * p + 1], outside[2 * p + 1 : 2 * p + 2])[0]
            remote(
                extra_src.at[p], extra.at[lon], lx_send.at[0], lx_recv.at[0], *owner_of(edge, p)
            ).start()
        over(RINGS, lambda i: send_block(far_first(RINGS - 1 - i)))

        wait_bytes(cuts_ref, cut_send.at[0])

        wait_bytes(extra_src, lx_send.at[0])
        wait_bytes(strip_src, sx_send.at[0])
        wait_bytes(lam_src, in_send.at[0])
        wait_bytes(coef_src, cf_send.at[0])
        wait_bytes(out, out_recv.at[0])

    @pl.when(jnp.logical_not(polar))
    def _():
        wait_rows()
        here = slice(8, 8 + WIDE)
        lane = iota((WIDE, LANES), 1)
        total = jnp.zeros((WIDE, LANES), F32)
        for p in range(PLANES):
            v = ext[p, here]
            u = jnp.where(lane < EDGE, v, pltpu.roll(v, 2 * EDGE, 1))
            if p:
                u = pltpu.roll(u, 8 * p, 1)
            total = jnp.where((lane // 8) == p, u, total)
        packed[...] = total
        to_left = remote(packed, packed_r, col_send.at[0], col_recv.at[0], lat, left)
        to_right = remote(packed, packed_l, col_send.at[1], col_recv.at[1], lat, right)
        to_left.start()
        to_right.start()
        @pl.when(beside)
        def _():
            for load in table_loads:
                load.wait()
            high = wide_ref[...].astype(jnp.bfloat16)
            high_ref[...] = high
            low_ref[...] = (wide_ref[...] - high.astype(F32)).astype(jnp.bfloat16)

            def hand_on(t):
                ring = far_first(RINGS - 1 - t)
                wait_bytes(coef.at[y, ring], cf_recv.at[ring])
                for c in range(1, COLS):
                    remote(
                        coef.at[y, ring], coef.at[y, ring], pass_send.at[0], pass_recv.at[0],
                        lat, COLS * z + lax.rem(y + c, COLS),
                    ).start()

            over(RINGS, hand_on)

            @pl.when(is_edge)
            def _():
                wait_bytes(strip.at[y], sx_recv.at[0])
                for c in range(1, COLS):
                    remote(
                        strip.at[y], strip.at[y], px_send.at[0], px_recv.at[0],
                        lat, COLS * z + lax.rem(y + c, COLS),
                    ).start()

        to_left.wait_recv()
        to_right.wait_recv()

        def beyond(p):
            from_right = packed_r[...]
            if p:
                from_right = pltpu.roll(from_right, LANES - 8 * p, 1)
            from_left = pltpu.roll(packed_l[...], (LANES - 8 - 8 * p) % LANES, 1)
            return jnp.where(lane < LANES // 2, from_right, from_left)

        def east_of(x):
            near, far = (pltpu.roll(v, LANES - 1, 1) for v in x)
            last = lane == LANES - 1
            return jnp.where(last, far, near), jnp.where(last, near, far)

        def west_of(x):
            near, far = (pltpu.roll(v, 1, 1) for v in x)
            last = lane == 0
            return jnp.where(last, far, near), jnp.where(last, near, far)

        def north_of(x):
            return [pltpu.roll(v, WIDE - 1, 0) for v in x]

        def south_of(x):
            return [pltpu.roll(v, 1, 0) for v in x]

        kappa_e, speed_e, kappa_n, speed_n, open_m = (
            (ext[LEVELS + k, here], beyond(LEVELS + k)) for k in range(5)
        )

        def minus(kappa, speed):
            return [m * (-k - 0.5 * f) for m, k, f in zip(open_m, kappa, speed)]

        def plus(kappa, speed):
            return [m * (k - 0.5 * f) for m, k, f in zip(open_m, kappa, speed)]

        wide_faces = (
            [a * b for a, b in zip(minus(kappa_e, speed_e), east_of(open_m))],
            [-a * b for a, b in zip(open_m, west_of(plus(kappa_e, speed_e)))],
            [a * b for a, b in zip(minus(kappa_n, speed_n), north_of(open_m))],
            [-a * b for a, b in zip(open_m, south_of(plus(kappa_n, speed_n)))],
        )
        for k in range(4):
            for side in range(2):
                wide_coef[k, side] = wide_faces[k][side]

        def level(p):
            from_right = pltpu.roll(packed_r[...], LANES - 8 * p, 1)
            from_left = pltpu.roll(packed_l[...], LANES - 8 - 8 * p, 1)
            x = (ext[p, here], jnp.where(lane < LANES // 2, from_right, from_left))
            for _ in range(STEPS):
                new = list(x)
                for k, near in enumerate((east_of(x), west_of(x), north_of(x), south_of(x))):
                    for side in range(2):
                        new[side] = new[side] + wide_coef[k, side] * (x[side] - near[side])
                x = tuple(new)
            mid_out[p] = x[0][8 : 8 + ROWS]

        over(LEVELS, level)

        store = pltpu.make_async_copy(mid_out, out, store_sem.at[0])
        store.start()

        @pl.when(beside)
        def _():
            wait_bytes(cuts_ref, cut_recv.at[0])
            cuts = cuts_ref[...].astype(jnp.int32)
            shape = (TILES, 8, LANES)
            wave = iota(shape, 0) + TILES * iota(shape, 2)
            wave = jnp.minimum(wave, NLON - wave)
            for half in range(2):
                kept_ref[half] = jnp.where(wave <= cuts[half][None], 1.0 / NLON, 0.0).astype(
                    F32
                ).reshape(2 * LANES, LANES)
            wait_bytes(lam, in_recv.at[0])

            @pl.when(is_edge)
            def _():
                wait_bytes(extra, lx_recv.at[0])

            def filtered():
                for half in range(2):
                    real, imag = filter_circles(
                        lam[:, 0, half], lam[:, 1, half], kept_ref[half], high_ref, low_ref,
                        turn_ref,
                    )
                    fil[:, 0, half] = real
                    fil[:, 1, half] = imag

            def step(s):
                filtered()

                @pl.when(s == 0)
                def _():
                    wait_bytes(coef.at[pl.ds(0, COLS - 1)], pass_recv.at[0])

                    def circle(k):
                        parts = [coef[c, :, k] for c in range(COLS)]
                        return jnp.stack(parts, axis=1).reshape(TILES, 2, 8, LANES)

                    mine = circle(4)
                    faces[:, 0] = circle(0) * neighbour(mine, -1)
                    faces[:, 1] = -mine * neighbour(circle(1), 1)
                    faces[:, 2] = circle(2)
                    faces[:, 3] = circle(3)

                @pl.when(jnp.logical_and(is_edge, s == 0))
                def _():
                    wait_bytes(strip.at[pl.ds(0, COLS - 1)], px_recv.at[0])

                    def circle(k):
                        parts = [strip[c, :, k // 2] for c in range(COLS)]
                        both = jnp.stack(parts, axis=1).reshape(TILES, 8, LANES)
                        turned = pltpu.roll(both, 4, 1)
                        lower = iota(both.shape, 1) < EDGE
                        if k % 2:
                            return jnp.where(lower, turned, both)
                        return jnp.where(lower, both, turned)

                    mine = circle(4)
                    faces_x[:, 0] = circle(0) * neighbour(mine, -1)
                    faces_x[:, 1] = -mine * neighbour(circle(1), 1)
                    faces_x[:, 2] = circle(2)
                    faces_x[:, 3] = circle(3)

                @pl.when(is_edge)
                def _():
                    lam[...], extra[...] = edge_step(
                        fil[...], faces[...], extra[...], faces_x[...]
                    )

                @pl.when(jnp.logical_not(is_edge))
                def _():
                    lam[...] = circle_step(fil[...], faces[...])

            over(STEPS - 1, step)
            filtered()

            my_levels = pl.ds(2 * pair, 2)
            rows = pl.ds(pl.multiple_of(8 * z, 8), 8)

            @pl.when(is_edge)
            def _():
                total, _ = edge_step(fil[...], faces[...], extra[...], faces_x[...])
                done[...] = total[:, :, 0]
                done_x[...] = total[:, :, 1]

            def finish(i):
                ring = i
                first = COLS * ring

                @pl.when(jnp.logical_not(is_edge))
                def _():
                    done[pl.ds(first, COLS)] = last_step(
                        fil[pl.ds(first, COLS)],
                        fil[lax.rem(first + TILES - 1, TILES), :, 0],
                        fil[lax.rem(first + COLS, TILES), :, 0],
                        faces[pl.ds(first, COLS), :, 0],
                    )

                for c in range(COLS):
                    tile = first + lax.rem(y + c, COLS)
                    remote(
                        done.at[tile], out.at[my_levels, rows], out_send.at[0],
                        out_recv.at[0], polar_lat, tile,
                    ).start()

                    @pl.when(jnp.logical_and(is_edge, tile != lon))
                    def _():
                        remote(
                            done_x.at[tile], row_x.at[my_levels], ox_send.at[0], ox_recv.at[0],
                            beside_lat, tile,
                        ).start()

                    @pl.when(jnp.logical_and(is_edge, tile == lon))
                    def _():
                        pltpu.make_async_copy(
                            done_x.at[tile], row_x.at[my_levels], ox_recv.at[0]
                        ).start()

            over(RINGS, finish)

        @pl.when(beside)
        def _():
            wait_bytes(coef.at[pl.ds(0, COLS - 1)], pass_send.at[0])
            wait_bytes(done, out_send.at[0])

            @pl.when(is_edge)
            def _():
                wait_bytes(strip.at[pl.ds(0, COLS - 1)], px_send.at[0])
                wait_bytes(done_x.at[pl.ds(0, TILES - 1)], ox_send.at[0])


        to_left.wait_send()
        to_right.wait_send()

        @pl.when(beside)
        def _():
            wait_bytes(row_x, ox_recv.at[0])

        store.wait()

    @pl.when(lat > 0)
    def _():
        to_south.wait_send()

    @pl.when(lat < LATS - 1)
    def _():
        to_north.wait_send()


def shards(cotangent, diff_east, diff_north, flow_east, flow_north, sea_mask, cutoff):
    wide, turn = tables()
    hbm = pl.BlockSpec(memory_space=pltpu.HBM)
    dma = pltpu.SemaphoreType.DMA

    def room(*shape):
        return pltpu.VMEM(shape, F32)

    table = pltpu.VMEM((2 * LANES, 2 * LANES), jnp.bfloat16)
    field, shared = pl.pallas_call(
        kernel,
        out_shape=[
            jax.ShapeDtypeStruct((LEVELS, ROWS, LANES), F32),
            jax.ShapeDtypeStruct((LEVELS, 8, LANES), F32),
        ],
        in_specs=[hbm] * 9,
        out_specs=[hbm, hbm],
        scratch_shapes=[
            pltpu.VMEM((ROWS, LANES), jnp.int32),
            pltpu.SMEM((ROWS,), jnp.int32),
            room(2 * LANES, 2 * LANES),
            table,
            table,
            room(72, 8, LANES),
            room(PLANES, EXT, LANES),
            room(BLOCKS, LEVELS, 2, 8, LANES),
            room(BLOCKS, 5, 2, 8, LANES),
            room(BLOCKS, 2, 8, LANES),
            room(PAIRS, 8, LANES),
            room(EXTRA, 8, LANES),
            room(TILES, 8, LANES),
            room(COLS, RINGS, EXTRA, 8, LANES),
            room(TILES, 4, 8, LANES),
            room(TILES, 2, 8, LANES),
            room(TILES, 2, 2, 8, LANES),
            room(TILES, 2, 2, 8, LANES),
            room(TILES, 2, 8, LANES),
            room(COLS, RINGS, 5, 2, 8, LANES),
            room(TILES, 4, 2, 8, LANES),
            room(2, 2 * LANES, LANES),
            room(2, 8, LANES),
            room(WIDE, LANES),
            room(WIDE, LANES),
            room(WIDE, LANES),
            room(4, 2, WIDE, LANES),
            room(LEVELS, ROWS, LANES),
            dma((9,)),
            dma((2,)), dma((2,)), dma((2,)), dma((2,)), dma((2,)), dma((1,)), dma((1,)), dma((1,)),
            dma((1,)), dma((RINGS,)), dma((1,)), dma((1,)), dma((1,)), dma((1,)), dma((1,)), dma((1,)),
            dma((1,)), dma((1,)), dma((1,)), dma((1,)), dma((1,)), dma((1,)), dma((1,)),
        ],
        compiler_params=pltpu.CompilerParams(
            collective_id=0, has_side_effects=True, vmem_limit_bytes=63 * 1024 * 1024
        ),
    )(
        cotangent, diff_east, diff_north, flow_east, flow_north, sea_mask, cutoff,
        jnp.asarray(wide), jnp.asarray(turn),
    )
    lat = lax.axis_index("lat")
    row = lax.broadcasted_iota(jnp.int32, field.shape, 1)
    taken = jnp.logical_or(
        jnp.logical_and(lat == 1, row < EDGE), jnp.logical_and(lat == LATS - 2, row >= ROWS - EDGE)
    )
    return jnp.where(taken, jnp.tile(shared, (1, ROWS // 8, 1)), field)


def solution(mesh):
    return jax.shard_map(
        shards,
        mesh=mesh,
        in_specs=(
            P(None, "lat", "lon"),
            P("lat", "lon"),
            P("lat", "lon"),
            P("lat", "lon"),
            P("lat", "lon"),
            P("lat", "lon"),
            P("lat"),
        ),
        out_specs=P(None, "lat", "lon"),
        check_vma=False,
    )
```

```python
import functools
import math

import jax
import jax.numpy as jnp
import numpy as np
from jax import lax
from jax.experimental import pallas as pl
from jax.experimental.pallas import tpu as pltpu
from jax.sharding import PartitionSpec as P

STEPS = 4
LEVELS = 8
ROWS = 64
LANES = 128
TILES = 32
NLON = TILES * LANES
BLOCKS = 8
PAIRS = 4
HALO = 16
EXT = ROWS + 2 * HALO
WIDE = ROWS + HALO
PLANES = LEVELS + 5
MASK = LEVELS + 4
EDGE = 4
LATS = 8
COLS = 4
RINGS = 8
EXTRA = 3

F32 = jnp.float32


def tables():
    n = np.arange(LANES)
    angle = 2 * np.pi * (np.outer(n, n) % LANES) / LANES
    cos, sin = np.cos(angle), np.sin(angle)
    wide = np.block([[cos, -sin], [sin, cos]])
    q = np.arange(8)[:, None, None]
    c = np.arange(4)[None, :, None]
    first = 2 * np.pi * ((q * (n[None, None, :] + LANES * c)) % NLON) / NLON
    r = np.arange(4)[:, None]
    second = 2 * np.pi * ((r * n[None, :]) % 512) / 512

    def spread(values):
        values = values.reshape(-1, 1, LANES)
        return np.broadcast_to(values, (values.shape[0], 8, LANES)).astype(np.float32)

    turn = np.concatenate(
        [spread(np.cos(first)), spread(np.sin(first)), spread(np.cos(second)), spread(np.sin(second))]
    )
    return wide.astype(np.float32), turn


def cadd(x, y):
    return x[0] + y[0], x[1] + y[1]


def csub(x, y):
    return x[0] - y[0], x[1] - y[1]


def quarter(x, sign):
    if sign < 0:
        return x[1], -x[0]
    return -x[1], x[0]


def dft4(x, sign):
    even, odd = cadd(x[0], x[2]), csub(x[0], x[2])
    even2, odd2 = cadd(x[1], x[3]), quarter(csub(x[1], x[3]), sign)
    return [cadd(even, even2), cadd(odd, odd2), csub(even, even2), csub(odd, odd2)]


def dft8(x, sign):
    even = dft4([x[0], x[2], x[4], x[6]], sign)
    odd = dft4([x[1], x[3], x[5], x[7]], sign)
    half = math.sqrt(0.5)

    def eighth(v):
        rot = quarter(v, sign)
        return (v[0] + rot[0]) * half, (v[1] + rot[1]) * half

    odd[1] = eighth(odd[1])
    odd[2] = quarter(odd[2], sign)
    odd[3] = quarter(eighth(odd[3]), sign)
    return [cadd(e, o) for e, o in zip(even, odd)] + [csub(e, o) for e, o in zip(even, odd)]


def cmul(x, cos, sin, sign):
    if sign < 0:
        return x[0] * cos + x[1] * sin, x[1] * cos - x[0] * sin
    return x[0] * cos - x[1] * sin, x[1] * cos + x[0] * sin


def split_dot(left, high_ref, low_ref):
    high = left.astype(jnp.bfloat16)
    low = (left - high.astype(F32)).astype(jnp.bfloat16)
    dot = functools.partial(jnp.dot, preferred_element_type=F32)
    return dot(high, high_ref[...]) + (dot(low, high_ref[...]) + dot(high, low_ref[...]))


def filter_circles(real, imag, kept, high_ref, low_ref, turn_ref):
    shape = (8, 4, 8, LANES)
    cos1 = turn_ref[0:32].reshape(shape)
    sin1 = turn_ref[32:64].reshape(shape)
    real, imag = real.reshape(shape), imag.reshape(shape)
    parts = dft8([(real[a], imag[a]) for a in range(8)], -1)
    parts = [cmul(parts[q], cos1[q], sin1[q], -1) for q in range(8)]
    real = jnp.stack([p[0] for p in parts])
    imag = jnp.stack([p[1] for p in parts])
    parts = dft4([(real[:, c], imag[:, c]) for c in range(4)], -1)
    parts = [parts[0]] + [
        cmul(parts[r], turn_ref[64 + r], turn_ref[68 + r], -1) for r in range(1, 4)
    ]
    real = jnp.concatenate([p[0] for p in parts]).reshape(256, LANES)
    imag = jnp.concatenate([p[1] for p in parts]).reshape(256, LANES)
    spec = split_dot(jnp.concatenate([real, imag], axis=1), high_ref, low_ref)
    real = spec[:, :LANES] * kept
    imag = spec[:, LANES:] * kept
    back = split_dot(jnp.concatenate([imag, real], axis=1), high_ref, low_ref)
    real = back[:, LANES:].reshape(4, 8, 8, LANES)
    imag = back[:, :LANES].reshape(4, 8, 8, LANES)
    parts = [(real[0], imag[0])] + [
        cmul((real[r], imag[r]), turn_ref[64 + r], turn_ref[68 + r], 1) for r in range(1, 4)
    ]
    parts = dft4(parts, 1)
    real = jnp.stack([p[0] for p in parts], axis=1)
    imag = jnp.stack([p[1] for p in parts], axis=1)
    parts = [cmul((real[q], imag[q]), cos1[q], sin1[q], 1) for q in range(8)]
    parts = dft8(parts, 1)
    real = jnp.concatenate([p[0] for p in parts])
    imag = jnp.concatenate([p[1] for p in parts])
    return real, imag


def iota(shape, dim):
    return lax.broadcasted_iota(jnp.int32, shape, dim)


def circle_step(x, coef):
    shape = (TILES * 4, 8, LANES)
    full = (TILES, 2, 2, 8, LANES)
    lane = iota(shape, 2)
    row = iota(full, 3)
    flat = x.reshape(shape)
    east = pltpu.roll(flat, LANES - 1, 2)
    east = jnp.where(lane == LANES - 1, jnp.concatenate([east[4:], east[:4]]), east)
    west = pltpu.roll(flat, 1, 2)
    west = jnp.where(lane == 0, jnp.concatenate([west[-4:], west[:-4]]), west)

    def across(turned, edge):
        turned = turned.reshape(full)
        other = jnp.stack([turned[:, :, 1], turned[:, :, 0]], axis=2)
        return jnp.where(row == edge, other, turned)

    up = across(pltpu.roll(flat, 7, 1), 7)
    down = across(pltpu.roll(flat, 1, 1), 0)
    total = x
    for k, near in enumerate((east.reshape(full), west.reshape(full), up, down)):
        total = total + coef[:, k : k + 1] * (x - near)
    return total


def last_step(cells, before, after, coef):
    x = cells[:, :, 0]
    rim = cells[:, :, 1]
    count = x.shape[0]
    lane = iota(x.shape, 3)
    row = iota(x.shape, 2)

    def turn(v, step, dim):
        flat = pltpu.roll(v.reshape(-1, 8, LANES), step % v.shape[dim], dim - 1)
        return flat.reshape(v.shape)

    east = turn(x, -1, 3)
    next_east = turn(jnp.concatenate([x[1:], after[None]]), -1, 3)
    east = jnp.where(lane == LANES - 1, next_east, east)
    west = turn(x, 1, 3)
    next_west = turn(jnp.concatenate([before[None], x[: count - 1]]), 1, 3)
    west = jnp.where(lane == 0, next_west, west)
    up = jnp.where(row == 7, turn(rim, -1, 2), turn(x, -1, 2))
    down = jnp.where(row == 0, turn(rim, 1, 2), turn(x, 1, 2))
    total = x
    for k, near in enumerate((east, west, up, down)):
        total = total + coef[:, k : k + 1] * (x - near)
    return total


def neighbour(x, step):
    shape = (x.size // (8 * LANES), 8, LANES)
    width = shape[0] // TILES
    lane = iota(shape, 2)
    turned = pltpu.roll(x.reshape(shape), step % LANES, 2)
    moved = jnp.concatenate([turned[-width * step :], turned[: -width * step]])
    edge = 0 if step > 0 else LANES - 1
    return jnp.where(lane == edge, moved, turned).reshape(x.shape)


def edge_step(x, coef, extra, coef_x):
    full = (TILES, 2, 8, LANES)
    row = iota(full, 2)
    own, rim = x[:, :, 0], x[:, :, 1]

    def turn(v, step):
        return pltpu.roll(v.reshape(-1, 8, LANES), step, 1).reshape(v.shape)

    up_own = jnp.where(row == 7, turn(rim, 7), turn(own, 7))
    down_own = jnp.where(row == 0, turn(rim, 1), turn(own, 1))
    up_rim = jnp.where(row == 7, turn(own, 7), turn(rim, 7))
    up_rim = jnp.where(row == 3, jnp.stack([turn(extra, 3), turn(extra, 7)], axis=1), up_rim)
    down_rim = jnp.where(row == 0, turn(own, 1), turn(rim, 1))
    down_rim = jnp.where(row == 4, jnp.stack([turn(extra, 1), turn(extra, 5)], axis=1), down_rim)
    row = iota(extra.shape, 1)
    up_x = jnp.where(row == 3, turn(rim[:, 0], 7), turn(extra, 7))
    up_x = jnp.where(row == 7, turn(rim[:, 1], 3), up_x)
    down_x = jnp.where(row == 0, turn(rim[:, 0], 5), turn(extra, 1))
    down_x = jnp.where(row == 4, turn(rim[:, 1], 1), down_x)

    up = jnp.stack([up_own, up_rim], axis=2)
    down = jnp.stack([down_own, down_rim], axis=2)
    total = x
    for k, near in enumerate((neighbour(x, -1), neighbour(x, 1), up, down)):
        total = total + coef[:, k : k + 1] * (x - near)
    total_x = extra
    for k, near in enumerate((neighbour(extra, -1), neighbour(extra, 1), up_x, down_x)):
        total_x = total_x + coef_x[:, k] * (extra - near)
    return total, total_x


def kernel(
    cot, diff_east_in, diff_north_in, flow_east_in, flow_north_in, sea_in, cutoff_in, wide_in,
    turn_in,
    out, row_x,
    sea, cutoff, wide_ref, high_ref, low_ref, turn_ref,
    ext, lam_src, coef_src, cut_src, extra_src, strip_src, extra, strip, faces_x, done_x,
    lam, fil, done, coef, faces, kept_ref, cuts_ref, packed, packed_l, packed_r, wide_coef, mid_out,
    load_sem, row_send, row_recv, col_send, col_recv, cut_send, cut_recv, in_send, in_recv,
    cf_send, cf_recv, pass_send, pass_recv, out_send, out_recv, ox_recv, store_sem, lx_send, lx_recv,
    sx_send, sx_recv, px_send, px_recv, ox_send,
):
    lon = lax.axis_index("lon")
    lat = lax.axis_index("lat")
    y = lax.rem(lon, 4)
    z = lon // 4
    first_band = lat < LATS // 2
    polar = jnp.logical_or(lat == 0, lat == LATS - 1)
    beside = jnp.logical_or(lat == 1, lat == LATS - 2)
    polar_lat = jnp.where(first_band, 0, LATS - 1)
    beside_lat = jnp.where(first_band, 1, LATS - 2)
    edge = jnp.where(first_band, BLOCKS - 1, 0)

    def flip(b):
        return jnp.where(first_band, BLOCKS - 1 - b, b)

    edge_ring = flip(edge)
    is_edge = jnp.logical_and(beside, z == edge_ring)
    pair = y

    def owner_of(b, p):
        return beside_lat, COLS * flip(b) + p

    main = pl.ds(HALO, ROWS)
    plane_loads = [
        pltpu.make_async_copy(src, dst, load_sem.at[k])
        for k, (src, dst) in enumerate(
            (
                (sea_in, sea),
                (diff_east_in, ext.at[LEVELS, main]),
                (flow_east_in, ext.at[LEVELS + 1, main]),
                (diff_north_in, ext.at[LEVELS + 2, main]),
                (flow_north_in, ext.at[LEVELS + 3, main]),
                (cot, ext.at[pl.ds(0, LEVELS), main]),
            )
        )
    ]
    cut_load = pltpu.make_async_copy(cutoff_in, cutoff, load_sem.at[6])
    table_loads = [
        pltpu.make_async_copy(turn_in, turn_ref, load_sem.at[7]),
        pltpu.make_async_copy(wide_in, wide_ref, load_sem.at[8]),
    ]
    for load in plane_loads:
        load.start()

    @pl.when(polar)
    def _():
        cut_load.start()

    @pl.when(beside)
    def _():
        for load in table_loads:
            load.start()

    barrier = pltpu.get_barrier_semaphore()

    def at(to_lat, to_lon):
        return {"lon": to_lon, "lat": to_lat}

    def hail(to_lat, to_lon):
        pl.semaphore_signal(
            barrier, inc=1, device_id=at(to_lat, to_lon), device_id_type=pl.DeviceIdType.MESH
        )

    def remote(src, dst, send, recv, to_lat, to_lon):
        return pltpu.make_async_remote_copy(
            src_ref=src, dst_ref=dst, send_sem=send, recv_sem=recv,
            device_id=at(to_lat, to_lon), device_id_type=pl.DeviceIdType.MESH,
        )

    def wait_bytes(ref, sem):
        pltpu.make_async_copy(ref, ref, sem).wait()

    def over(count, body):
        def go(k, carry):
            body(k)
            return carry

        lax.fori_loop(0, count, go, 0)

    def far_first(i):
        return lax.rem(z + 4 + ((i + 1) // 2) * (1 - 2 * lax.rem(i, 2)), RINGS)

    right = lax.rem(lon + 1, TILES)
    left = lax.rem(lon + TILES - 1, TILES)

    @pl.when(polar)
    def _():
        def greet(i):
            b = flip(far_first(i))
            for p in range(PAIRS):
                hail(*owner_of(b, p))

        over(BLOCKS, greet)

    @pl.when(beside)
    def _():
        def greet(i):
            for c in range(COLS):
                hail(polar_lat, COLS * far_first(i) + lax.rem(y + c, COLS))

        over(RINGS, greet)
        for c in range(1, COLS):
            hail(lat, COLS * z + lax.rem(y + c, COLS))

    @pl.when(beside)
    def _():
        for p in range(PAIRS):
            @pl.when(COLS * edge_ring + p != lon)
            def _():
                hail(lat, COLS * edge_ring + p)

    @pl.when(jnp.logical_not(polar))
    def _():
        hail(lat, left)
        hail(lat, right)

    @pl.when(lat > 0)
    def _():
        hail(lat - 1, lon)

    @pl.when(lat < LATS - 1)
    def _():
        hail(lat + 1, lon)

    for load in plane_loads:
        load.wait()
    ext[MASK, HALO : HALO + ROWS] = sea[...].astype(F32)
    sub = iota((LEVELS, 8, LANES), 1)

    def fill(b, tile):
        rows = 8 * tile
        lam_src[b, :, 0] = ext[0:LEVELS, rows : rows + 8]
        lam_src[b, :, 1] = jnp.where(
            sub < EDGE, ext[0:LEVELS, rows + 8 : rows + 16], ext[0:LEVELS, rows - 8 : rows]
        )

    def face_tiles(start, count):
        rows = pl.ds(pl.multiple_of(start, 8), 8 * count)
        mine = ext[MASK, rows]
        kappa_e, speed_e, kappa_n, speed_n = (ext[LEVELS + k, rows] for k in range(4))
        minus_n = mine * (-kappa_n - 0.5 * speed_n)
        plus_n = mine * (kappa_n - 0.5 * speed_n)
        planes = (
            mine * (-kappa_e - 0.5 * speed_e),
            mine * (kappa_e - 0.5 * speed_e),
            minus_n * pltpu.roll(mine, 8 * count - 1, 0),
            -mine * pltpu.roll(plus_n, 1, 0),
            mine,
        )
        return [plane.reshape(count, 8, LANES) for plane in planes]

    low = iota((1, 8, LANES), 1) < EDGE
    free = jnp.where(first_band, 0, 1)
    @pl.when(polar)
    def _():
        zeros = jnp.zeros((PLANES, 8, LANES), F32)
        ext[:, 0:8] = zeros
        ext[:, EXT - 8 : EXT] = zeros

        @pl.when(lat == 0)
        def _():
            ext[:, 8:16] = zeros
            for b in range(BLOCKS - 1):
                fill(b, b + 2)

        @pl.when(lat > 0)
        def _():
            ext[:, EXT - 16 : EXT - 8] = zeros
            for b in range(1, BLOCKS):
                fill(b, b + 2)

        for k, face in enumerate(face_tiles(jnp.where(first_band, 8, 16), BLOCKS + 1)):
            coef_src[pl.ds(free, BLOCKS - 1), k, 0] = face[1:8]
            coef_src[pl.ds(free, BLOCKS - 1), k, 1] = jnp.where(low, face[2:9], face[0:7])

        cut_load.wait()
        row = iota((8, LANES), 0)
        open_cut = jnp.full((8, LANES), float(NLON // 2), F32)
        cuts = [open_cut, open_cut]
        for b in range(BLOCKS):
            tile = open_cut
            for j in range(8):
                tile = jnp.where(row == j, cutoff[8 * b + j].astype(F32), tile)
            cuts.append(tile)
        cuts += [open_cut, open_cut]
        for b in range(BLOCKS):
            cut_src[b, 0] = cuts[b + 2]
            cut_src[b, 1] = jnp.where(row < EDGE, cuts[b + 3], cuts[b + 1])

    peers = jnp.where(polar, 1 + BLOCKS * PAIRS, 4)
    peers = peers + jnp.where(beside, TILES + COLS - 1, 0)
    peers = peers + jnp.where(is_edge, TILES - 1, 0)
    pl.semaphore_wait(barrier, peers)

    low_rows = ext.at[:, pl.ds(HALO, 8)]
    high_rows = ext.at[:, pl.ds(HALO + ROWS - 8, 8)]
    south_rows = ext.at[:, pl.ds(HALO - 8, 8)]
    north_rows = ext.at[:, pl.ds(HALO + ROWS, 8)]
    to_south = remote(low_rows, north_rows, row_send.at[0], row_recv.at[0], lat - 1, lon)
    to_north = remote(high_rows, south_rows, row_send.at[1], row_recv.at[1], lat + 1, lon)

    @pl.when(lat > 0)
    def _():
        to_south.start()

    @pl.when(lat < LATS - 1)
    def _():
        to_north.start()

    def wait_rows():
        @pl.when(lat < LATS - 1)
        def _():
            to_south.wait_recv()

        @pl.when(lat > 0)
        def _():
            to_north.wait_recv()

    @pl.when(polar)
    def _():
        def send_block(b):
            for p in range(PAIRS):
                remote(
                    lam_src.at[b, pl.ds(2 * p, 2)], lam.at[lon], in_send.at[0], in_recv.at[0],
                    *owner_of(b, p),
                ).start()

        def send_coef(b):
            remote(
                coef_src.at[b], coef.at[y, z], cf_send.at[0], cf_recv.at[z], *owner_of(b, y)
            ).start()

        def send_free(i):
            b = flip(far_first(i))

            @pl.when(b != edge)
            def _():
                send_coef(b)

        over(RINGS, lambda i: send_free(RINGS - 1 - i))
        pltpu.make_async_remote_copy(
            src_ref=cut_src.at[flip(z)], dst_ref=cuts_ref, send_sem=cut_send.at[0],
            recv_sem=cut_recv.at[0], device_id=at(beside_lat, lon),
            device_id_type=pl.DeviceIdType.MESH,
        ).start()

        wait_rows()
        def halves(low_from, high_from):
            lower = jnp.where(first_band, pltpu.roll(low_from, 4, 1), low_from)
            upper = jnp.where(first_band, high_from, pltpu.roll(high_from, 4, 1))
            return jnp.where(low, lower, upper)

        strips = []
        for k, face in enumerate(face_tiles(jnp.where(first_band, ROWS, 0), 4)):
            coef_src[edge, k, 0] = jnp.where(first_band, face[1], face[2])
            coef_src[edge, k, 1] = jnp.where(
                low[0], jnp.where(first_band, face[2], face[3]), jnp.where(first_band, face[0], face[1])
            )
            strips.append(jnp.where(first_band, face[2], face[1])[None])
        for j in range(EXTRA):
            strip_src[j] = halves(strips[2 * j], strips[min(2 * j + 1, 4)])[0]
        send_coef(edge)
        remote(
            strip_src, strip.at[y, z], sx_send.at[0], sx_recv.at[0], *owner_of(edge, y)
        ).start()

        @pl.when(lat == 0)
        def _():
            fill(BLOCKS - 1, BLOCKS + 1)

        @pl.when(lat > 0)
        def _():
            fill(0, 2)

        beyond_rows = pl.ds(pl.multiple_of(jnp.where(first_band, HALO + ROWS, HALO - 8), 8), 8)
        outside = ext[pl.ds(0, LEVELS), beyond_rows]
        for p in range(PAIRS):
            extra_src[p] = halves(outside[2 * p : 2 * p + 1], outside[2 * p + 1 : 2 * p + 2])[0]
            remote(
                extra_src.at[p], extra.at[lon], lx_send.at[0], lx_recv.at[0], *owner_of(edge, p)
            ).start()
        over(RINGS, lambda i: send_block(flip(far_first(RINGS - 1 - i))))

        wait_bytes(cuts_ref, cut_send.at[0])

        wait_bytes(extra_src, lx_send.at[0])
        wait_bytes(strip_src, sx_send.at[0])
        wait_bytes(lam_src, in_send.at[0])
        wait_bytes(coef_src, cf_send.at[0])
        wait_bytes(out, out_recv.at[0])

    @pl.when(jnp.logical_not(polar))
    def _():
        wait_rows()
        here = slice(8, 8 + WIDE)
        lane = iota((WIDE, LANES), 1)
        total = jnp.zeros((WIDE, LANES), F32)
        for p in range(PLANES):
            v = ext[p, here]
            u = jnp.where(lane < EDGE, v, pltpu.roll(v, 2 * EDGE, 1))
            if p:
                u = pltpu.roll(u, 8 * p, 1)
            total = jnp.where((lane // 8) == p, u, total)
        packed[...] = total
        to_left = remote(packed, packed_r, col_send.at[0], col_recv.at[0], lat, left)
        to_right = remote(packed, packed_l, col_send.at[1], col_recv.at[1], lat, right)
        to_left.start()
        to_right.start()
        @pl.when(beside)
        def _():
            for load in table_loads:
                load.wait()
            high = wide_ref[...].astype(jnp.bfloat16)
            high_ref[...] = high
            low_ref[...] = (wide_ref[...] - high.astype(F32)).astype(jnp.bfloat16)

            def hand_on(t):
                ring = far_first(RINGS - 1 - t)
                wait_bytes(coef.at[y, ring], cf_recv.at[ring])
                for c in range(1, COLS):
                    remote(
                        coef.at[y, ring], coef.at[y, ring], pass_send.at[0], pass_recv.at[0],
                        lat, COLS * z + lax.rem(y + c, COLS),
                    ).start()

            over(RINGS, hand_on)

            @pl.when(is_edge)
            def _():
                wait_bytes(strip.at[y], sx_recv.at[0])
                for c in range(1, COLS):
                    remote(
                        strip.at[y], strip.at[y], px_send.at[0], px_recv.at[0],
                        lat, COLS * z + lax.rem(y + c, COLS),
                    ).start()

        to_left.wait_recv()
        to_right.wait_recv()

        def beyond(p):
            from_right = packed_r[...]
            if p:
                from_right = pltpu.roll(from_right, LANES - 8 * p, 1)
            from_left = pltpu.roll(packed_l[...], (LANES - 8 - 8 * p) % LANES, 1)
            return jnp.where(lane < LANES // 2, from_right, from_left)

        def east_of(x):
            near, far = (pltpu.roll(v, LANES - 1, 1) for v in x)
            last = lane == LANES - 1
            return jnp.where(last, far, near), jnp.where(last, near, far)

        def west_of(x):
            near, far = (pltpu.roll(v, 1, 1) for v in x)
            last = lane == 0
            return jnp.where(last, far, near), jnp.where(last, near, far)

        def north_of(x):
            return [pltpu.roll(v, WIDE - 1, 0) for v in x]

        def south_of(x):
            return [pltpu.roll(v, 1, 0) for v in x]

        kappa_e, speed_e, kappa_n, speed_n, open_m = (
            (ext[LEVELS + k, here], beyond(LEVELS + k)) for k in range(5)
        )

        def minus(kappa, speed):
            return [m * (-k - 0.5 * f) for m, k, f in zip(open_m, kappa, speed)]

        def plus(kappa, speed):
            return [m * (k - 0.5 * f) for m, k, f in zip(open_m, kappa, speed)]

        wide_faces = (
            [a * b for a, b in zip(minus(kappa_e, speed_e), east_of(open_m))],
            [-a * b for a, b in zip(open_m, west_of(plus(kappa_e, speed_e)))],
            [a * b for a, b in zip(minus(kappa_n, speed_n), north_of(open_m))],
            [-a * b for a, b in zip(open_m, south_of(plus(kappa_n, speed_n)))],
        )
        for k in range(4):
            for side in range(2):
                wide_coef[k, side] = wide_faces[k][side]

        def level(p):
            from_right = pltpu.roll(packed_r[...], LANES - 8 * p, 1)
            from_left = pltpu.roll(packed_l[...], LANES - 8 - 8 * p, 1)
            x = (ext[p, here], jnp.where(lane < LANES // 2, from_right, from_left))
            for _ in range(STEPS):
                new = list(x)
                for k, near in enumerate((east_of(x), west_of(x), north_of(x), south_of(x))):
                    for side in range(2):
                        new[side] = new[side] + wide_coef[k, side] * (x[side] - near[side])
                x = tuple(new)
            mid_out[p] = x[0][8 : 8 + ROWS]

        over(LEVELS, level)

        store = pltpu.make_async_copy(mid_out, out, store_sem.at[0])
        store.start()

        @pl.when(beside)
        def _():
            wait_bytes(cuts_ref, cut_recv.at[0])
            cuts = cuts_ref[...].astype(jnp.int32)
            shape = (TILES, 8, LANES)
            wave = iota(shape, 0) + TILES * iota(shape, 2)
            wave = jnp.minimum(wave, NLON - wave)
            for half in range(2):
                kept_ref[half] = jnp.where(wave <= cuts[half][None], 1.0 / NLON, 0.0).astype(
                    F32
                ).reshape(2 * LANES, LANES)
            wait_bytes(lam, in_recv.at[0])

            @pl.when(is_edge)
            def _():
                wait_bytes(extra, lx_recv.at[0])

            def filtered():
                for half in range(2):
                    real, imag = filter_circles(
                        lam[:, 0, half], lam[:, 1, half], kept_ref[half], high_ref, low_ref,
                        turn_ref,
                    )
                    fil[:, 0, half] = real
                    fil[:, 1, half] = imag

            def step(s):
                filtered()

                @pl.when(s == 0)
                def _():
                    wait_bytes(coef.at[pl.ds(0, COLS - 1)], pass_recv.at[0])

                    def circle(k):
                        parts = [coef[c, :, k] for c in range(COLS)]
                        return jnp.stack(parts, axis=1).reshape(TILES, 2, 8, LANES)

                    mine = circle(4)
                    faces[:, 0] = circle(0) * neighbour(mine, -1)
                    faces[:, 1] = -mine * neighbour(circle(1), 1)
                    faces[:, 2] = circle(2)
                    faces[:, 3] = circle(3)

                @pl.when(jnp.logical_and(is_edge, s == 0))
                def _():
                    wait_bytes(strip.at[pl.ds(0, COLS - 1)], px_recv.at[0])

                    def circle(k):
                        parts = [strip[c, :, k // 2] for c in range(COLS)]
                        both = jnp.stack(parts, axis=1).reshape(TILES, 8, LANES)
                        turned = pltpu.roll(both, 4, 1)
                        lower = iota(both.shape, 1) < EDGE
                        if k % 2:
                            return jnp.where(lower, turned, both)
                        return jnp.where(lower, both, turned)

                    mine = circle(4)
                    faces_x[:, 0] = circle(0) * neighbour(mine, -1)
                    faces_x[:, 1] = -mine * neighbour(circle(1), 1)
                    faces_x[:, 2] = circle(2)
                    faces_x[:, 3] = circle(3)

                @pl.when(is_edge)
                def _():
                    lam[...], extra[...] = edge_step(
                        fil[...], faces[...], extra[...], faces_x[...]
                    )

                @pl.when(jnp.logical_not(is_edge))
                def _():
                    lam[...] = circle_step(fil[...], faces[...])

            over(STEPS - 1, step)
            filtered()

            my_levels = pl.ds(2 * pair, 2)
            rows = pl.ds(pl.multiple_of(8 * flip(z), 8), 8)

            @pl.when(is_edge)
            def _():
                total, _ = edge_step(fil[...], faces[...], extra[...], faces_x[...])
                done[...] = total[:, :, 0]
                done_x[...] = total[:, :, 1]

            def finish(i):
                ring = i
                first = COLS * ring

                @pl.when(jnp.logical_not(is_edge))
                def _():
                    done[pl.ds(first, COLS)] = last_step(
                        fil[pl.ds(first, COLS)],
                        fil[lax.rem(first + TILES - 1, TILES), :, 0],
                        fil[lax.rem(first + COLS, TILES), :, 0],
                        faces[pl.ds(first, COLS), :, 0],
                    )

                for c in range(COLS):
                    tile = first + lax.rem(y + c, COLS)
                    remote(
                        done.at[tile], out.at[my_levels, rows], out_send.at[0],
                        out_recv.at[0], polar_lat, tile,
                    ).start()

                    @pl.when(jnp.logical_and(is_edge, tile != lon))
                    def _():
                        remote(
                            done_x.at[tile], row_x.at[my_levels], ox_send.at[0], ox_recv.at[0],
                            beside_lat, tile,
                        ).start()

                    @pl.when(jnp.logical_and(is_edge, tile == lon))
                    def _():
                        pltpu.make_async_copy(
                            done_x.at[tile], row_x.at[my_levels], ox_recv.at[0]
                        ).start()

            over(RINGS, finish)

        @pl.when(beside)
        def _():
            wait_bytes(coef.at[pl.ds(0, COLS - 1)], pass_send.at[0])
            wait_bytes(done, out_send.at[0])

            @pl.when(is_edge)
            def _():
                wait_bytes(strip.at[pl.ds(0, COLS - 1)], px_send.at[0])
                wait_bytes(done_x.at[pl.ds(0, TILES - 1)], ox_send.at[0])


        to_left.wait_send()
        to_right.wait_send()

        @pl.when(beside)
        def _():
            wait_bytes(row_x, ox_recv.at[0])

        store.wait()

    @pl.when(lat > 0)
    def _():
        to_south.wait_send()

    @pl.when(lat < LATS - 1)
    def _():
        to_north.wait_send()


def merge(field, shared, result, rows, extra, load_sem, store_sem):
    lat = lax.axis_index("lat")
    beside = jnp.logical_or(lat == 1, lat == LATS - 2)
    loads, stores = [], []
    for l in range(0, LEVELS, 1):
        some = pl.ds(l, 1)
        loads.append(pltpu.make_async_copy(field.at[some], rows.at[some], load_sem.at[l]))
        stores.append(pltpu.make_async_copy(rows.at[some], result.at[some], store_sem.at[l]))
    load_extra = pltpu.make_async_copy(shared, extra, load_sem.at[LEVELS])
    for load in loads:
        load.start()

    @pl.when(beside)
    def _():
        load_extra.start()
        load_extra.wait()

    row = iota((1, 8, LANES), 1)
    for k, l in enumerate(range(0, LEVELS, 1)):
        loads[k].wait()
        some = slice(l, l + 1)

        @pl.when(lat == 1)
        def _():
            rows[some, 0:8] = jnp.where(row < EDGE, extra[some], rows[some, 0:8])

        @pl.when(lat == LATS - 2)
        def _():
            rows[some, ROWS - 8 : ROWS] = jnp.where(
                row < EDGE, rows[some, ROWS - 8 : ROWS], extra[some]
            )

        stores[k].start()
    for store in stores:
        store.wait()


def shards(cotangent, diff_east, diff_north, flow_east, flow_north, sea_mask, cutoff):
    wide, turn = tables()
    hbm = pl.BlockSpec(memory_space=pltpu.HBM)
    dma = pltpu.SemaphoreType.DMA

    def room(*shape):
        return pltpu.VMEM(shape, F32)

    table = pltpu.VMEM((2 * LANES, 2 * LANES), jnp.bfloat16)
    field, shared = pl.pallas_call(
        kernel,
        out_shape=[
            jax.ShapeDtypeStruct((LEVELS, ROWS, LANES), F32),
            jax.ShapeDtypeStruct((LEVELS, 8, LANES), F32),
        ],
        in_specs=[hbm] * 9,
        out_specs=[hbm, hbm],
        scratch_shapes=[
            pltpu.VMEM((ROWS, LANES), jnp.int32),
            pltpu.SMEM((ROWS,), jnp.int32),
            room(2 * LANES, 2 * LANES),
            table,
            table,
            room(72, 8, LANES),
            room(PLANES, EXT, LANES),
            room(BLOCKS, LEVELS, 2, 8, LANES),
            room(BLOCKS, 5, 2, 8, LANES),
            room(BLOCKS, 2, 8, LANES),
            room(PAIRS, 8, LANES),
            room(EXTRA, 8, LANES),
            room(TILES, 8, LANES),
            room(COLS, RINGS, EXTRA, 8, LANES),
            room(TILES, 4, 8, LANES),
            room(TILES, 2, 8, LANES),
            room(TILES, 2, 2, 8, LANES),
            room(TILES, 2, 2, 8, LANES),
            room(TILES, 2, 8, LANES),
            room(COLS, RINGS, 5, 2, 8, LANES),
            room(TILES, 4, 2, 8, LANES),
            room(2, 2 * LANES, LANES),
            room(2, 8, LANES),
            room(WIDE, LANES),
            room(WIDE, LANES),
            room(WIDE, LANES),
            room(4, 2, WIDE, LANES),
            room(LEVELS, ROWS, LANES),
            dma((9,)),
            dma((2,)), dma((2,)), dma((2,)), dma((2,)), dma((2,)), dma((1,)), dma((1,)), dma((1,)),
            dma((1,)), dma((RINGS,)), dma((1,)), dma((1,)), dma((1,)), dma((1,)), dma((1,)), dma((1,)),
            dma((1,)), dma((1,)), dma((1,)), dma((1,)), dma((1,)), dma((1,)), dma((1,)),
        ],
        compiler_params=pltpu.CompilerParams(
            collective_id=0, has_side_effects=True, vmem_limit_bytes=63 * 1024 * 1024
        ),
    )(
        cotangent, diff_east, diff_north, flow_east, flow_north, sea_mask, cutoff,
        jnp.asarray(wide), jnp.asarray(turn),
    )
    return pl.pallas_call(
        merge,
        out_shape=jax.ShapeDtypeStruct((LEVELS, ROWS, LANES), F32),
        in_specs=[hbm, hbm],
        out_specs=hbm,
        scratch_shapes=[
            room(LEVELS, ROWS, LANES),
            room(LEVELS, 8, LANES),
            dma((LEVELS + 1,)),
            dma((LEVELS + 1,)),
        ],
        compiler_params=pltpu.CompilerParams(vmem_limit_bytes=63 * 1024 * 1024),
    )(field, shared)


def solution(mesh):
    return jax.shard_map(
        shards,
        mesh=mesh,
        in_specs=(
            P(None, "lat", "lon"),
            P("lat", "lon"),
            P("lat", "lon"),
            P("lat", "lon"),
            P("lat", "lon"),
            P("lat", "lon"),
            P("lat"),
        ),
        out_specs=P(None, "lat", "lon"),
        check_vma=False,
    )
```

```python
import functools
import math

import jax
import jax.numpy as jnp
import numpy as np
from jax import lax
from jax.experimental import pallas as pl
from jax.experimental.pallas import tpu as pltpu
from jax.sharding import PartitionSpec as P

STEPS = 4
LEVELS = 8
ROWS = 64
LANES = 128
TILES = 32
NLON = TILES * LANES
BLOCKS = 8
PAIRS = 4
HALO = 16
EXT = ROWS + 2 * HALO
WIDE = ROWS + HALO
PLANES = LEVELS + 5
MASK = LEVELS + 4
EDGE = 4
LATS = 8
COLS = 4
RINGS = 8
EXTRA = 3

F32 = jnp.float32


def tables():
    n = np.arange(LANES)
    angle = 2 * np.pi * (np.outer(n, n) % LANES) / LANES
    cos, sin = np.cos(angle), np.sin(angle)
    wide = np.block([[cos, -sin], [sin, cos]])
    q = np.arange(8)[:, None, None]
    c = np.arange(4)[None, :, None]
    first = 2 * np.pi * ((q * (n[None, None, :] + LANES * c)) % NLON) / NLON
    r = np.arange(4)[:, None]
    second = 2 * np.pi * ((r * n[None, :]) % 512) / 512

    def spread(values):
        values = values.reshape(-1, 1, LANES)
        return np.broadcast_to(values, (values.shape[0], 8, LANES)).astype(np.float32)

    turn = np.concatenate(
        [spread(np.cos(first)), spread(np.sin(first)), spread(np.cos(second)), spread(np.sin(second))]
    )
    return wide.astype(np.float32), turn


def cadd(x, y):
    return x[0] + y[0], x[1] + y[1]


def csub(x, y):
    return x[0] - y[0], x[1] - y[1]


def quarter(x, sign):
    if sign < 0:
        return x[1], -x[0]
    return -x[1], x[0]


def dft4(x, sign):
    even, odd = cadd(x[0], x[2]), csub(x[0], x[2])
    even2, odd2 = cadd(x[1], x[3]), quarter(csub(x[1], x[3]), sign)
    return [cadd(even, even2), cadd(odd, odd2), csub(even, even2), csub(odd, odd2)]


def dft8(x, sign):
    even = dft4([x[0], x[2], x[4], x[6]], sign)
    odd = dft4([x[1], x[3], x[5], x[7]], sign)
    half = math.sqrt(0.5)

    def eighth(v):
        rot = quarter(v, sign)
        return (v[0] + rot[0]) * half, (v[1] + rot[1]) * half

    odd[1] = eighth(odd[1])
    odd[2] = quarter(odd[2], sign)
    odd[3] = quarter(eighth(odd[3]), sign)
    return [cadd(e, o) for e, o in zip(even, odd)] + [csub(e, o) for e, o in zip(even, odd)]


def cmul(x, cos, sin, sign):
    if sign < 0:
        return x[0] * cos + x[1] * sin, x[1] * cos - x[0] * sin
    return x[0] * cos - x[1] * sin, x[1] * cos + x[0] * sin


def split_dot(left, high_ref, low_ref):
    high = left.astype(jnp.bfloat16)
    low = (left - high.astype(F32)).astype(jnp.bfloat16)
    dot = functools.partial(jnp.dot, preferred_element_type=F32)
    return dot(high, high_ref[...]) + (dot(low, high_ref[...]) + dot(high, low_ref[...]))


def filter_circles(real, imag, kept, high_ref, low_ref, turn_ref):
    shape = (8, 4, 8, LANES)
    cos1 = turn_ref[0:32].reshape(shape)
    sin1 = turn_ref[32:64].reshape(shape)
    real, imag = real.reshape(shape), imag.reshape(shape)
    parts = dft8([(real[a], imag[a]) for a in range(8)], -1)
    parts = [cmul(parts[q], cos1[q], sin1[q], -1) for q in range(8)]
    real = jnp.stack([p[0] for p in parts])
    imag = jnp.stack([p[1] for p in parts])
    parts = dft4([(real[:, c], imag[:, c]) for c in range(4)], -1)
    parts = [parts[0]] + [
        cmul(parts[r], turn_ref[64 + r], turn_ref[68 + r], -1) for r in range(1, 4)
    ]
    real = jnp.concatenate([p[0] for p in parts]).reshape(256, LANES)
    imag = jnp.concatenate([p[1] for p in parts]).reshape(256, LANES)
    spec = split_dot(jnp.concatenate([real, imag], axis=1), high_ref, low_ref)
    real = spec[:, :LANES] * kept
    imag = spec[:, LANES:] * kept
    back = split_dot(jnp.concatenate([imag, real], axis=1), high_ref, low_ref)
    real = back[:, LANES:].reshape(4, 8, 8, LANES)
    imag = back[:, :LANES].reshape(4, 8, 8, LANES)
    parts = [(real[0], imag[0])] + [
        cmul((real[r], imag[r]), turn_ref[64 + r], turn_ref[68 + r], 1) for r in range(1, 4)
    ]
    parts = dft4(parts, 1)
    real = jnp.stack([p[0] for p in parts], axis=1)
    imag = jnp.stack([p[1] for p in parts], axis=1)
    parts = [cmul((real[q], imag[q]), cos1[q], sin1[q], 1) for q in range(8)]
    parts = dft8(parts, 1)
    real = jnp.concatenate([p[0] for p in parts])
    imag = jnp.concatenate([p[1] for p in parts])
    return real, imag


def iota(shape, dim):
    return lax.broadcasted_iota(jnp.int32, shape, dim)


def circle_step(x, coef):
    shape = (TILES * 4, 8, LANES)
    full = (TILES, 2, 2, 8, LANES)
    lane = iota(shape, 2)
    row = iota(full, 3)
    flat = x.reshape(shape)
    east = pltpu.roll(flat, LANES - 1, 2)
    east = jnp.where(lane == LANES - 1, jnp.concatenate([east[4:], east[:4]]), east)
    west = pltpu.roll(flat, 1, 2)
    west = jnp.where(lane == 0, jnp.concatenate([west[-4:], west[:-4]]), west)

    def across(turned, edge):
        turned = turned.reshape(full)
        other = jnp.stack([turned[:, :, 1], turned[:, :, 0]], axis=2)
        return jnp.where(row == edge, other, turned)

    up = across(pltpu.roll(flat, 7, 1), 7)
    down = across(pltpu.roll(flat, 1, 1), 0)
    total = x
    for k, near in enumerate((east.reshape(full), west.reshape(full), up, down)):
        total = total + coef[:, k : k + 1] * (x - near)
    return total


def last_step(cells, before, after, coef):
    x = cells[:, :, 0]
    rim = cells[:, :, 1]
    count = x.shape[0]
    lane = iota(x.shape, 3)
    row = iota(x.shape, 2)

    def turn(v, step, dim):
        flat = pltpu.roll(v.reshape(-1, 8, LANES), step % v.shape[dim], dim - 1)
        return flat.reshape(v.shape)

    east = turn(x, -1, 3)
    next_east = turn(jnp.concatenate([x[1:], after[None]]), -1, 3)
    east = jnp.where(lane == LANES - 1, next_east, east)
    west = turn(x, 1, 3)
    next_west = turn(jnp.concatenate([before[None], x[: count - 1]]), 1, 3)
    west = jnp.where(lane == 0, next_west, west)
    up = jnp.where(row == 7, turn(rim, -1, 2), turn(x, -1, 2))
    down = jnp.where(row == 0, turn(rim, 1, 2), turn(x, 1, 2))
    total = x
    for k, near in enumerate((east, west, up, down)):
        total = total + coef[:, k : k + 1] * (x - near)
    return total


def neighbour(x, step):
    shape = (x.size // (8 * LANES), 8, LANES)
    width = shape[0] // TILES
    lane = iota(shape, 2)
    turned = pltpu.roll(x.reshape(shape), step % LANES, 2)
    moved = jnp.concatenate([turned[-width * step :], turned[: -width * step]])
    edge = 0 if step > 0 else LANES - 1
    return jnp.where(lane == edge, moved, turned).reshape(x.shape)


def edge_step(x, coef, extra, coef_x):
    full = (TILES, 2, 8, LANES)
    row = iota(full, 2)
    own, rim = x[:, :, 0], x[:, :, 1]

    def turn(v, step):
        return pltpu.roll(v.reshape(-1, 8, LANES), step, 1).reshape(v.shape)

    up_own = jnp.where(row == 7, turn(rim, 7), turn(own, 7))
    down_own = jnp.where(row == 0, turn(rim, 1), turn(own, 1))
    up_rim = jnp.where(row == 7, turn(own, 7), turn(rim, 7))
    up_rim = jnp.where(row == 3, jnp.stack([turn(extra, 3), turn(extra, 7)], axis=1), up_rim)
    down_rim = jnp.where(row == 0, turn(own, 1), turn(rim, 1))
    down_rim = jnp.where(row == 4, jnp.stack([turn(extra, 1), turn(extra, 5)], axis=1), down_rim)
    row = iota(extra.shape, 1)
    up_x = jnp.where(row == 3, turn(rim[:, 0], 7), turn(extra, 7))
    up_x = jnp.where(row == 7, turn(rim[:, 1], 3), up_x)
    down_x = jnp.where(row == 0, turn(rim[:, 0], 5), turn(extra, 1))
    down_x = jnp.where(row == 4, turn(rim[:, 1], 1), down_x)

    up = jnp.stack([up_own, up_rim], axis=2)
    down = jnp.stack([down_own, down_rim], axis=2)
    total = x
    for k, near in enumerate((neighbour(x, -1), neighbour(x, 1), up, down)):
        total = total + coef[:, k : k + 1] * (x - near)
    total_x = extra
    for k, near in enumerate((neighbour(extra, -1), neighbour(extra, 1), up_x, down_x)):
        total_x = total_x + coef_x[:, k] * (extra - near)
    return total, total_x


def kernel(
    cot, diff_east_in, diff_north_in, flow_east_in, flow_north_in, sea_in, cutoff_in, wide_in,
    turn_in,
    out, row_x,
    sea, cutoff, wide_ref, high_ref, low_ref, turn_ref,
    ext, lam_src, coef_src, cut_src, extra_src, strip_src, extra, strip, faces_x, done_x,
    lam, fil, done, coef, faces, kept_ref, cuts_ref, packed, packed_l, packed_r, wide_coef, mid_out,
    load_sem, row_send, row_recv, col_send, col_recv, cut_send, cut_recv, in_send, in_recv,
    cf_send, cf_recv, pass_send, pass_recv, out_send, out_recv, ox_recv, store_sem, lx_send, lx_recv,
    sx_send, sx_recv, px_send, px_recv, ox_send,
):
    lon = lax.axis_index("lon")
    lat = lax.axis_index("lat")
    y = lax.rem(lon, 4)
    z = lon // 4
    first_band = lat < LATS // 2
    polar = jnp.logical_or(lat == 0, lat == LATS - 1)
    beside = jnp.logical_or(lat == 1, lat == LATS - 2)
    polar_lat = jnp.where(first_band, 0, LATS - 1)
    beside_lat = jnp.where(first_band, 1, LATS - 2)
    edge = jnp.where(first_band, BLOCKS - 1, 0)
    is_edge = jnp.logical_and(beside, z == edge)
    pair = y

    def owner_of(b, p):
        return beside_lat, COLS * b + p

    main = pl.ds(HALO, ROWS)
    plane_loads = [
        pltpu.make_async_copy(src, dst, load_sem.at[k])
        for k, (src, dst) in enumerate(
            (
                (sea_in, sea),
                (diff_east_in, ext.at[LEVELS, main]),
                (flow_east_in, ext.at[LEVELS + 1, main]),
                (diff_north_in, ext.at[LEVELS + 2, main]),
                (flow_north_in, ext.at[LEVELS + 3, main]),
                (cot, ext.at[pl.ds(0, LEVELS), main]),
            )
        )
    ]
    cut_load = pltpu.make_async_copy(cutoff_in, cutoff, load_sem.at[6])
    table_loads = [
        pltpu.make_async_copy(turn_in, turn_ref, load_sem.at[7]),
        pltpu.make_async_copy(wide_in, wide_ref, load_sem.at[8]),
    ]
    for load in plane_loads:
        load.start()

    @pl.when(polar)
    def _():
        cut_load.start()

    @pl.when(beside)
    def _():
        for load in table_loads:
            load.start()

    barrier = pltpu.get_barrier_semaphore()

    def at(to_lat, to_lon):
        return {"lon": to_lon, "lat": to_lat}

    def hail(to_lat, to_lon):
        pl.semaphore_signal(
            barrier, inc=1, device_id=at(to_lat, to_lon), device_id_type=pl.DeviceIdType.MESH
        )

    def remote(src, dst, send, recv, to_lat, to_lon):
        return pltpu.make_async_remote_copy(
            src_ref=src, dst_ref=dst, send_sem=send, recv_sem=recv,
            device_id=at(to_lat, to_lon), device_id_type=pl.DeviceIdType.MESH,
        )

    def wait_bytes(ref, sem):
        pltpu.make_async_copy(ref, ref, sem).wait()

    def over(count, body):
        def go(k, carry):
            body(k)
            return carry

        lax.fori_loop(0, count, go, 0)

    def far_first(i):
        return lax.rem(z + 4 + ((i + 1) // 2) * (1 - 2 * lax.rem(i, 2)), RINGS)

    right = lax.rem(lon + 1, TILES)
    left = lax.rem(lon + TILES - 1, TILES)

    @pl.when(polar)
    def _():
        def greet(i):
            b = far_first(i)
            for p in range(PAIRS):
                hail(*owner_of(b, p))

        over(BLOCKS, greet)

    @pl.when(beside)
    def _():
        def greet(i):
            for c in range(COLS):
                hail(polar_lat, COLS * far_first(i) + lax.rem(y + c, COLS))

        over(RINGS, greet)
        for c in range(1, COLS):
            hail(lat, COLS * z + lax.rem(y + c, COLS))

    @pl.when(beside)
    def _():
        for p in range(PAIRS):
            @pl.when(COLS * edge + p != lon)
            def _():
                hail(lat, COLS * edge + p)

    @pl.when(jnp.logical_not(polar))
    def _():
        hail(lat, left)
        hail(lat, right)

    @pl.when(lat > 0)
    def _():
        hail(lat - 1, lon)

    @pl.when(lat < LATS - 1)
    def _():
        hail(lat + 1, lon)

    for load in plane_loads:
        load.wait()
    ext[MASK, HALO : HALO + ROWS] = sea[...].astype(F32)
    sub = iota((LEVELS, 8, LANES), 1)

    def fill(b, tile):
        rows = 8 * tile
        lam_src[b, :, 0] = ext[0:LEVELS, rows : rows + 8]
        lam_src[b, :, 1] = jnp.where(
            sub < EDGE, ext[0:LEVELS, rows + 8 : rows + 16], ext[0:LEVELS, rows - 8 : rows]
        )

    def face_tiles(start, count):
        rows = pl.ds(pl.multiple_of(start, 8), 8 * count)
        mine = ext[MASK, rows]
        kappa_e, speed_e, kappa_n, speed_n = (ext[LEVELS + k, rows] for k in range(4))
        minus_n = mine * (-kappa_n - 0.5 * speed_n)
        plus_n = mine * (kappa_n - 0.5 * speed_n)
        planes = (
            mine * (-kappa_e - 0.5 * speed_e),
            mine * (kappa_e - 0.5 * speed_e),
            minus_n * pltpu.roll(mine, 8 * count - 1, 0),
            -mine * pltpu.roll(plus_n, 1, 0),
            mine,
        )
        return [plane.reshape(count, 8, LANES) for plane in planes]

    low = iota((1, 8, LANES), 1) < EDGE
    free = jnp.where(first_band, 0, 1)
    @pl.when(polar)
    def _():
        zeros = jnp.zeros((PLANES, 8, LANES), F32)
        ext[:, 0:8] = zeros
        ext[:, EXT - 8 : EXT] = zeros

        @pl.when(lat == 0)
        def _():
            ext[:, 8:16] = zeros
            for b in range(BLOCKS - 1):
                fill(b, b + 2)

        @pl.when(lat > 0)
        def _():
            ext[:, EXT - 16 : EXT - 8] = zeros
            for b in range(1, BLOCKS):
                fill(b, b + 2)

        for k, face in enumerate(face_tiles(jnp.where(first_band, 8, 16), BLOCKS + 1)):
            coef_src[pl.ds(free, BLOCKS - 1), k, 0] = face[1:8]
            coef_src[pl.ds(free, BLOCKS - 1), k, 1] = jnp.where(low, face[2:9], face[0:7])

        cut_load.wait()
        row = iota((8, LANES), 0)
        open_cut = jnp.full((8, LANES), float(NLON // 2), F32)
        cuts = [open_cut, open_cut]
        for b in range(BLOCKS):
            tile = open_cut
            for j in range(8):
                tile = jnp.where(row == j, cutoff[8 * b + j].astype(F32), tile)
            cuts.append(tile)
        cuts += [open_cut, open_cut]
        for b in range(BLOCKS):
            cut_src[b, 0] = cuts[b + 2]
            cut_src[b, 1] = jnp.where(row < EDGE, cuts[b + 3], cuts[b + 1])

    peers = jnp.where(polar, 1 + BLOCKS * PAIRS, 4)
    peers = peers + jnp.where(beside, TILES + COLS - 1, 0)
    peers = peers + jnp.where(is_edge, TILES - 1, 0)
    pl.semaphore_wait(barrier, peers)

    low_rows = ext.at[:, pl.ds(HALO, 8)]
    high_rows = ext.at[:, pl.ds(HALO + ROWS - 8, 8)]
    south_rows = ext.at[:, pl.ds(HALO - 8, 8)]
    north_rows = ext.at[:, pl.ds(HALO + ROWS, 8)]
    to_south = remote(low_rows, north_rows, row_send.at[0], row_recv.at[0], lat - 1, lon)
    to_north = remote(high_rows, south_rows, row_send.at[1], row_recv.at[1], lat + 1, lon)

    @pl.when(lat > 0)
    def _():
        to_south.start()

    @pl.when(lat < LATS - 1)
    def _():
        to_north.start()

    def wait_rows():
        @pl.when(lat < LATS - 1)
        def _():
            to_south.wait_recv()

        @pl.when(lat > 0)
        def _():
            to_north.wait_recv()

    @pl.when(polar)
    def _():
        def send_block(b):
            for p in range(PAIRS):
                remote(
                    lam_src.at[b, pl.ds(2 * p, 2)], lam.at[lon], in_send.at[0], in_recv.at[0],
                    *owner_of(b, p),
                ).start()

        def send_coef(b):
            remote(
                coef_src.at[b], coef.at[y, z], cf_send.at[0], cf_recv.at[z], *owner_of(b, y)
            ).start()

        def send_free(i):
            @pl.when(far_first(i) != edge)
            def _():
                send_coef(far_first(i))

        over(RINGS, lambda i: send_free(RINGS - 1 - i))
        pltpu.make_async_remote_copy(
            src_ref=cut_src.at[z], dst_ref=cuts_ref, send_sem=cut_send.at[0],
            recv_sem=cut_recv.at[0], device_id=at(beside_lat, lon),
            device_id_type=pl.DeviceIdType.MESH,
        ).start()

        wait_rows()
        def halves(low_from, high_from):
            lower = jnp.where(first_band, pltpu.roll(low_from, 4, 1), low_from)
            upper = jnp.where(first_band, high_from, pltpu.roll(high_from, 4, 1))
            return jnp.where(low, lower, upper)

        strips = []
        for k, face in enumerate(face_tiles(jnp.where(first_band, ROWS, 0), 4)):
            coef_src[edge, k, 0] = jnp.where(first_band, face[1], face[2])
            coef_src[edge, k, 1] = jnp.where(
                low[0], jnp.where(first_band, face[2], face[3]), jnp.where(first_band, face[0], face[1])
            )
            strips.append(jnp.where(first_band, face[2], face[1])[None])
        for j in range(EXTRA):
            strip_src[j] = halves(strips[2 * j], strips[min(2 * j + 1, 4)])[0]
        send_coef(edge)
        remote(
            strip_src, strip.at[y, z], sx_send.at[0], sx_recv.at[0], *owner_of(edge, y)
        ).start()

        @pl.when(lat == 0)
        def _():
            fill(BLOCKS - 1, BLOCKS + 1)

        @pl.when(lat > 0)
        def _():
            fill(0, 2)

        beyond_rows = pl.ds(pl.multiple_of(jnp.where(first_band, HALO + ROWS, HALO - 8), 8), 8)
        outside = ext[pl.ds(0, LEVELS), beyond_rows]
        for p in range(PAIRS):
            extra_src[p] = halves(outside[2 * p : 2 * p + 1], outside[2 * p + 1 : 2 * p + 2])[0]
            remote(
                extra_src.at[p], extra.at[lon], lx_send.at[0], lx_recv.at[0], *owner_of(edge, p)
            ).start()
        over(RINGS, lambda i: send_block(far_first(RINGS - 1 - i)))

        wait_bytes(cuts_ref, cut_send.at[0])

        wait_bytes(extra_src, lx_send.at[0])
        wait_bytes(strip_src, sx_send.at[0])
        wait_bytes(lam_src, in_send.at[0])
        wait_bytes(coef_src, cf_send.at[0])
        wait_bytes(out, out_recv.at[0])

    @pl.when(jnp.logical_not(polar))
    def _():
        wait_rows()
        here = slice(8, 8 + WIDE)
        lane = iota((WIDE, LANES), 1)
        total = jnp.zeros((WIDE, LANES), F32)
        for p in range(PLANES):
            v = ext[p, here]
            u = jnp.where(lane < EDGE, v, pltpu.roll(v, 2 * EDGE, 1))
            if p:
                u = pltpu.roll(u, 8 * p, 1)
            total = jnp.where((lane // 8) == p, u, total)
        packed[...] = total
        to_left = remote(packed, packed_r, col_send.at[0], col_recv.at[0], lat, left)
        to_right = remote(packed, packed_l, col_send.at[1], col_recv.at[1], lat, right)
        to_left.start()
        to_right.start()
        @pl.when(beside)
        def _():
            for load in table_loads:
                load.wait()
            high = wide_ref[...].astype(jnp.bfloat16)
            high_ref[...] = high
            low_ref[...] = (wide_ref[...] - high.astype(F32)).astype(jnp.bfloat16)

            def hand_on(t):
                ring = far_first(RINGS - 1 - t)
                wait_bytes(coef.at[y, ring], cf_recv.at[ring])
                for c in range(1, COLS):
                    remote(
                        coef.at[y, ring], coef.at[y, ring], pass_send.at[0], pass_recv.at[0],
                        lat, COLS * z + lax.rem(y + c, COLS),
                    ).start()

            over(RINGS, hand_on)

            @pl.when(is_edge)
            def _():
                wait_bytes(strip.at[y], sx_recv.at[0])
                for c in range(1, COLS):
                    remote(
                        strip.at[y], strip.at[y], px_send.at[0], px_recv.at[0],
                        lat, COLS * z + lax.rem(y + c, COLS),
                    ).start()

        to_left.wait_recv()
        to_right.wait_recv()

        def beyond(p):
            from_right = packed_r[...]
            if p:
                from_right = pltpu.roll(from_right, LANES - 8 * p, 1)
            from_left = pltpu.roll(packed_l[...], (LANES - 8 - 8 * p) % LANES, 1)
            return jnp.where(lane < LANES // 2, from_right, from_left)

        def east_of(x):
            near, far = (pltpu.roll(v, LANES - 1, 1) for v in x)
            last = lane == LANES - 1
            return jnp.where(last, far, near), jnp.where(last, near, far)

        def west_of(x):
            near, far = (pltpu.roll(v, 1, 1) for v in x)
            last = lane == 0
            return jnp.where(last, far, near), jnp.where(last, near, far)

        def north_of(x):
            return [pltpu.roll(v, WIDE - 1, 0) for v in x]

        def south_of(x):
            return [pltpu.roll(v, 1, 0) for v in x]

        kappa_e, speed_e, kappa_n, speed_n, open_m = (
            (ext[LEVELS + k, here], beyond(LEVELS + k)) for k in range(5)
        )

        def minus(kappa, speed):
            return [m * (-k - 0.5 * f) for m, k, f in zip(open_m, kappa, speed)]

        def plus(kappa, speed):
            return [m * (k - 0.5 * f) for m, k, f in zip(open_m, kappa, speed)]

        wide_faces = (
            [a * b for a, b in zip(minus(kappa_e, speed_e), east_of(open_m))],
            [-a * b for a, b in zip(open_m, west_of(plus(kappa_e, speed_e)))],
            [a * b for a, b in zip(minus(kappa_n, speed_n), north_of(open_m))],
            [-a * b for a, b in zip(open_m, south_of(plus(kappa_n, speed_n)))],
        )
        for k in range(4):
            for side in range(2):
                wide_coef[k, side] = wide_faces[k][side]

        def level(p):
            from_right = pltpu.roll(packed_r[...], LANES - 8 * p, 1)
            from_left = pltpu.roll(packed_l[...], LANES - 8 - 8 * p, 1)
            x = (ext[p, here], jnp.where(lane < LANES // 2, from_right, from_left))
            for _ in range(STEPS):
                new = list(x)
                for k, near in enumerate((east_of(x), west_of(x), north_of(x), south_of(x))):
                    for side in range(2):
                        new[side] = new[side] + wide_coef[k, side] * (x[side] - near[side])
                x = tuple(new)
            mid_out[p] = x[0][8 : 8 + ROWS]

        over(LEVELS, level)

        store = pltpu.make_async_copy(mid_out, out, store_sem.at[0])
        store.start()

        @pl.when(beside)
        def _():
            wait_bytes(cuts_ref, cut_recv.at[0])
            cuts = cuts_ref[...].astype(jnp.int32)
            shape = (TILES, 8, LANES)
            wave = iota(shape, 0) + TILES * iota(shape, 2)
            wave = jnp.minimum(wave, NLON - wave)
            for half in range(2):
                kept_ref[half] = jnp.where(wave <= cuts[half][None], 1.0 / NLON, 0.0).astype(
                    F32
                ).reshape(2 * LANES, LANES)
            wait_bytes(lam, in_recv.at[0])

            @pl.when(is_edge)
            def _():
                wait_bytes(extra, lx_recv.at[0])

            def filtered():
                for half in range(2):
                    real, imag = filter_circles(
                        lam[:, 0, half], lam[:, 1, half], kept_ref[half], high_ref, low_ref,
                        turn_ref,
                    )
                    fil[:, 0, half] = real
                    fil[:, 1, half] = imag

            def step(s):
                filtered()

                @pl.when(s == 0)
                def _():
                    wait_bytes(coef.at[pl.ds(0, COLS - 1)], pass_recv.at[0])

                    def circle(k):
                        parts = [coef[c, :, k] for c in range(COLS)]
                        return jnp.stack(parts, axis=1).reshape(TILES, 2, 8, LANES)

                    mine = circle(4)
                    faces[:, 0] = circle(0) * neighbour(mine, -1)
                    faces[:, 1] = -mine * neighbour(circle(1), 1)
                    faces[:, 2] = circle(2)
                    faces[:, 3] = circle(3)

                @pl.when(jnp.logical_and(is_edge, s == 0))
                def _():
                    wait_bytes(strip.at[pl.ds(0, COLS - 1)], px_recv.at[0])

                    def circle(k):
                        parts = [strip[c, :, k // 2] for c in range(COLS)]
                        both = jnp.stack(parts, axis=1).reshape(TILES, 8, LANES)
                        turned = pltpu.roll(both, 4, 1)
                        lower = iota(both.shape, 1) < EDGE
                        if k % 2:
                            return jnp.where(lower, turned, both)
                        return jnp.where(lower, both, turned)

                    mine = circle(4)
                    faces_x[:, 0] = circle(0) * neighbour(mine, -1)
                    faces_x[:, 1] = -mine * neighbour(circle(1), 1)
                    faces_x[:, 2] = circle(2)
                    faces_x[:, 3] = circle(3)

                @pl.when(is_edge)
                def _():
                    lam[...], extra[...] = edge_step(
                        fil[...], faces[...], extra[...], faces_x[...]
                    )

                @pl.when(jnp.logical_not(is_edge))
                def _():
                    lam[...] = circle_step(fil[...], faces[...])

            over(STEPS - 1, step)
            filtered()

            my_levels = pl.ds(2 * pair, 2)
            rows = pl.ds(pl.multiple_of(8 * z, 8), 8)

            @pl.when(is_edge)
            def _():
                total, _ = edge_step(fil[...], faces[...], extra[...], faces_x[...])
                done[...] = total[:, :, 0]
                done_x[...] = total[:, :, 1]

            def finish(i):
                ring = i
                first = COLS * ring

                @pl.when(jnp.logical_not(is_edge))
                def _():
                    done[pl.ds(first, COLS)] = last_step(
                        fil[pl.ds(first, COLS)],
                        fil[(first + TILES - 1) % TILES, :, 0],
                        fil[(first + COLS) % TILES, :, 0],
                        faces[pl.ds(first, COLS), :, 0],
                    )

                for c in range(COLS):
                    tile = first + c
                    remote(
                        done.at[tile], out.at[my_levels, rows], out_send.at[0],
                        out_recv.at[0], polar_lat, tile,
                    ).start()

                    @pl.when(jnp.logical_and(is_edge, tile != lon))
                    def _():
                        remote(
                            done_x.at[tile], row_x.at[my_levels], ox_send.at[0], ox_recv.at[0],
                            beside_lat, tile,
                        ).start()

                    @pl.when(jnp.logical_and(is_edge, tile == lon))
                    def _():
                        pltpu.make_async_copy(
                            done_x.at[tile], row_x.at[my_levels], ox_recv.at[0]
                        ).start()

            for i in range(RINGS):
                finish(i)

        @pl.when(beside)
        def _():
            wait_bytes(coef.at[pl.ds(0, COLS - 1)], pass_send.at[0])
            wait_bytes(done, out_send.at[0])

            @pl.when(is_edge)
            def _():
                wait_bytes(strip.at[pl.ds(0, COLS - 1)], px_send.at[0])
                wait_bytes(done_x.at[pl.ds(0, TILES - 1)], ox_send.at[0])


        to_left.wait_send()
        to_right.wait_send()

        @pl.when(beside)
        def _():
            wait_bytes(row_x, ox_recv.at[0])

        store.wait()

    @pl.when(lat > 0)
    def _():
        to_south.wait_send()

    @pl.when(lat < LATS - 1)
    def _():
        to_north.wait_send()


def shards(cotangent, diff_east, diff_north, flow_east, flow_north, sea_mask, cutoff):
    wide, turn = tables()
    hbm = pl.BlockSpec(memory_space=pltpu.HBM)
    dma = pltpu.SemaphoreType.DMA

    def room(*shape):
        return pltpu.VMEM(shape, F32)

    table = pltpu.VMEM((2 * LANES, 2 * LANES), jnp.bfloat16)
    field, shared = pl.pallas_call(
        kernel,
        out_shape=[
            jax.ShapeDtypeStruct((LEVELS, ROWS, LANES), F32),
            jax.ShapeDtypeStruct((LEVELS, 8, LANES), F32),
        ],
        in_specs=[hbm] * 9,
        out_specs=[hbm, hbm],
        scratch_shapes=[
            pltpu.VMEM((ROWS, LANES), jnp.int32),
            pltpu.SMEM((ROWS,), jnp.int32),
            room(2 * LANES, 2 * LANES),
            table,
            table,
            room(72, 8, LANES),
            room(PLANES, EXT, LANES),
            room(BLOCKS, LEVELS, 2, 8, LANES),
            room(BLOCKS, 5, 2, 8, LANES),
            room(BLOCKS, 2, 8, LANES),
            room(PAIRS, 8, LANES),
            room(EXTRA, 8, LANES),
            room(TILES, 8, LANES),
            room(COLS, RINGS, EXTRA, 8, LANES),
            room(TILES, 4, 8, LANES),
            room(TILES, 2, 8, LANES),
            room(TILES, 2, 2, 8, LANES),
            room(TILES, 2, 2, 8, LANES),
            room(TILES, 2, 8, LANES),
            room(COLS, RINGS, 5, 2, 8, LANES),
            room(TILES, 4, 2, 8, LANES),
            room(2, 2 * LANES, LANES),
            room(2, 8, LANES),
            room(WIDE, LANES),
            room(WIDE, LANES),
            room(WIDE, LANES),
            room(4, 2, WIDE, LANES),
            room(LEVELS, ROWS, LANES),
            dma((9,)),
            dma((2,)), dma((2,)), dma((2,)), dma((2,)), dma((2,)), dma((1,)), dma((1,)), dma((1,)),
            dma((1,)), dma((RINGS,)), dma((1,)), dma((1,)), dma((1,)), dma((1,)), dma((1,)), dma((1,)),
            dma((1,)), dma((1,)), dma((1,)), dma((1,)), dma((1,)), dma((1,)), dma((1,)),
        ],
        compiler_params=pltpu.CompilerParams(
            collective_id=0, has_side_effects=True, vmem_limit_bytes=63 * 1024 * 1024
        ),
    )(
        cotangent, diff_east, diff_north, flow_east, flow_north, sea_mask, cutoff,
        jnp.asarray(wide), jnp.asarray(turn),
    )
    lat = lax.axis_index("lat")
    row = lax.broadcasted_iota(jnp.int32, field.shape, 1)
    taken = jnp.logical_or(
        jnp.logical_and(lat == 1, row < EDGE), jnp.logical_and(lat == LATS - 2, row >= ROWS - EDGE)
    )
    return jnp.where(taken, jnp.tile(shared, (1, ROWS // 8, 1)), field)


def solution(mesh):
    return jax.shard_map(
        shards,
        mesh=mesh,
        in_specs=(
            P(None, "lat", "lon"),
            P("lat", "lon"),
            P("lat", "lon"),
            P("lat", "lon"),
            P("lat", "lon"),
            P("lat", "lon"),
            P("lat"),
        ),
        out_specs=P(None, "lat", "lon"),
        check_vma=False,
    )
```
